32 devices in a mesh: test: 2 (over core), bx: 4 (over y, x), by: 4 (over z).
Axes of the slice: x: 2, y: 2, z: 4, core: 2. Of those that a mesh axis runs over, the one named last changes fastest.
Arguments:
- log_conductivity: float32 [32, 32, 256], P('bx', 'by'), may hold values from -3 to 3
- storage: float32 [32, 32, 256], P('bx', 'by'), may hold values from 0.5 to 2
- recharge: float32 [32, 32, 256], P('bx', 'by'), may hold values from -6 to 6
- pump_rate: float32 [8], P('test'), may hold values from 4 to 16
- pump_well: int32 [8], P('test'), may hold values from 0 to 511
- observed: float32 [8, 512], P('test'), may hold values from -9 to 9
- owner: int32 [512], replicated, may hold values from 0 to 15, as said below
- screen_column: int32 [512], replicated, may hold values from 0 to 63
- screen_top: int32 [512], replicated, may hold values from 0 to 248
Outputs:
- gradient: float32 [32, 32, 256], P('bx', 'by', 'test')
The draws below stay inside these ranges and needn't reach their ends.
Inputs may be any that keep to these rules, and one draw needn't show every extreme that they name: `owner`: each brick owns exactly 32 wells.
All inputs are finite; a program needn't handle non-finite values.
Results may differ from the reference program's by a relative error of at most 0.0001.
Values sent between devices are 32-bit elements; how exact they have to be, the bound alone decides.
No kernel may reach another device: no remote copies, remote signals or barrier semaphores. Data moves between devices by JAX's collectives and lax.ppermute only.
A program may use at most 64 MiB of HBM per device.

```python
import math
import jax
import jax.numpy as jnp
from jax import lax

CX = 8
CY = 8
NZ = 256
SWEEPS = 3
SCREEN = 8
NX = 32
NY = 32
TESTS = 8
BRICKS = 16
WELLS = 512
N_BY = 4


def owner_table(key):
    return (jax.random.permutation(jax.random.fold_in(key, 3), WELLS) % BRICKS).astype(jnp.int32)


def draw_owner(key, part):
    return owner_table(key)


def draw_observed(key, part):
    ramp = 1.0 + 2.0 * owner_table(key).astype(jnp.float32) / max(BRICKS - 1, 1)
    noise_key = jax.random.fold_in(key, 11)
    values = jnp.clip(jax.random.normal(noise_key, (TESTS, WELLS), jnp.float32), -3.0, 3.0)
    return values * ramp[None, :]


def set_ends(values, key, least, high):
    longest = values.shape.index(max(values.shape))
    spots = []
    for shift in (0, 1):
        where = [jax.random.randint(jax.random.fold_in(key, axis), (), 0, length) for axis, length in enumerate(values.shape)]
        where[longest] = (where[longest] + shift) % values.shape[longest]
        spots.append(tuple(where))
    return values.at[spots[0]].set(least).at[spots[1]].set(high)


def block_levels(rng, dims, cuts, smallest, largest):
    level = 1.0
    for dim, shards_of in cuts:
        steps = jax.random.uniform(jax.random.fold_in(jax.random.fold_in(rng, 6), dim), (shards_of,), jnp.float32, smallest / len(cuts), largest / len(cuts))
        level = level * jnp.repeat(jnp.exp(steps), dims[dim] // shards_of).reshape((-1,) + (1,) * (len(dims) - 1 - dim))
    return level


def noise(stream_key, shape, deviation, bound, cuts=(), held_as=jnp.bfloat16):
    result = jax.random.normal(stream_key, shape, jnp.float32) * deviation
    if len(cuts) > 0:
        result = block_levels(stream_key, shape, cuts, -0.22, 0.18) * result
    return jnp.clip(result, min=-bound, max=bound).astype(held_as)


def setup_inputs(seed: int = 0) -> dict:
    seeds = jax.random.split(jax.random.key(seed), 10)
    return {
        "log_conductivity": noise(seeds[0], (NX, NY, NZ), 0.7, 3.0, ((0, 4), (1, 4)), jnp.float32),
        "storage": jnp.clip(jnp.exp(math.log(2.0) - 1.3862944 * jax.random.uniform(seeds[1], (NX, NY, NZ), jnp.float32) ** block_levels(seeds[1], (NX, NY, NZ), ((0, 4), (1, 4)), -0.2, 0.2)), 0.5, 2.0),
        "recharge": noise(seeds[2], (NX, NY, NZ), 1.0, 6.0, ((0, 4), (1, 4)), jnp.float32),
        "pump_rate": jnp.clip(jnp.exp(math.log(16.0) - 1.3862944 * jax.random.uniform(seeds[3], (TESTS,), jnp.float32) ** block_levels(seeds[3], (TESTS,), ((0, 2),), -0.2, 0.2)), 4.0, 16.0),
        "pump_well": set_ends(jax.random.randint(seeds[4], (TESTS,), 0, WELLS), jax.random.fold_in(seeds[4], 1), 0, WELLS - 1).astype(jnp.int32),
        "observed": draw_observed(jax.random.fold_in(seeds[9], 71), 0),
        "owner": draw_owner(jax.random.fold_in(seeds[9], 71), 0),
        "screen_column": set_ends(jax.random.randint(seeds[7], (WELLS,), 0, CX * CY), jax.random.fold_in(seeds[7], 1), 0, (CX * CY) - 1).astype(jnp.int32),
        "screen_top": set_ends(jax.random.randint(seeds[8], (WELLS,), 0, NZ - SCREEN + 1), jax.random.fold_in(seeds[8], 1), 0, NZ - SCREEN).astype(jnp.int32),
    }


epsilon = 1e-6


def pad_depth(values):
    return jnp.pad(values, [(0, 0)] * (values.ndim - 1) + [(1, 1)])


def neighbours(padded, centre):
    z_padded = pad_depth(centre)
    return [padded[..., 2:, 1:-1, :], padded[..., :-2, 1:-1, :],
            padded[..., 1:-1, 2:, :], padded[..., 1:-1, :-2, :],
            z_padded[..., 2:], z_padded[..., :-2]]


def weighted(conductance, others):
    accumulated = conductance[0] * others[0]
    for position in range(1, 6):
        accumulated = accumulated + conductance[position] * others[position]
    return accumulated


def sensitivity(conductance, heads_field, heads_padded, adjoint_field, adjoint_padded):
    near_heads = neighbours(heads_padded, heads_field)
    near_adjoint = neighbours(adjoint_padded, adjoint_field)
    accumulated = jnp.zeros_like(heads_field)
    for position in range(6):
        accumulated = accumulated + conductance[position] * (heads_field - near_heads[position]) * (adjoint_field - near_adjoint[position])
    return -0.5 * accumulated


def pad_plane(values):
    return jnp.pad(values, ((1, 1), (1, 1), (0, 0)))


def reference(log_conductivity, storage, recharge, pump_rate, pump_well, observed, owner, screen_column, screen_top):
    conductance = [jnp.exp(0.5 * (log_conductivity + other)) for other in neighbours(pad_plane(log_conductivity), log_conductivity)]
    diagonal = storage + weighted(conductance, [1.0] * 6)
    offsets = jnp.arange(SCREEN, dtype=jnp.int32)
    cell_z = screen_top[:, None] + offsets[None, :]
    cell_x = jnp.broadcast_to(((owner // N_BY) * CX + screen_column // CY)[:, None], cell_z.shape).astype(jnp.int32)
    cell_y = jnp.broadcast_to(((owner % N_BY) * CY + screen_column % CY)[:, None], cell_z.shape).astype(jnp.int32)

    def relax_field(source):
        iterate = source / diagonal
        for sweep_index in range(SWEEPS - 1):
            iterate = (source + weighted(conductance, neighbours(pad_plane(iterate), iterate))) / diagonal
        return iterate

    def one_test(running_sum, inputs):
        pump_value, well_index, observed_row = inputs
        source = recharge.at[cell_x[well_index], cell_y[well_index], cell_z[well_index]].add(-pump_value)
        heads_field = relax_field(source)
        well_heads = jnp.mean(heads_field[cell_x, cell_y, cell_z], axis=1)
        residual = well_heads - observed_row
        misfit = jnp.sum(residual * residual) / residual.shape[0] + epsilon
        values = jnp.broadcast_to((residual / misfit)[:, None], cell_z.shape)
        adjoint_source = jnp.zeros_like(heads_field).at[cell_x, cell_y, cell_z].add(values)
        adjoint_field = relax_field(adjoint_source)
        terms = sensitivity(conductance, heads_field, pad_plane(heads_field), adjoint_field, pad_plane(adjoint_field))
        return running_sum + terms, None

    running_sum, unused = lax.scan(one_test, jnp.zeros(log_conductivity.shape, jnp.float32), (pump_rate, pump_well, observed))
    return running_sum / TESTS
```

```python
import functools

import jax
import jax.numpy as jnp
from jax import lax
from jax.experimental import pallas as pl
from jax.experimental.pallas import tpu as pltpu
from jax.sharding import PartitionSpec as P

SCREEN = 8
LANES = 128
DEEP = 4
EPSILON = 1e-06


def row_plan(size):
    rows = []
    for field, reach in ((0, DEEP), (1, DEEP - 1), (2, DEEP - 1)):
        for dx in range(1, reach):
            rows.append((field, dx, reach - dx))
    return rows


def corner_rows(plan):
    return 2 * sum(count for _, _, count in plan)


def block_index(field, dx):
    return (0, DEEP, 2 * DEEP - 1)[field] + dx - 1


def side_partners(axis, count, tests):
    even, odd = [], []
    for test in range(tests):
        for place in range(count):
            me = test * count + place
            other = (test ^ 1 if (test ^ 1) < tests else test) * count + place
            up = place ^ 1
            even.append((me, test * count + up if up < count else other))
            down = ((place + 1) ^ 1) - 1
            odd.append((me, test * count + down if 0 <= down < count else other))
    return even, odd


def swap_sides(send_even, send_odd, axis, tests):
    even, odd = side_partners(axis, lax.axis_size(axis), tests)
    return lax.ppermute(send_even, ("test", axis), even), lax.ppermute(send_odd, ("test", axis), odd)


def pack_y(log_ref, sto_ref, rec_ref, even_ref, odd_ref):
    size_x, size_y, _ = log_ref.shape
    is_even = lax.axis_index("by") % 2 == 0
    rows = 3 * DEEP - 2
    for x in range(size_x):
        start = 0
        for ref, reach in ((log_ref, DEEP), (sto_ref, DEEP - 1), (rec_ref, DEEP - 1)):
            up = ref[x, size_y - reach :, :]
            down = ref[x, :reach, :]
            at = pl.ds(x * rows + start, reach)
            even_ref[at, :] = jnp.where(is_even, up, down)
            odd_ref[at, :] = jnp.where(is_even, down, up)
            start += reach


def pack_x(plan, log_ref, sto_ref, rec_ref, ey_ref, oy_ref, even_ref, odd_ref):
    size_x, size_y, _ = log_ref.shape
    y_even = lax.axis_index("by") % 2 == 0
    x_even = lax.axis_index("bx") % 2 == 0
    rows = 3 * DEEP - 2
    blocks = (3 * DEEP - 2) * size_y
    first = (0, DEEP, 2 * DEEP - 1)
    for field, (ref, reach) in enumerate(((log_ref, DEEP), (sto_ref, DEEP - 1), (rec_ref, DEEP - 1))):
        for dx in range(1, reach + 1):
            up, down = ref[size_x - dx], ref[dx - 1]
            at = pl.ds(block_index(field, dx) * size_y, size_y)
            even_ref[at, :] = jnp.where(x_even, up, down)
            odd_ref[at, :] = jnp.where(x_even, down, up)
    place = blocks
    for field, dx, count in plan:
        reach = DEEP if field == 0 else DEEP - 1
        for x_up, x_down, side in ((size_x - dx, dx - 1, 0), (size_x - dx, dx - 1, 1)):
            parts = []
            for x in (x_up, x_down):
                start = x * rows + first[field] + (reach - count if side == 0 else 0)
                got_e, got_o = ey_ref[pl.ds(start, count), :], oy_ref[pl.ds(start, count), :]
                parts.append(jnp.where(y_even, got_o, got_e) if side == 0 else jnp.where(y_even, got_e, got_o))
            at = pl.ds(place, count)
            even_ref[at, :] = jnp.where(x_even, parts[0], parts[1])
            odd_ref[at, :] = jnp.where(x_even, parts[1], parts[0])
            place += count


def tile_marks(tests):
    sub = lax.broadcasted_iota(jnp.int32, (8, LANES), 0)
    lane = lax.broadcasted_iota(jnp.int32, (8, LANES), 1)
    half = sub // tests
    return sub, lane, half


def shift_up(values, lane, half):
    turned = pltpu.roll(values, LANES - 1, values.ndim - 1)
    crossed = jnp.where(half == 0, pltpu.roll(turned, 4, values.ndim - 2), 0.0)
    return jnp.where(lane == LANES - 1, crossed, turned)


def shift_down(values, lane, half):
    turned = pltpu.roll(values, 1, values.ndim - 1)
    crossed = jnp.where(half == 1, pltpu.roll(turned, 4, values.ndim - 2), 0.0)
    return jnp.where(lane == 0, crossed, turned)


def sum_z(values, lane, half):
    down = pltpu.roll(values, 1, values.ndim - 1)
    up = pltpu.roll(values, LANES - 1, values.ndim - 1)
    crossed = pltpu.roll(jnp.where(lane == 0, down, up), 4, values.ndim - 2)
    edge = ((lane == 0) & (half == 1)) | ((lane == LANES - 1) & (half == 0))
    crossed = jnp.where(edge, crossed, 0.0)
    return jnp.where(lane == 0, crossed, down) + jnp.where(lane == LANES - 1, crossed, up)


def sweep(source_ref, gamma_ref, from_ref, to_ref, low, high, lane, half):
    def one_row(x, carry):
        centre = from_ref[x, low:high]
        total = from_ref[x - 1, low:high] + from_ref[x + 1, low:high]
        total = total + from_ref[x, low - 1 : high - 1] + from_ref[x, low + 1 : high + 1]
        total = total + sum_z(centre, lane, half)
        to_ref[x, low:high] = source_ref[x, low:high] + gamma_ref[x, low:high] * total
        return carry

    lax.fori_loop(low, high, one_row, 0)


def wells_kernel(tests, per_brick, owner_ref, packed_ref, observed_ref, window_ref, own_ref, obs_ref, count_ref, index_ref):
    bricks = count_ref.shape[0]
    for brick in range(bricks):
        count_ref[brick] = 0
    n_wells = owner_ref.shape[0]

    def one_well(well, found):
        brick = owner_ref[well]
        packed = packed_ref[well]
        rank = count_ref[brick]
        count_ref[brick] = rank + 1
        window_ref[found] = packed + ((brick * per_brick + rank) << 16)
        at = jnp.where((packed >> 29) & 1 == 1, rank, per_brick)
        own_ref[at] = packed
        index_ref[at] = well
        return found + ((packed >> 30) & 1)

    found = lax.fori_loop(0, n_wells, one_well, jnp.int32(0), unroll=8)
    window_ref[n_wells] = found
    lane = lax.broadcasted_iota(jnp.int32, (1, LANES), 1)

    def one_value(rank, values):
        well = index_ref[rank]
        for test in range(tests):
            values = jnp.where(lane == test * per_brick + rank, observed_ref[test, well], values)
        return values

    obs_ref[...] = lax.fori_loop(0, per_brick, one_value, jnp.zeros((1, LANES), jnp.float32), unroll=8)


def heads_kernel(
    plan,
    tests,
    per_brick,
    log_ref,
    sto_ref,
    rec_ref,
    ey_ref,
    oy_ref,
    ex_ref,
    ox_ref,
    own_ref,
    obs_ref,
    pump_ref,
    rate_ref,
    gamma_ref,
    delta_ref,
    e_ref,
    inv_e_ref,
    head_ref,
    row_ref,
    log_w,
    sto_w,
    rec_w,
    e_w,
    gam_w,
    del_w,
    bet_w,
    one_ref,
    two_ref,
    bet_ref,
):
    size_x, size_y, size_z = log_ref.shape
    wide_x, wide_y = size_x + 2 * DEEP, size_y + 2 * DEEP
    bx, by = lax.axis_index("bx"), lax.axis_index("by")
    y_even, x_even = by % 2 == 0, bx % 2 == 0
    no_low_y, no_high_y = by == 0, by == lax.axis_size("by") - 1
    no_low_x, no_high_x = bx == 0, bx == lax.axis_size("bx") - 1
    rows = 3 * DEEP - 2
    blocks = rows * size_y
    first = (0, DEEP, 2 * DEEP - 1)
    fields = ((log_ref, log_w, DEEP), (sto_ref, sto_w, DEEP - 1), (rec_ref, rec_w, DEEP - 1))
    for field, (ref, wide, reach) in enumerate(fields):
        fill = 1.0 if field == 1 else 0.0
        wide[...] = jnp.full(wide.shape, fill, jnp.float32)
        for x in range(size_x):
            wide[DEEP + x, DEEP : DEEP + size_y, :] = ref[x]
            at = pl.ds(x * rows + first[field], reach)
            got_e, got_o = ey_ref[at, :], oy_ref[at, :]
            low, high = jnp.where(y_even, got_o, got_e), jnp.where(y_even, got_e, got_o)
            wide[DEEP + x, DEEP - reach : DEEP, :] = jnp.where(no_low_y, fill, low)
            wide[DEEP + x, DEEP + size_y : DEEP + size_y + reach, :] = jnp.where(no_high_y, fill, high)
        for dx in range(1, reach + 1):
            at = pl.ds(block_index(field, dx) * size_y, size_y)
            got_e, got_o = ex_ref[at, :], ox_ref[at, :]
            low, high = jnp.where(x_even, got_o, got_e), jnp.where(x_even, got_e, got_o)
            wide[DEEP - dx, DEEP : DEEP + size_y, :] = jnp.where(no_low_x, fill, low)
            wide[DEEP + size_x + dx - 1, DEEP : DEEP + size_y, :] = jnp.where(no_high_x, fill, high)
    place = blocks
    for field, dx, count in plan:
        wide = fields[field][1]
        fill = 1.0 if field == 1 else 0.0
        for side in (0, 1):
            at = pl.ds(place, count)
            got_e, got_o = ex_ref[at, :], ox_ref[at, :]
            low, high = jnp.where(x_even, got_o, got_e), jnp.where(x_even, got_e, got_o)
            to = pl.ds(DEEP - count, count) if side == 0 else pl.ds(DEEP + size_y, count)
            absent = no_low_y if side == 0 else no_high_y
            wide[DEEP - dx, to, :] = jnp.where(absent | no_low_x, fill, low)
            wide[DEEP + size_x + dx - 1, to, :] = jnp.where(absent | no_high_x, fill, high)
            place += count

    row_at = lax.broadcasted_iota(jnp.int32, (wide_y, size_z), 0)
    z_at = lax.broadcasted_iota(jnp.int32, (wide_y, size_z), 1)
    inside_y = ((row_at >= DEEP) | jnp.logical_not(no_low_y)) & ((row_at < DEEP + size_y) | jnp.logical_not(no_high_y))

    def one_exp(x, carry):
        e_w[x] = jnp.exp(0.5 * log_w[x])
        return carry

    lax.fori_loop(0, wide_x, one_exp, 0)

    def one_row(x, carry):
        e = e_w[x]
        total = e_w[x - 1] + e_w[x + 1]
        total = total + pltpu.roll(e, 1, 0) + pltpu.roll(e, wide_y - 1, 0)
        total = total + jnp.where(z_at == 0, 1.0, pltpu.roll(e, 1, 1))
        total = total + jnp.where(z_at == size_z - 1, 1.0, pltpu.roll(e, size_z - 1, 1))
        inside_x = ((x >= DEEP) | jnp.logical_not(no_low_x)) & ((x < DEEP + size_x) | jnp.logical_not(no_high_x))
        delta = jnp.where(inside_y & inside_x, e / (sto_w[x] + e * total), 0.0)
        del_w[x] = delta
        gam_w[x] = delta * e
        bet_w[x] = delta * rec_w[x]
        return carry

    lax.fori_loop(1, wide_x - 1, one_row, 0)
    sub, lane, half = tile_marks(tests)

    def spread(wide, x, y):
        low = jnp.broadcast_to(wide[x, pl.ds(y, 1), :LANES], (8, LANES))
        high = jnp.broadcast_to(wide[x, pl.ds(y, 1), LANES:], (8, LANES))
        return jnp.where(half == 0, low, high)

    def spread_row(x, carry):
        for y in range(1, wide_y - 1):
            gamma_ref[x, y] = spread(gam_w, x, y)
            delta_ref[x, y] = spread(del_w, x, y)
            bet_ref[x, y] = spread(bet_w, x, y)
        return carry

    lax.fori_loop(1, wide_x - 1, spread_row, 0)

    def spread_near(x, carry):
        for y in range(DEEP - 1, DEEP + size_y + 1):
            e = spread(e_w, x, y)
            e_ref[x, y] = e
            inv_e_ref[x, y] = 1.0 / e
        return carry

    lax.fori_loop(DEEP - 1, DEEP + size_x + 1, spread_near, 0)
    z_of = half * LANES + lane
    for test in range(tests):
        packed = pump_ref[test]

        @pl.when((packed >> 30) & 1 == 1)
        def _(packed=packed, test=test):
            x, y, top = (packed >> 12) & 15, (packed >> 8) & 15, packed & 255
            hit = (z_of >= top) & (z_of < top + SCREEN) & (sub % tests == test)
            bet_ref[x, y] = bet_ref[x, y] - jnp.where(hit, delta_ref[x, y] * rate_ref[test], 0.0)

    sweep(bet_ref, gamma_ref, bet_ref, one_ref, 2, wide_y - 2, lane, half)
    sweep(bet_ref, gamma_ref, one_ref, two_ref, 3, wide_y - 3, lane, half)

    def one_head(x, carry):
        head_ref[x, 3 : wide_y - 3] = two_ref[x, 3 : wide_y - 3] * inv_e_ref[x, 3 : wide_y - 3]
        return carry

    lax.fori_loop(3, wide_x - 3, one_head, 0)
    slot_of = lane - per_brick * (sub % tests)
    gathered = jnp.zeros((8, LANES), jnp.float32)
    for rank in range(per_brick):
        packed = own_ref[rank]
        x, y, top = (packed >> 12) & 15, (packed >> 8) & 15, packed & 255
        hit = (z_of >= top) & (z_of < top + SCREEN)
        mean = jnp.sum(jnp.where(hit, head_ref[x, y], 0.0), axis=1, keepdims=True)
        gathered = jnp.where(slot_of == rank, mean, gathered)
    residual = jnp.sum(gathered, axis=0, keepdims=True) * (1.0 / SCREEN) - obs_ref[...]
    row_ref[...] = jnp.broadcast_to(residual[None], row_ref.shape)


def adjoint_kernel(
    tests,
    per_brick,
    split,
    scale,
    resid_ref,
    window_ref,
    gamma_ref,
    delta_ref,
    e_ref,
    inv_e_ref,
    head_ref,
    *rest,
):
    outs, (weight_ref, bet_ref, one_ref, two_ref, adj_ref) = rest[:-5], rest[-5:]
    wide_x, wide_y = gamma_ref.shape[:2]
    size_x, size_y = wide_x - 2 * DEEP, wide_y - 2 * DEEP
    n_wells = window_ref.shape[0] - 1
    sub, lane, half = tile_marks(tests)
    z_of = half * LANES + lane
    resid = resid_ref[:, 0, :]
    squares = jnp.sum(resid * resid, axis=0, keepdims=True)
    row_lane = lax.broadcasted_iota(jnp.int32, (1, LANES), 1)
    misfit = jnp.zeros((1, LANES), jnp.float32)
    for test in range(tests):
        mine = row_lane // per_brick == test
        total = jnp.sum(jnp.where(mine, squares, 0.0), axis=1, keepdims=True)
        misfit = jnp.where(mine, total / n_wells + EPSILON, misfit)
    weight_ref[...] = resid / misfit

    def clear(x, carry):
        bet_ref[x] = jnp.zeros(bet_ref.shape[1:], jnp.float32)
        return carry

    lax.fori_loop(0, wide_x, clear, 0)
    slot_of = lane - per_brick * (sub % tests)

    def one_well(place, carry):
        packed = window_ref[place]
        x, y, top = (packed >> 12) & 15, (packed >> 8) & 15, packed & 255
        slot = (packed >> 16) & 0x1FFF
        brick, rank = slot // per_brick, slot % per_brick
        row = jnp.broadcast_to(weight_ref[pl.ds(brick, 1), :], (8, LANES))
        value = jnp.sum(jnp.where(slot_of == rank, row, 0.0), axis=1, keepdims=True)
        hit = (z_of >= top) & (z_of < top + SCREEN)
        bet_ref[x, y] = bet_ref[x, y] + jnp.where(hit, value, 0.0)
        return carry

    lax.fori_loop(0, window_ref[n_wells], one_well, 0)

    def scaled(x, carry):
        bet_ref[x, 1 : wide_y - 1] = bet_ref[x, 1 : wide_y - 1] * delta_ref[x, 1 : wide_y - 1]
        return carry

    lax.fori_loop(1, wide_x - 1, scaled, 0)
    sweep(bet_ref, gamma_ref, bet_ref, one_ref, 2, wide_y - 2, lane, half)
    sweep(bet_ref, gamma_ref, one_ref, two_ref, 3, wide_y - 3, lane, half)

    def one_adjoint(x, carry):
        adj_ref[x, 3 : wide_y - 3] = two_ref[x, 3 : wide_y - 3] * inv_e_ref[x, 3 : wide_y - 3]
        return carry

    lax.fori_loop(3, wide_x - 3, one_adjoint, 0)
    own_y = slice(DEEP, DEEP + size_y)

    def one_row(x, carry):
        e, head, adjoint = e_ref[x, own_y], head_ref[x, own_y], adj_ref[x, own_y]

        def face(near_x, near_y):
            gap = (head - head_ref[near_x, near_y]) * (adjoint - adj_ref[near_x, near_y])
            return e_ref[near_x, near_y] * gap

        total = face(x - 1, own_y) + face(x + 1, own_y)
        total = total + face(x, slice(DEEP - 1, DEEP + size_y - 1)) + face(x, slice(DEEP + 1, DEEP + size_y + 1))
        total = total * e
        last = (lane == LANES - 1) & (half == 1)
        e_next = jnp.where(last, 1.0, shift_up(e, lane, half))
        gap = (head - shift_up(head, lane, half)) * (adjoint - shift_up(adjoint, lane, half))
        upper = e * e_next * gap
        begin = (lane == 0) & (half == 0)
        lower = jnp.where(begin, e * head * adjoint, shift_down(upper, lane, half))
        total = (total + upper + lower) * scale
        total = total + pltpu.roll(total, 7, 1)
        total = total + pltpu.roll(total, 6, 1)
        for y in range(size_y):
            low, high = total[y, 0:1], total[y, 4:5]
            if split:
                first = lax.axis_index("test") == 0
                outs[0][x - DEEP, pl.ds(y, 1), :] = jnp.where(first, low, high)
                outs[1][x - DEEP, pl.ds(y, 1), :] = jnp.where(first, high, low)
            else:
                outs[0][x - DEEP, pl.ds(y, 1), :LANES] = low
                outs[0][x - DEEP, pl.ds(y, 1), LANES:] = high
        return carry

    lax.fori_loop(DEEP, DEEP + size_x, one_row, 0)


def vmem():
    return pl.BlockSpec(memory_space=pltpu.VMEM)


def smem():
    return pl.BlockSpec(memory_space=pltpu.SMEM)


def f32(*shape):
    return jax.ShapeDtypeStruct(shape, jnp.float32)


def i32(*shape):
    return jax.ShapeDtypeStruct(shape, jnp.int32)


PARAMS = pltpu.CompilerParams(vmem_limit_bytes=24 * 1024 * 1024)


def local(log_conductivity, storage, recharge, pump_rate, pump_well, observed, owner, screen_column, screen_top):
    size_x, size_y, size_z = log_conductivity.shape
    tests = pump_rate.shape[0]
    n_wells = owner.shape[0]
    groups, n_bx, n_by = lax.axis_size("test"), lax.axis_size("bx"), lax.axis_size("by")
    bricks = n_bx * n_by
    per_brick = n_wells // bricks
    plan = row_plan(size_y)
    rows_y = (3 * DEEP - 2) * size_x
    rows_x = (3 * DEEP - 2) * size_y + corner_rows(plan)
    wide_x, wide_y = size_x + 2 * DEEP, size_y + 2 * DEEP

    bx, by = lax.axis_index("bx"), lax.axis_index("by")
    well_x = (owner // n_by - bx) * size_x + screen_column // size_y + DEEP
    well_y = (owner % n_by - by) * size_y + screen_column % size_y + DEEP
    out_x = jnp.maximum(jnp.maximum(DEEP - well_x, well_x - (DEEP + size_x - 1)), 0)
    out_y = jnp.maximum(jnp.maximum(DEEP - well_y, well_y - (DEEP + size_y - 1)), 0)
    in_window = (out_x + out_y < DEEP).astype(jnp.int32)
    owned = ((out_x == 0) & (out_y == 0)).astype(jnp.int32)
    packed = (in_window << 30) + (owned << 29) + ((well_x & 15) << 12) + ((well_y & 15) << 8) + screen_top
    pump_packed = packed[pump_well]

    even_y, odd_y = pl.pallas_call(
        pack_y,
        out_shape=[f32(rows_y, size_z)] * 2,
        in_specs=[vmem()] * 3,
        out_specs=[vmem()] * 2,
        compiler_params=PARAMS,
        name="pack_y",
    )(log_conductivity, storage, recharge)
    got_even_y, got_odd_y = swap_sides(even_y, odd_y, "by", groups)

    window, own, obs = pl.pallas_call(
        functools.partial(wells_kernel, tests, per_brick),
        out_shape=[i32(n_wells + 1), i32(per_brick + 1), f32(1, LANES)],
        in_specs=[smem()] * 3,
        out_specs=[smem(), smem(), vmem()],
        scratch_shapes=[pltpu.SMEM((bricks,), jnp.int32), pltpu.SMEM((per_brick + 1,), jnp.int32)],
        compiler_params=PARAMS,
        name="wells",
    )(owner, packed, observed)

    even_x, odd_x = pl.pallas_call(
        functools.partial(pack_x, plan),
        out_shape=[f32(rows_x, size_z)] * 2,
        in_specs=[vmem()] * 5,
        out_specs=[vmem()] * 2,
        compiler_params=PARAMS,
        name="pack_x",
    )(log_conductivity, storage, recharge, got_even_y, got_odd_y)
    got_even_x, got_odd_x = swap_sides(even_x, odd_x, "bx", groups)

    tiles = (wide_x, wide_y, 8, LANES)
    wide = (wide_x, wide_y, size_z)
    gamma, delta, e, inv_e, head, row = pl.pallas_call(
        functools.partial(heads_kernel, plan, tests, per_brick),
        out_shape=[f32(*tiles)] * 5 + [f32(bricks, 1, LANES)],
        in_specs=[vmem()] * 7 + [smem(), vmem(), smem(), smem()],
        out_specs=[vmem()] * 6,
        scratch_shapes=[pltpu.VMEM(wide, jnp.float32)] * 7 + [pltpu.VMEM(tiles, jnp.float32)] * 3,
        compiler_params=PARAMS,
        name="heads",
    )(log_conductivity, storage, recharge, got_even_y, got_odd_y, got_even_x, got_odd_x, own, obs, pump_packed, pump_rate)

    residuals = lax.all_to_all(row, ("bx", "by"), 0, 0)

    all_tests = tests * groups
    split = groups == 2
    out_shape = [f32(size_x, size_y, LANES)] * 2 if split else [f32(size_x, size_y, size_z)]
    partial = pl.pallas_call(
        functools.partial(adjoint_kernel, tests, per_brick, split, -0.5 / all_tests),
        out_shape=out_shape,
        in_specs=[vmem(), smem()] + [vmem()] * 5,
        out_specs=[vmem()] * len(out_shape),
        scratch_shapes=[pltpu.VMEM((bricks, LANES), jnp.float32)] + [pltpu.VMEM(tiles, jnp.float32)] * 4,
        compiler_params=PARAMS,
        name="adjoint",
    )(residuals, window, gamma, delta, e, inv_e, head)
    if split:
        return partial[0] + lax.ppermute(partial[1], "test", [(0, 1), (1, 0)])
    return lax.psum_scatter(partial[0], "test", scatter_dimension=2, tiled=True)


def solution(mesh):
    placed = (
        P("bx", "by", None),
        P("bx", "by", None),
        P("bx", "by", None),
        P("test"),
        P("test"),
        P("test", None),
        P(),
        P(),
        P(),
    )
    return jax.shard_map(local, mesh=mesh, in_specs=placed, out_specs=P("bx", "by", "test"), check_vma=False)
```

```python
import functools

import jax
import jax.numpy as jnp
from jax import lax
from jax.experimental import pallas as pl
from jax.experimental.pallas import tpu as pltpu
from jax.sharding import PartitionSpec as P

SCREEN = 8
LANES = 128
DEEP = 4
EPSILON = 1e-06
WELL_CHUNK = 512
WELLS_AT_ONCE = 16


def list_length(per_brick):
    return -(-9 * per_brick // LANES) * LANES


def row_plan(size):
    rows = []
    for field, reach in ((0, DEEP), (1, DEEP - 1), (2, DEEP - 1)):
        for dx in range(1, reach):
            rows.append((field, dx, reach - dx))
    return rows


def corner_rows(plan):
    return 2 * sum(count for _, _, count in plan)


def block_index(field, dx):
    return (0, DEEP, 2 * DEEP - 1)[field] + dx - 1


def side_partners(axis, count, tests):
    even, odd = [], []
    for test in range(tests):
        for place in range(count):
            me = test * count + place
            other = (test ^ 1 if (test ^ 1) < tests else test) * count + place
            up = place ^ 1
            even.append((me, test * count + up if up < count else other))
            down = ((place + 1) ^ 1) - 1
            odd.append((me, test * count + down if 0 <= down < count else other))
    return even, odd


def swap_sides(send_even, send_odd, axis, tests):
    even, odd = side_partners(axis, lax.axis_size(axis), tests)
    return lax.ppermute(send_even, ("test", axis), even), lax.ppermute(send_odd, ("test", axis), odd)


def load_and_pack(*refs):
    n_in = (len(refs) - 3) // 2
    sources, loaded, (even_ref, odd_ref, sems) = refs[:n_in], refs[n_in : 2 * n_in], refs[2 * n_in :]
    copies = [pltpu.make_async_copy(a, b, sems.at[i]) for i, (a, b) in enumerate(zip(sources, loaded))]
    for copy in copies:
        copy.start()
    for copy in copies[:3]:
        copy.wait()
    log_ref, sto_ref, rec_ref = loaded[:3]
    size_x, size_y, _ = log_ref.shape
    is_even = lax.axis_index("by") % 2 == 0
    rows = 3 * DEEP - 2
    for x in range(size_x):
        start = 0
        for ref, reach in ((log_ref, DEEP), (sto_ref, DEEP - 1), (rec_ref, DEEP - 1)):
            up = ref[x, size_y - reach :, :]
            down = ref[x, :reach, :]
            at = pl.ds(x * rows + start, reach)
            even_ref[at, :] = jnp.where(is_even, up, down)
            odd_ref[at, :] = jnp.where(is_even, down, up)
            start += reach
    for copy in copies[3:]:
        copy.wait()


def pack_x(plan, log_ref, sto_ref, rec_ref, ey_ref, oy_ref, even_ref, odd_ref):
    size_x, size_y, _ = log_ref.shape
    y_even = lax.axis_index("by") % 2 == 0
    x_even = lax.axis_index("bx") % 2 == 0
    rows = 3 * DEEP - 2
    blocks = (3 * DEEP - 2) * size_y
    first = (0, DEEP, 2 * DEEP - 1)
    for field, (ref, reach) in enumerate(((log_ref, DEEP), (sto_ref, DEEP - 1), (rec_ref, DEEP - 1))):
        for dx in range(1, reach + 1):
            up, down = ref[size_x - dx], ref[dx - 1]
            at = pl.ds(block_index(field, dx) * size_y, size_y)
            even_ref[at, :] = jnp.where(x_even, up, down)
            odd_ref[at, :] = jnp.where(x_even, down, up)
    place = blocks
    for field, dx, count in plan:
        reach = DEEP if field == 0 else DEEP - 1
        for x_up, x_down, side in ((size_x - dx, dx - 1, 0), (size_x - dx, dx - 1, 1)):
            parts = []
            for x in (x_up, x_down):
                start = x * rows + first[field] + (reach - count if side == 0 else 0)
                got_e, got_o = ey_ref[pl.ds(start, count), :], oy_ref[pl.ds(start, count), :]
                parts.append(jnp.where(y_even, got_o, got_e) if side == 0 else jnp.where(y_even, got_e, got_o))
            at = pl.ds(place, count)
            even_ref[at, :] = jnp.where(x_even, parts[0], parts[1])
            odd_ref[at, :] = jnp.where(x_even, parts[1], parts[0])
            place += count


def tile_marks(tests):
    sub = lax.broadcasted_iota(jnp.int32, (8, LANES), 0)
    lane = lax.broadcasted_iota(jnp.int32, (8, LANES), 1)
    half = sub // tests
    return sub, lane, half


def shift_up(values, lane, half):
    turned = pltpu.roll(values, LANES - 1, values.ndim - 1)
    crossed = jnp.where(half == 0, pltpu.roll(turned, 4, values.ndim - 2), 0.0)
    return jnp.where(lane == LANES - 1, crossed, turned)


def shift_down(values, lane, half):
    turned = pltpu.roll(values, 1, values.ndim - 1)
    crossed = jnp.where(half == 1, pltpu.roll(turned, 4, values.ndim - 2), 0.0)
    return jnp.where(lane == 0, crossed, turned)


def sum_z(values, lane, half):
    down = pltpu.roll(values, 1, values.ndim - 1)
    up = pltpu.roll(values, LANES - 1, values.ndim - 1)
    crossed = pltpu.roll(jnp.where(lane == 0, down, up), 4, values.ndim - 2)
    edge = ((lane == 0) & (half == 1)) | ((lane == LANES - 1) & (half == 0))
    crossed = jnp.where(edge, crossed, 0.0)
    return jnp.where(lane == 0, crossed, down) + jnp.where(lane == LANES - 1, crossed, up)


def sweep(source_ref, gamma_ref, from_ref, to_ref, low, high, lane, half):
    def one_row(x, carry):
        centre = from_ref[x, low:high]
        total = from_ref[x - 1, low:high] + from_ref[x + 1, low:high]
        total = total + from_ref[x, low - 1 : high - 1] + from_ref[x, low + 1 : high + 1]
        total = total + sum_z(centre, lane, half)
        to_ref[x, low:high] = source_ref[x, low:high] + gamma_ref[x, low:high] * total
        return carry

    lax.fori_loop(low, high, one_row, 0, unroll=True)


def wells_kernel(tests, per_brick, owner_ref, xy_ref, top_ref, window_ref, owned_ref, observed_ref, pump_ref, table_ref, obs_ref, bricks):
    n_wells = owner_ref.shape[1]
    chunk = WELL_CHUNK if n_wells % WELL_CHUNK == 0 else n_wells
    listed = list_length(per_brick)
    before = lax.broadcasted_iota(jnp.int32, (chunk, chunk), 0) < lax.broadcasted_iota(jnp.int32, (chunk, chunk), 1)
    before = jnp.where(before, 1.0, 0.0).astype(jnp.bfloat16)
    brick_at = lax.broadcasted_iota(jnp.int32, (bricks, chunk), 0)
    list_at = lax.broadcasted_iota(jnp.int32, (listed, chunk), 0).astype(jnp.float32)
    own_at = (lax.broadcasted_iota(jnp.int32, (LANES, chunk), 0) % per_brick).astype(jnp.float32)
    lane_at = lax.broadcasted_iota(jnp.int32, (1, chunk), 1)
    first_row = lax.broadcasted_iota(jnp.int32, (16, chunk), 0) == 0
    total = jnp.zeros((bricks + 16, 1), jnp.float32)
    result = jnp.zeros((32, listed + LANES + 16), jnp.float32)
    for start in range(0, n_wells, chunk):
        part = slice(start, start + chunk)
        owner = owner_ref[:, part]
        near, mine = window_ref[:, part], owned_ref[:, part]
        ones = jnp.where(brick_at == owner, 1.0, 0.0)
        counted = jnp.concatenate([ones, jnp.where(first_row, near, 0.0)], axis=0)
        prefix = jnp.dot(counted.astype(jnp.bfloat16), before, preferred_element_type=jnp.float32) + total
        total = total + jnp.sum(counted, axis=1, keepdims=True)
        rank = jnp.sum(ones * prefix[:bricks], axis=0, keepdims=True)
        in_list = jnp.where((list_at == prefix[bricks : bricks + 1]) & (near > 0.5), 1.0, 0.0)
        in_own = jnp.where((own_at == rank) & (mine > 0.5), 1.0, 0.0)
        pumps = [jnp.where(lane_at + start == pump_ref[:, test : test + 1], 1.0, 0.0) for test in range(tests)]
        pumps.append(jnp.zeros((16 - tests, chunk), jnp.float32))
        chosen = jnp.concatenate([in_list, in_own] + pumps, axis=0).astype(jnp.bfloat16)
        slot = owner * per_brick + rank.astype(jnp.int32)
        numbers = [xy_ref[:, part], top_ref[:, part], slot & 255, slot >> 8]
        rows = [number.astype(jnp.float32) for number in numbers] + [near]
        for test in range(tests):
            value = observed_ref[test : test + 1, part]
            for _ in range(3):
                piece = value.astype(jnp.bfloat16).astype(jnp.float32)
                rows.append(piece)
                value = value - piece
        rows.append(jnp.zeros((32 - len(rows), chunk), jnp.float32))
        carried = jnp.concatenate(rows, axis=0).astype(jnp.bfloat16)
        result = result + lax.dot_general(carried, chosen, (((1,), (1,)), ((), ())), preferred_element_type=jnp.float32)
    numbers = [result[row : row + 1].astype(jnp.int32) for row in range(5)]
    words = numbers[1] + (numbers[0] << 8) + (numbers[2] << 16) + (numbers[3] << 24) + (numbers[4] << 30)
    listed_rows = listed // LANES
    for row in range(listed_rows + 1):
        table_ref[row : row + 1, :] = words[:, row * LANES : (row + 1) * LANES]
    table_ref[listed_rows + 1 : listed_rows + 2, : LANES // 8] = words[:, listed + LANES :]
    found = jnp.broadcast_to(total[bricks : bricks + 1], (1, LANES)).astype(jnp.int32)
    table_ref[listed_rows + 2 : listed_rows + 3, :] = found
    lane = lax.broadcasted_iota(jnp.int32, (1, LANES), 1)
    values = jnp.zeros((1, LANES), jnp.float32)
    for test in range(tests):
        pieces = [result[row : row + 1, listed : listed + LANES] for row in range(5 + 3 * test, 8 + 3 * test)]
        values = jnp.where(lane // per_brick == test, pieces[0] + (pieces[1] + pieces[2]), values)
    obs_ref[...] = values


def heads_kernel(
    plan,
    tests,
    per_brick,
    log_ref,
    sto_ref,
    rec_ref,
    ey_ref,
    oy_ref,
    ex_ref,
    ox_ref,
    table_ref,
    obs_ref,
    rate_ref,
    gamma_ref,
    delta_ref,
    e_ref,
    inv_e_ref,
    head_ref,
    row_ref,
    log_w,
    sto_w,
    rec_w,
    e_w,
    gam_w,
    del_w,
    bet_w,
    one_ref,
    two_ref,
    bet_ref,
):
    size_x, size_y, size_z = log_ref.shape
    wide_x, wide_y = size_x + 2 * DEEP, size_y + 2 * DEEP
    bx, by = lax.axis_index("bx"), lax.axis_index("by")
    y_even, x_even = by % 2 == 0, bx % 2 == 0
    no_low_y, no_high_y = by == 0, by == lax.axis_size("by") - 1
    no_low_x, no_high_x = bx == 0, bx == lax.axis_size("bx") - 1
    rows = 3 * DEEP - 2
    blocks = rows * size_y
    first = (0, DEEP, 2 * DEEP - 1)
    fields = ((log_ref, log_w, DEEP), (sto_ref, sto_w, DEEP - 1), (rec_ref, rec_w, DEEP - 1))
    for field, (ref, wide, reach) in enumerate(fields):
        fill = 1.0 if field == 1 else 0.0
        wide[...] = jnp.full(wide.shape, fill, jnp.float32)
        for x in range(size_x):
            wide[DEEP + x, DEEP : DEEP + size_y, :] = ref[x]
            at = pl.ds(x * rows + first[field], reach)
            got_e, got_o = ey_ref[at, :], oy_ref[at, :]
            low, high = jnp.where(y_even, got_o, got_e), jnp.where(y_even, got_e, got_o)
            wide[DEEP + x, DEEP - reach : DEEP, :] = jnp.where(no_low_y, fill, low)
            wide[DEEP + x, DEEP + size_y : DEEP + size_y + reach, :] = jnp.where(no_high_y, fill, high)
        for dx in range(1, reach + 1):
            at = pl.ds(block_index(field, dx) * size_y, size_y)
            got_e, got_o = ex_ref[at, :], ox_ref[at, :]
            low, high = jnp.where(x_even, got_o, got_e), jnp.where(x_even, got_e, got_o)
            wide[DEEP - dx, DEEP : DEEP + size_y, :] = jnp.where(no_low_x, fill, low)
            wide[DEEP + size_x + dx - 1, DEEP : DEEP + size_y, :] = jnp.where(no_high_x, fill, high)
    place = blocks
    for field, dx, count in plan:
        wide = fields[field][1]
        fill = 1.0 if field == 1 else 0.0
        for side in (0, 1):
            at = pl.ds(place, count)
            got_e, got_o = ex_ref[at, :], ox_ref[at, :]
            low, high = jnp.where(x_even, got_o, got_e), jnp.where(x_even, got_e, got_o)
            to = pl.ds(DEEP - count, count) if side == 0 else pl.ds(DEEP + size_y, count)
            absent = no_low_y if side == 0 else no_high_y
            wide[DEEP - dx, to, :] = jnp.where(absent | no_low_x, fill, low)
            wide[DEEP + size_x + dx - 1, to, :] = jnp.where(absent | no_high_x, fill, high)
            place += count

    row_at = lax.broadcasted_iota(jnp.int32, (wide_y, size_z), 0)
    z_at = lax.broadcasted_iota(jnp.int32, (wide_y, size_z), 1)
    inside_y = ((row_at >= DEEP) | jnp.logical_not(no_low_y)) & ((row_at < DEEP + size_y) | jnp.logical_not(no_high_y))

    def one_exp(x, carry):
        e_w[x] = jnp.exp(0.5 * log_w[x])
        return carry

    lax.fori_loop(0, wide_x, one_exp, 0, unroll=True)

    def one_row(x, carry):
        e = e_w[x]
        total = e_w[x - 1] + e_w[x + 1]
        total = total + pltpu.roll(e, 1, 0) + pltpu.roll(e, wide_y - 1, 0)
        total = total + jnp.where(z_at == 0, 1.0, pltpu.roll(e, 1, 1))
        total = total + jnp.where(z_at == size_z - 1, 1.0, pltpu.roll(e, size_z - 1, 1))
        inside_x = ((x >= DEEP) | jnp.logical_not(no_low_x)) & ((x < DEEP + size_x) | jnp.logical_not(no_high_x))
        delta = jnp.where(inside_y & inside_x, e / (sto_w[x] + e * total), 0.0)
        del_w[x] = delta
        gam_w[x] = delta * e
        bet_w[x] = delta * rec_w[x]
        return carry

    lax.fori_loop(1, wide_x - 1, one_row, 0, unroll=True)
    sub, lane, half = tile_marks(tests)

    def spread(wide, x, y):
        low = jnp.broadcast_to(wide[x, pl.ds(y, 1), :LANES], (8, LANES))
        high = jnp.broadcast_to(wide[x, pl.ds(y, 1), LANES:], (8, LANES))
        return jnp.where(half == 0, low, high)

    def spread_row(x, carry):
        for y in range(1, wide_y - 1):
            gamma_ref[x, y] = spread(gam_w, x, y)
            delta_ref[x, y] = spread(del_w, x, y)
            bet_ref[x, y] = spread(bet_w, x, y)
        return carry

    lax.fori_loop(1, wide_x - 1, spread_row, 0, unroll=True)

    def spread_near(x, carry):
        for y in range(DEEP - 1, DEEP + size_y + 1):
            e = spread(e_w, x, y)
            e_ref[x, y] = e
            inv_e_ref[x, y] = 1.0 / e
        return carry

    lax.fori_loop(DEEP - 1, DEEP + size_x + 1, spread_near, 0, unroll=True)
    z_of = half * LANES + lane
    listed_rows = list_length(per_brick) // LANES
    for test in range(tests):
        packed = table_ref[listed_rows + 1, test]

        @pl.when((packed >> 30) & 1 == 1)
        def _(packed=packed, test=test):
            x, y, top = (packed >> 12) & 15, (packed >> 8) & 15, packed & 255
            hit = (z_of >= top) & (z_of < top + SCREEN) & (sub % tests == test)
            bet_ref[x, y] = bet_ref[x, y] - jnp.where(hit, delta_ref[x, y] * rate_ref[:, test : test + 1], 0.0)

    sweep(bet_ref, gamma_ref, bet_ref, one_ref, 2, wide_y - 2, lane, half)
    sweep(bet_ref, gamma_ref, one_ref, two_ref, 3, wide_y - 3, lane, half)

    def one_head(x, carry):
        head_ref[x, 3 : wide_y - 3] = two_ref[x, 3 : wide_y - 3] * inv_e_ref[x, 3 : wide_y - 3]
        return carry

    lax.fori_loop(3, wide_x - 3, one_head, 0, unroll=True)
    slot_of = lane - per_brick * (sub % tests)
    gathered = jnp.zeros((8, LANES), jnp.float32)
    for rank in range(per_brick):
        packed = table_ref[listed_rows, rank]
        x, y, top = (packed >> 12) & 15, (packed >> 8) & 15, packed & 255
        hit = (z_of >= top) & (z_of < top + SCREEN)
        mean = jnp.sum(jnp.where(hit, head_ref[x, y], 0.0), axis=1, keepdims=True)
        gathered = jnp.where(slot_of == rank, mean, gathered)
    residual = jnp.sum(gathered, axis=0, keepdims=True) * (1.0 / SCREEN) - obs_ref[...]
    row_ref[...] = jnp.broadcast_to(residual[None], row_ref.shape)


def adjoint_kernel(
    tests,
    per_brick,
    split,
    scale,
    n_wells,
    resid_ref,
    table_ref,
    gamma_ref,
    delta_ref,
    e_ref,
    inv_e_ref,
    head_ref,
    *rest,
):
    outs, (weight_ref, bet_ref, one_ref, two_ref, adj_ref) = rest[:-5], rest[-5:]
    wide_x, wide_y = gamma_ref.shape[:2]
    size_x, size_y = wide_x - 2 * DEEP, wide_y - 2 * DEEP
    sub, lane, half = tile_marks(tests)
    z_of = half * LANES + lane
    resid = resid_ref[:, 0, :]
    squares = jnp.sum(resid * resid, axis=0, keepdims=True)
    row_lane = lax.broadcasted_iota(jnp.int32, (1, LANES), 1)
    misfit = jnp.zeros((1, LANES), jnp.float32)
    for test in range(tests):
        mine = row_lane // per_brick == test
        total = jnp.sum(jnp.where(mine, squares, 0.0), axis=1, keepdims=True)
        misfit = jnp.where(mine, total / n_wells + EPSILON, misfit)
    weight_ref[...] = resid / misfit

    def clear(x, carry):
        bet_ref[x] = jnp.zeros(bet_ref.shape[1:], jnp.float32)
        return carry

    lax.fori_loop(0, wide_x, clear, 0, unroll=True)
    slot_of = lane - per_brick * (sub % tests)

    listed_rows = list_length(per_brick) // LANES
    pick = per_brick * (sub % tests)

    def some_wells(turn, carry):
        todo = []
        for step in range(WELLS_AT_ONCE):
            place = turn * WELLS_AT_ONCE + step
            packed = table_ref[place // LANES, place % LANES]
            x, y, top = (packed >> 12) & 15, (packed >> 8) & 15, packed & 255
            slot = (packed >> 16) & 0x1FFF
            row = jnp.broadcast_to(weight_ref[pl.ds(slot // per_brick, 1), :], (8, LANES))
            value = jnp.take_along_axis(row, pick + slot % per_brick, axis=1, mode="promise_in_bounds")
            hit = (z_of >= top) & (z_of < top + SCREEN)
            todo.append((x, y, jnp.where(hit, value, 0.0)))
        for x, y, value in todo:
            bet_ref[x, y] = bet_ref[x, y] + value
        return carry

    turns = (table_ref[listed_rows + 2, 0] + WELLS_AT_ONCE - 1) // WELLS_AT_ONCE
    lax.fori_loop(0, turns, some_wells, 0)

    def scaled(x, carry):
        bet_ref[x, 1 : wide_y - 1] = bet_ref[x, 1 : wide_y - 1] * delta_ref[x, 1 : wide_y - 1]
        return carry

    lax.fori_loop(1, wide_x - 1, scaled, 0, unroll=True)
    sweep(bet_ref, gamma_ref, bet_ref, one_ref, 2, wide_y - 2, lane, half)
    sweep(bet_ref, gamma_ref, one_ref, two_ref, 3, wide_y - 3, lane, half)

    def one_adjoint(x, carry):
        adj_ref[x, 3 : wide_y - 3] = two_ref[x, 3 : wide_y - 3] * inv_e_ref[x, 3 : wide_y - 3]
        return carry

    lax.fori_loop(3, wide_x - 3, one_adjoint, 0, unroll=True)
    own_y = slice(DEEP, DEEP + size_y)

    def one_row(x, carry):
        e, head, adjoint = e_ref[x, own_y], head_ref[x, own_y], adj_ref[x, own_y]

        def face(near_x, near_y):
            gap = (head - head_ref[near_x, near_y]) * (adjoint - adj_ref[near_x, near_y])
            return e_ref[near_x, near_y] * gap

        total = face(x - 1, own_y) + face(x + 1, own_y)
        total = total + face(x, slice(DEEP - 1, DEEP + size_y - 1)) + face(x, slice(DEEP + 1, DEEP + size_y + 1))
        total = total * e
        last = (lane == LANES - 1) & (half == 1)
        e_next = jnp.where(last, 1.0, shift_up(e, lane, half))
        gap = (head - shift_up(head, lane, half)) * (adjoint - shift_up(adjoint, lane, half))
        upper = e * e_next * gap
        begin = (lane == 0) & (half == 0)
        lower = jnp.where(begin, e * head * adjoint, shift_down(upper, lane, half))
        total = (total + upper + lower) * scale
        total = total + pltpu.roll(total, 7, 1)
        total = total + pltpu.roll(total, 6, 1)
        for y in range(size_y):
            low, high = total[y, 0:1], total[y, 4:5]
            if split:
                first = lax.axis_index("test") == 0
                outs[0][x - DEEP, pl.ds(y, 1), :] = jnp.where(first, low, high)
                outs[1][x - DEEP, pl.ds(y, 1), :] = jnp.where(first, high, low)
            else:
                outs[0][x - DEEP, pl.ds(y, 1), :LANES] = low
                outs[0][x - DEEP, pl.ds(y, 1), LANES:] = high
        return carry

    lax.fori_loop(DEEP, DEEP + size_x, one_row, 0, unroll=True)


def vmem():
    return pl.BlockSpec(memory_space=pltpu.VMEM)


def smem():
    return pl.BlockSpec(memory_space=pltpu.SMEM)


def f32(*shape):
    return jax.ShapeDtypeStruct(shape, jnp.float32)


def i32(*shape):
    return jax.ShapeDtypeStruct(shape, jnp.int32)


PARAMS = pltpu.CompilerParams(vmem_limit_bytes=24 * 1024 * 1024)


def local(log_conductivity, storage, recharge, pump_rate, pump_well, observed, owner, screen_column, screen_top):
    size_x, size_y, size_z = log_conductivity.shape
    tests = pump_rate.shape[0]
    n_wells = owner.shape[0]
    groups, n_bx, n_by = lax.axis_size("test"), lax.axis_size("bx"), lax.axis_size("by")
    bricks = n_bx * n_by
    per_brick = n_wells // bricks
    plan = row_plan(size_y)
    rows_y = (3 * DEEP - 2) * size_x
    rows_x = (3 * DEEP - 2) * size_y + corner_rows(plan)
    wide_x, wide_y = size_x + 2 * DEEP, size_y + 2 * DEEP

    inputs = (
        log_conductivity,
        storage,
        recharge,
        owner.reshape(1, n_wells),
        screen_column.reshape(1, n_wells),
        screen_top.reshape(1, n_wells),
        observed,
        pump_rate.reshape(1, tests),
        pump_well.reshape(1, tests),
    )
    log_k, sto, rec, owner, column, top, observed, rate, wells_pumped, even_y, odd_y = pl.pallas_call(
        load_and_pack,
        out_shape=[jax.ShapeDtypeStruct(a.shape, a.dtype) for a in inputs] + [f32(rows_y, size_z)] * 2,
        in_specs=[pl.BlockSpec(memory_space=pltpu.HBM)] * len(inputs),
        out_specs=[vmem()] * (len(inputs) + 2),
        scratch_shapes=[pltpu.SemaphoreType.DMA((len(inputs),))],
        compiler_params=PARAMS,
        name="load_and_pack",
    )(*[pltpu.with_memory_space_constraint(a, pltpu.HBM) for a in inputs])
    got_even_y, got_odd_y = swap_sides(even_y, odd_y, "by", groups)

    bx, by = lax.axis_index("bx"), lax.axis_index("by")
    well_x = (owner // n_by - bx) * size_x + column // size_y + DEEP
    well_y = (owner % n_by - by) * size_y + column % size_y + DEEP
    out_x = jnp.maximum(jnp.maximum(DEEP - well_x, well_x - (DEEP + size_x - 1)), 0)
    out_y = jnp.maximum(jnp.maximum(DEEP - well_y, well_y - (DEEP + size_y - 1)), 0)
    in_window = (out_x + out_y < DEEP).astype(jnp.float32)
    owned = ((out_x == 0) & (out_y == 0)).astype(jnp.float32)
    xy = ((well_x & 15) << 4) + (well_y & 15)
    table, obs = pl.pallas_call(
        functools.partial(wells_kernel, tests, per_brick, bricks=bricks),
        out_shape=[i32(8, LANES), f32(1, LANES)],
        in_specs=[vmem()] * 7,
        out_specs=[vmem()] * 2,
        compiler_params=PARAMS,
        name="wells",
    )(owner, xy, top, in_window, owned, observed, wells_pumped)

    even_x, odd_x = pl.pallas_call(
        functools.partial(pack_x, plan),
        out_shape=[f32(rows_x, size_z)] * 2,
        in_specs=[vmem()] * 5,
        out_specs=[vmem()] * 2,
        compiler_params=PARAMS,
        name="pack_x",
    )(log_k, sto, rec, got_even_y, got_odd_y)
    got_even_x, got_odd_x = swap_sides(even_x, odd_x, "bx", groups)

    tiles = (wide_x, wide_y, 8, LANES)
    wide = (wide_x, wide_y, size_z)
    gamma, delta, e, inv_e, head, row = pl.pallas_call(
        functools.partial(heads_kernel, plan, tests, per_brick),
        out_shape=[f32(*tiles)] * 5 + [f32(bricks, 1, LANES)],
        in_specs=[vmem()] * 7 + [smem(), vmem(), vmem()],
        out_specs=[vmem()] * 6,
        scratch_shapes=[pltpu.VMEM(wide, jnp.float32)] * 7 + [pltpu.VMEM(tiles, jnp.float32)] * 3,
        compiler_params=PARAMS,
        name="heads",
    )(log_k, sto, rec, got_even_y, got_odd_y, got_even_x, got_odd_x, table, obs, rate)

    residuals = lax.all_to_all(row, ("bx", "by"), 0, 0)

    all_tests = tests * groups
    split = groups == 2
    out_shape = [f32(size_x, size_y, LANES)] * 2 if split else [f32(size_x, size_y, size_z)]
    partial = pl.pallas_call(
        functools.partial(adjoint_kernel, tests, per_brick, split, -0.5 / all_tests, n_wells),
        out_shape=out_shape,
        in_specs=[vmem(), smem()] + [vmem()] * 5,
        out_specs=[vmem()] * len(out_shape),
        scratch_shapes=[pltpu.VMEM((bricks, LANES), jnp.float32)] + [pltpu.VMEM(tiles, jnp.float32)] * 4,
        compiler_params=PARAMS,
        name="adjoint",
    )(residuals, table, gamma, delta, e, inv_e, head)
    if split:
        return partial[0] + lax.ppermute(partial[1], "test", [(0, 1), (1, 0)])
    return lax.psum_scatter(partial[0], "test", scatter_dimension=2, tiled=True)


def solution(mesh):
    placed = (
        P("bx", "by", None),
        P("bx", "by", None),
        P("bx", "by", None),
        P("test"),
        P("test"),
        P("test", None),
        P(),
        P(),
        P(),
    )
    return jax.shard_map(local, mesh=mesh, in_specs=placed, out_specs=P("bx", "by", "test"), check_vma=False)
```

```python
import functools

import jax
import jax.numpy as jnp
from jax import lax
from jax.experimental import pallas as pl
from jax.experimental.pallas import tpu as pltpu
from jax.sharding import PartitionSpec as P

SCREEN = 8
LANES = 128
DEEP = 4
EPSILON = 1e-06
WELL_CHUNK = 512
WELLS_AT_ONCE = 16


def list_length(per_brick):
    return -(-6 * per_brick // LANES) * LANES


def slab_plan(half_x):
    plan = []
    for field, reach in ((0, DEEP), (1, DEEP - 1), (2, DEEP - 1)):
        for x in range(half_x + 2 * DEEP):
            rows = reach - max(DEEP - x, x - (DEEP + half_x - 1), 0)
            if rows > 0:
                plan.append((field, x, rows))
    return plan


def pair_of(test, tests):
    return test ^ 1 if (test ^ 1) < tests else test


def side_partners(count, tests):
    even, odd = [], []
    for test in range(tests):
        for place in range(count):
            me = test * count + place
            other = pair_of(test, tests) * count + place
            up = place ^ 1
            even.append((me, test * count + up if up < count else other))
            down = ((place + 1) ^ 1) - 1
            odd.append((me, test * count + down if 0 <= down < count else other))
    return even, odd


def circle(count, tests):
    pairs = []
    for test in range(tests):
        for place in range(count):
            to = place + 1 if test % 2 == 0 else place - 1
            me = test * count + place
            pairs.append((me, test * count + to if 0 <= to < count else pair_of(test, tests) * count + place))
    return pairs


def second_half():
    return lax.axis_index("test") % 2 == 1


def edge_kernel(log_ref, sto_ref, rec_ref, slab_ref, sems):
    size_x = log_ref.shape[0]
    copies, place = [], 0
    for field, (ref, reach) in enumerate(((log_ref, DEEP), (sto_ref, DEEP - 1), (rec_ref, DEEP - 1))):
        first = jnp.where(second_half(), 0, size_x - reach)
        copies.append(pltpu.make_async_copy(ref.at[pl.ds(first, reach)], slab_ref.at[pl.ds(place, reach)], sems.at[field]))
        place += reach
    for copy in copies:
        copy.start()
    for copy in copies:
        copy.wait()


def load_kernel(observed, rate, pumped, *refs):
    sources, loaded, facts_ref, (rate_ref, pumped_ref, sems) = refs[:6], refs[7:13], refs[13], refs[14:]
    tests = observed.shape[0]
    moves = [(observed, facts_ref.at[pl.ds(0, tests)]), (rate, rate_ref), (pumped, pumped_ref)] + list(zip(sources, loaded))
    copies = [pltpu.make_async_copy(a, b, sems.at[i]) for i, (a, b) in enumerate(moves)]
    for copy in copies:
        copy.start()
    for copy in copies:
        copy.wait()
    facts_ref[tests : tests + 1, 0:tests] = rate_ref[...]
    facts_ref[tests + 1 : tests + 2, 0:tests] = pumped_ref[...].astype(jnp.float32)


def wells_kernel(tests, per_brick, bricks, owner_ref, place_ref, top_ref, window_ref, owned_ref, facts_ref, other_ref, _, table_ref, obs_ref, clear_ref, clear_more_ref):
    n_wells = owner_ref.shape[1]
    chunk = WELL_CHUNK if n_wells % WELL_CHUNK == 0 else n_wells
    listed = list_length(per_brick)
    before = lax.broadcasted_iota(jnp.int32, (chunk, chunk), 0) < lax.broadcasted_iota(jnp.int32, (chunk, chunk), 1)
    before = jnp.where(before, 1.0, 0.0).astype(jnp.bfloat16)
    brick_at = lax.broadcasted_iota(jnp.int32, (bricks, chunk), 0)
    list_at = lax.broadcasted_iota(jnp.int32, (listed, chunk), 0).astype(jnp.float32)
    own_at = (lax.broadcasted_iota(jnp.int32, (LANES, chunk), 0) % per_brick).astype(jnp.float32)
    lane_at = lax.broadcasted_iota(jnp.int32, (1, chunk), 1).astype(jnp.float32)
    first_row = lax.broadcasted_iota(jnp.int32, (16, chunk), 0) == 0
    swapped = second_half()
    mine, theirs = facts_ref[...], other_ref[...]
    facts = (jnp.where(swapped, theirs, mine), jnp.where(swapped, mine, theirs))
    total = jnp.zeros((bricks + 16, 1), jnp.float32)
    result = jnp.zeros((32, listed + LANES + 16), jnp.float32)
    for start in range(0, n_wells, chunk):
        part = slice(start, start + chunk)
        owner = owner_ref[:, part]
        near, own = window_ref[:, part], owned_ref[:, part]
        ones = jnp.where(brick_at == owner, 1.0, 0.0)
        counted = jnp.concatenate([ones, jnp.where(first_row, near, 0.0)], axis=0)
        prefix = jnp.dot(counted.astype(jnp.bfloat16), before, preferred_element_type=jnp.float32) + total
        total = total + jnp.sum(counted, axis=1, keepdims=True)
        rank = jnp.sum(ones * prefix[:bricks], axis=0, keepdims=True)
        in_list = jnp.where((list_at == prefix[bricks : bricks + 1]) & (near > 0.5), 1.0, 0.0)
        in_own = jnp.where((own_at == rank) & (own > 0.5), 1.0, 0.0)
        pumps = []
        for test in range(2 * tests):
            pumped = facts[test // tests][tests + 1 : tests + 2, test % tests : test % tests + 1]
            pumps.append(jnp.where(lane_at + float(start) == pumped, 1.0, 0.0))
        pumps.append(jnp.zeros((16 - 2 * tests, chunk), jnp.float32))
        chosen = jnp.concatenate([in_list, in_own] + pumps, axis=0).astype(jnp.bfloat16)
        rows = [number.astype(jnp.float32) for number in (place_ref[:, part], top_ref[:, part], owner)] + [rank, near]
        for test in range(2 * tests):
            value = facts[test // tests][test % tests : test % tests + 1, part]
            for _ in range(3):
                piece = value.astype(jnp.bfloat16).astype(jnp.float32)
                rows.append(piece)
                value = value - piece
        rows.append(jnp.zeros((32 - len(rows), chunk), jnp.float32))
        carried = jnp.concatenate(rows, axis=0).astype(jnp.bfloat16)
        result = result + lax.dot_general(carried, chosen, (((1,), (1,)), ((), ())), preferred_element_type=jnp.float32)
    numbers = [result[row : row + 1].astype(jnp.int32) for row in range(5)]
    words = numbers[0] + (numbers[1] << 8) + (numbers[2] << 16) + (numbers[3] << 24) + (numbers[4] << 30)
    listed_rows = listed // LANES
    for row in range(listed_rows + 1):
        table_ref[row : row + 1, :] = words[:, row * LANES : (row + 1) * LANES]
    table_ref[listed_rows + 1 : listed_rows + 2, :16] = words[:, listed + LANES :]
    found = jnp.broadcast_to(total[bricks : bricks + 1], (1, LANES)).astype(jnp.int32)
    table_ref[listed_rows + 2 : listed_rows + 3, :] = found
    lane = lax.broadcasted_iota(jnp.int32, (1, LANES), 1)
    for part in range(2):
        values = jnp.zeros((1, LANES), jnp.float32)
        for test in range(tests):
            first = 5 + 3 * (part * tests + test)
            pieces = [result[row : row + 1, listed : listed + LANES] for row in range(first, first + 3)]
            values = jnp.where(lane // per_brick == test, pieces[0] + (pieces[1] + pieces[2]), values)
        obs_ref[part : part + 1, :] = values
        obs_ref[3 + part : 4 + part, 0:tests] = facts[part][tests : tests + 1, 0:tests]
    obs_ref[2:3, :] = result[4:5, listed : listed + LANES]
    clear_ref[...] = jnp.zeros(clear_ref.shape, jnp.float32)
    clear_more_ref[...] = jnp.zeros(clear_ref.shape, jnp.float32)


def at_window_rows(value):
    return pltpu.roll(jnp.concatenate([value, value], axis=0), DEEP, 0)


def window_kernel(log_ref, sto_ref, rec_ref, e_ref, sto_w, rec_w):
    base = jnp.where(second_half(), 0, DEEP)
    for x in range(log_ref.shape[0]):
        e_ref[base + x] = at_window_rows(jnp.exp(0.5 * log_ref[x]))
        sto_w[base + x] = at_window_rows(sto_ref[x])
        rec_w[base + x] = at_window_rows(rec_ref[x])


def pack_y(plan, slab_ref, e_in, sto_in, rec_in, e_ref, sto_w, rec_w, even_ref, odd_ref):
    size_y = slab_ref.shape[1]
    swapped = second_half()
    bx = lax.axis_index("bx")
    absent = jnp.where(swapped, bx == lax.axis_size("bx") - 1, bx == 0)
    y_even = lax.axis_index("by") % 2 == 0
    wides = (e_ref, sto_w, rec_w)
    half_x = e_ref.shape[0] - 2 * DEEP
    place = 0
    for field, reach in enumerate((DEEP, DEEP - 1, DEEP - 1)):
        base = jnp.where(swapped, DEEP + half_x, DEEP - reach)
        for i in range(reach):
            value = slab_ref[place + i]
            value = jnp.exp(0.5 * value) if field == 0 else value
            wides[field][base + i] = at_window_rows(jnp.where(absent, (1.0, 1.0, 0.0)[field], value))
        place += reach
    place = 0
    for field, x, count in plan:
        wide = wides[field]
        up = wide[x, DEEP + size_y - count : DEEP + size_y, :]
        down = wide[x, DEEP : DEEP + count, :]
        at = pl.ds(place, count)
        even_ref[at, :] = jnp.where(y_even, up, down)
        odd_ref[at, :] = jnp.where(y_even, down, up)
        place += count


def field_rows(e_ref, sto_w, rec_w, delta_ref, gamma_ref, beta_ref):
    wide_x, wide_y, size_z = e_ref.shape
    half_x, size_y = wide_x - 2 * DEEP, wide_y - 2 * DEEP
    bx, by, swapped = lax.axis_index("bx"), lax.axis_index("by"), second_half()
    row_at = lax.broadcasted_iota(jnp.int32, (wide_y, size_z), 0)
    z_at = lax.broadcasted_iota(jnp.int32, (wide_y, size_z), 1)
    inside_y = ((row_at >= DEEP) | (by > 0)) & ((row_at < DEEP + size_y) | (by < lax.axis_size("by") - 1))
    for x in range(1, wide_x - 1):
        e = e_ref[x]
        total = e_ref[x - 1] + e_ref[x + 1]
        total = total + pltpu.roll(e, 1, 0) + pltpu.roll(e, wide_y - 1, 0)
        total = total + jnp.where(z_at == 0, 1.0, pltpu.roll(e, 1, 1))
        total = total + jnp.where(z_at == size_z - 1, 1.0, pltpu.roll(e, size_z - 1, 1))
        inside = inside_y
        if x < DEEP:
            inside = inside & (swapped | (bx > 0))
        if x >= DEEP + half_x:
            inside = inside & (jnp.logical_not(swapped) | (bx < lax.axis_size("bx") - 1))
        delta = jnp.where(inside, e / (sto_w[x] + e * total), 0.0)
        delta_ref[x] = delta
        gamma_ref[x] = delta * e
        beta_ref[x] = delta * rec_w[x]


def spread(ref, x, low, high):
    tiles = []
    for y in range(low, high):
        halves = [ref[x, pl.ds(y, 1), part * LANES : (part + 1) * LANES] for part in range(2)]
        tiles.append(jnp.stack([jnp.broadcast_to(half, (8, LANES)) for half in halves]))
    return jnp.stack(tiles)


def lanes():
    return lax.broadcasted_iota(jnp.int32, (8, LANES), 1)


def z_down(values, edge):
    turned = pltpu.roll(values, 1, 3)
    first = lanes() == 0
    return jnp.stack([jnp.where(first, edge, turned[:, 0]), jnp.where(first, turned[:, 0], turned[:, 1])], axis=1)


def z_up(values, edge):
    turned = pltpu.roll(values, LANES - 1, 3)
    last = lanes() == LANES - 1
    return jnp.stack([jnp.where(last, turned[:, 1], turned[:, 0]), jnp.where(last, edge, turned[:, 1])], axis=1)


def columns(ref, wide_y, x, low, high):
    return ref[x * wide_y + low : x * wide_y + high]


def sweep(source_ref, gamma_ref, from_ref, x, low, high):
    wide_y = gamma_ref.shape[1]
    centre = columns(from_ref, wide_y, x, low, high)
    total = columns(from_ref, wide_y, x - 1, low, high) + columns(from_ref, wide_y, x + 1, low, high)
    total = total + columns(from_ref, wide_y, x, low - 1, high - 1) + columns(from_ref, wide_y, x, low + 1, high + 1)
    total = total + z_down(centre, 0.0) + z_up(centre, 0.0)
    return columns(source_ref, wide_y, x, low, high) + spread(gamma_ref, x, low, high) * total


def reached(wide_x, wide_y, reach):
    cells = []
    for x in range(DEEP - reach, wide_x - DEEP + reach):
        left = reach - max(DEEP - x, x - (wide_x - DEEP - 1), 0)
        cells.append((x, DEEP - left, wide_y - DEEP + left))
    return cells


def solve(bet_ref, gamma_ref, inv_ref, one_ref, two_ref):
    wide_x, wide_y, _ = gamma_ref.shape
    for x, low, high in reached(wide_x, wide_y, DEEP - 2):
        one_ref[x * wide_y + low : x * wide_y + high] = sweep(bet_ref, gamma_ref, bet_ref, x, low, high)
    for x, low, high in reached(wide_x, wide_y, DEEP - 3):
        scaled = sweep(bet_ref, gamma_ref, one_ref, x, low, high)
        two_ref[x * wide_y + low : x * wide_y + high] = scaled * spread(inv_ref, x, low, high)


def z_of_tile():
    return jnp.stack([lanes(), lanes() + LANES])


def unpack(packed):
    return packed & 255, (packed >> 8) & 255


def heads_kernel(plan, tests, per_brick, even_ref, odd_ref, e_in, sto_in, rec_in, table_in, obs_ref,
                 e_ref, delta_ref, gamma_ref, inv_ref, head_ref, row_ref, sto_w, rec_w, beta_ref, bet_ref, one_ref, table_ref, sem):
    wide_x, wide_y, _ = e_ref.shape
    table_copy = pltpu.make_async_copy(table_in, table_ref, sem)
    table_copy.start()
    by = lax.axis_index("by")
    y_even = by % 2 == 0
    no_low, no_high = by == 0, by == lax.axis_size("by") - 1
    place = 0
    for field, x, count in plan:
        wide = (e_ref, sto_w, rec_w)[field]
        fill = (1.0, 1.0, 0.0)[field]
        got_e, got_o = even_ref[pl.ds(place, count), :], odd_ref[pl.ds(place, count), :]
        low, high = jnp.where(y_even, got_o, got_e), jnp.where(y_even, got_e, got_o)
        wide[x, DEEP - count : DEEP, :] = jnp.where(no_low, fill, low)
        wide[x, wide_y - DEEP : wide_y - DEEP + count, :] = jnp.where(no_high, fill, high)
        place += count
    field_rows(e_ref, sto_w, rec_w, delta_ref, gamma_ref, beta_ref)
    for x in range(3, wide_x - 3):
        inv_ref[x] = 1.0 / e_ref[x]
    for x, low, high in reached(wide_x, wide_y, DEEP - 1):
        bet_ref[x * wide_y + low : x * wide_y + high] = spread(beta_ref, x, low, high)
    sub = lax.broadcasted_iota(jnp.int32, (8, LANES), 0)
    z_of = z_of_tile()
    listed_rows = list_length(per_brick) // LANES
    table_copy.wait()
    pumped = []
    for test in range(2 * tests):
        packed = table_ref[listed_rows + 1, test]
        place, top = unpack(packed)
        near = (packed >> 30) & 1 == 1
        rate = obs_ref[3 + test // tests : 4 + test // tests, test % tests : test % tests + 1]
        delta = delta_ref[place // wide_y, pl.ds(place % wide_y, 1), :]
        delta = jnp.stack([jnp.broadcast_to(delta[:, part * LANES : (part + 1) * LANES], (8, LANES)) for part in range(2)])
        hit = (z_of >= top) & (z_of < top + SCREEN) & (sub == test) & near
        pumped.append((place, jnp.where(hit, delta * rate, 0.0)))
    for place, taken in pumped:
        bet_ref[place] = bet_ref[place] - taken
    solve(bet_ref, gamma_ref, inv_ref, one_ref, head_ref)
    slot_of = lanes() - per_brick * (sub % tests)
    gathered = jnp.zeros((8, LANES), jnp.float32)
    for rank in range(per_brick):
        place, top = unpack(table_ref[listed_rows, rank])
        hit = (z_of >= top) & (z_of < top + SCREEN)
        values = jnp.where(hit, head_ref[place], 0.0)
        gathered = jnp.where(slot_of == rank, jnp.sum(values[0] + values[1], axis=1, keepdims=True), gathered)
    mine = obs_ref[2:3, :] > 0.5
    parts = []
    for part in range(2):
        total = jnp.sum(jnp.where(sub // tests == part, gathered, 0.0), axis=0, keepdims=True)
        parts.append(jnp.where(mine, total * (1.0 / SCREEN) - obs_ref[part : part + 1, :], 0.0))
    row_ref[...] = jnp.broadcast_to(jnp.concatenate(parts, axis=0)[None], row_ref.shape)


def adjoint_kernel(tests, per_brick, n_wells, joined, scale, resid_ref, table_in, clear_ref, clear_more_ref, e_ref, delta_ref, gamma_ref, inv_ref, head_ref,
                   bet_ref, more_ref, adj_ref, send_ref, weight_ref, one_ref, table_ref, sem):
    wide_x, wide_y, _ = e_ref.shape
    table_copy = pltpu.make_async_copy(table_in, table_ref, sem)
    table_copy.start()
    bricks = n_wells // per_brick
    sub = lax.broadcasted_iota(jnp.int32, (8, LANES), 0)
    z_of = z_of_tile()
    resid = resid_ref[:bricks] + resid_ref[bricks:] if joined else resid_ref[...]
    squares = jnp.sum(resid * resid, axis=0)
    lane = lax.broadcasted_iota(jnp.int32, (2, LANES), 1)
    misfit = jnp.zeros((2, LANES), jnp.float32)
    for test in range(tests):
        mine = lane // per_brick == test
        total = jnp.sum(jnp.where(mine, squares, 0.0), axis=1, keepdims=True)
        misfit = jnp.where(mine, total / n_wells + EPSILON, misfit)
    inverse = 1.0 / misfit
    for brick in range(bricks):
        row = resid[brick] * inverse
        weight_ref[brick] = jnp.where(sub < tests, row[0:1], row[1:2])
    listed_rows = list_length(per_brick) // LANES
    pick = per_brick * (sub % tests)

    def some_wells(turn, carry):
        todo = []
        for step in range(WELLS_AT_ONCE):
            packed = table_ref[turn // turns_a_row, (turn % turns_a_row) * WELLS_AT_ONCE + step]
            column, top = unpack(packed)
            brick, rank = (packed >> 16) & 255, (packed >> 24) & 31
            value = jnp.take_along_axis(weight_ref[brick], pick + rank, axis=1, mode="promise_in_bounds")
            todo.append((column, jnp.where((z_of >= top) & (z_of < top + SCREEN), value[None], 0.0)))
        for step, (column, value) in enumerate(todo):
            into_ref = (bet_ref, more_ref)[step % 2]
            into_ref[column] = into_ref[column] + value
        return carry

    turns_a_row = LANES // WELLS_AT_ONCE
    table_copy.wait()
    turns = (table_ref[listed_rows + 2, 0] + WELLS_AT_ONCE - 1) // WELLS_AT_ONCE
    lax.fori_loop(0, turns, some_wells, 0)
    for x, low, high in reached(wide_x, wide_y, DEEP - 1):
        row = pl.ds(x * wide_y + low, high - low)
        bet_ref[row] = (bet_ref[row] + more_ref[row]) * spread(delta_ref, x, low, high)
    solve(bet_ref, gamma_ref, inv_ref, one_ref, adj_ref)

    gradient_half(jnp.where(second_half(), 0, 1), scale, e_ref, head_ref, adj_ref, send_ref)


def keep_kernel(scale, e_ref, head_ref, adj_ref, keep_ref):
    gradient_half(jnp.where(second_half(), 1, 0), scale, e_ref, head_ref, adj_ref, keep_ref)


def gradient_half(part, scale, e_ref, head_ref, adj_ref, out_ref):
    wide_x, wide_y, _ = e_ref.shape
    low, high = DEEP, wide_y - DEEP
    is_first = part == 0
    at_first, at_last = lanes() == 0, lanes() == LANES - 1

    def spread_part(x, first, last):
        rows = [e_ref[x, pl.ds(y, 1), pl.ds(pl.multiple_of(part * LANES, LANES), LANES)] for y in range(first, last)]
        return jnp.stack([jnp.broadcast_to(row, (8, LANES)) for row in rows])

    def tiles(ref, x, first, last, which):
        return ref[x * wide_y + first : x * wide_y + last, which]

    def crossing(values, others, edge, turn, end):
        turned, other = pltpu.roll(values, turn, 2), pltpu.roll(others, turn, 2)
        return jnp.where(end, jnp.where(is_first == (turn != 1), other, edge), turned)

    before = None
    for x in range(DEEP - 1, wide_x - DEEP):
        e, head, adjoint = spread_part(x, low, high), tiles(head_ref, x, low, high, part), tiles(adj_ref, x, low, high, part)
        gap = (head - tiles(head_ref, x + 1, low, high, part)) * (adjoint - tiles(adj_ref, x + 1, low, high, part))
        after = e * spread_part(x + 1, low, high) * gap
        if x >= DEEP:
            total = before + after
            e_y = spread_part(x, low - 1, high + 1)
            head_y, adjoint_y = tiles(head_ref, x, low - 1, high + 1, part), tiles(adj_ref, x, low - 1, high + 1, part)
            sides = e_y[:-1] * e_y[1:] * (head_y[:-1] - head_y[1:]) * (adjoint_y[:-1] - adjoint_y[1:])
            total = total + sides[:-1] + sides[1:]
            halves = [ref[x, low:high, other * LANES : (other + 1) * LANES] for ref in (e_ref,) for other in range(2)]
            e_other = jnp.stack([jnp.broadcast_to(jnp.where(is_first, halves[1], halves[0])[y : y + 1], (8, LANES)) for y in range(high - low)])
            head_other, adjoint_other = tiles(head_ref, x, low, high, 1 - part), tiles(adj_ref, x, low, high, 1 - part)
            for turn, end in ((LANES - 1, at_last), (1, at_first)):
                e_near = crossing(e, e_other, 1.0, turn, end)
                head_near, adjoint_near = crossing(head, head_other, 0.0, turn, end), crossing(adjoint, adjoint_other, 0.0, turn, end)
                total = total + e * e_near * (head - head_near) * (adjoint - adjoint_near)
            total = jnp.sum(total, axis=1, keepdims=True) * scale
            for y in range(high - low):
                out_ref[x - DEEP, pl.ds(y, 1), :] = total[y]
        before = after


def vmem():
    return pl.BlockSpec(memory_space=pltpu.VMEM)


def smem():
    return pl.BlockSpec(memory_space=pltpu.SMEM)


def f32(*shape):
    return jax.ShapeDtypeStruct(shape, jnp.float32)


def i32(*shape):
    return jax.ShapeDtypeStruct(shape, jnp.int32)


PARAMS = pltpu.CompilerParams(vmem_limit_bytes=24 * 1024 * 1024)


def local(log_conductivity, storage, recharge, pump_rate, pump_well, observed, owner, screen_column, screen_top):
    size_x, size_y, size_z = log_conductivity.shape
    half_x = size_x // 2
    tests = pump_rate.shape[0]
    n_wells = owner.shape[0]
    groups, n_bx, n_by = lax.axis_size("test"), lax.axis_size("bx"), lax.axis_size("by")
    bricks = n_bx * n_by
    per_brick = n_wells // bricks
    plan = slab_plan(half_x)
    rows_x = 3 * DEEP - 2
    rows_y = sum(count for _, _, count in plan)
    wide_x, wide_y = half_x + 2 * DEEP, size_y + 2 * DEEP
    tiles = (wide_x * wide_y, 2, 8, LANES)
    table_scratch = [pltpu.SMEM((8, LANES), jnp.int32), pltpu.SemaphoreType.DMA]

    def in_hbm(*arrays):
        return [pltpu.with_memory_space_constraint(a, pltpu.HBM) for a in arrays]

    hbm = pl.BlockSpec(memory_space=pltpu.HBM)
    slab = pl.pallas_call(
        edge_kernel,
        out_shape=f32(rows_x, size_y, size_z),
        in_specs=[hbm] * 3,
        out_specs=vmem(),
        scratch_shapes=[pltpu.SemaphoreType.DMA((3,))],
        compiler_params=PARAMS,
        name="edge",
    )(*in_hbm(log_conductivity, storage, recharge))
    got_x = lax.ppermute(slab, ("test", "bx"), circle(n_bx, groups))

    inputs = (
        observed,
        pump_rate.reshape(1, tests),
        pump_well.reshape(1, tests),
        owner.reshape(1, n_wells),
        screen_column.reshape(1, n_wells),
        screen_top.reshape(1, n_wells),
        log_conductivity,
        storage,
        recharge,
    )
    owner, column, top, log_k, sto, rec, facts = pl.pallas_call(
        load_kernel,
        out_shape=[jax.ShapeDtypeStruct(a.shape, a.dtype) for a in inputs[3:]] + [f32(8, n_wells)],
        in_specs=[hbm] * len(inputs) + [vmem()],
        out_specs=[vmem()] * (len(inputs) - 2),
        scratch_shapes=[pltpu.VMEM((1, tests), jnp.float32), pltpu.VMEM((1, tests), jnp.int32), pltpu.SemaphoreType.DMA((len(inputs),))],
        compiler_params=PARAMS,
        name="load",
    )(*in_hbm(*inputs), slab)
    pairs = [(test, pair_of(test, groups)) for test in range(groups)]
    other_facts = lax.ppermute(facts, "test", pairs)

    bx, by, second = lax.axis_index("bx"), lax.axis_index("by"), lax.axis_index("test") % 2
    well_x = (owner // n_by - bx) * size_x + column // size_y + DEEP - second * half_x
    well_y = (owner % n_by - by) * size_y + column % size_y + DEEP
    out_x = jnp.maximum(jnp.maximum(DEEP - well_x, well_x - (DEEP + half_x - 1)), 0)
    out_y = jnp.maximum(jnp.maximum(DEEP - well_y, well_y - (DEEP + size_y - 1)), 0)
    in_window = (out_x + out_y < DEEP).astype(jnp.float32)
    owned = (out_x + out_y == 0).astype(jnp.float32)
    place = jnp.where(in_window > 0.5, well_x * wide_y + well_y, 0)
    window = f32(wide_x, wide_y, size_z)
    e, sto_w, rec_w = pl.pallas_call(
        window_kernel,
        out_shape=[window] * 3,
        in_specs=[vmem()] * 3,
        out_specs=[vmem()] * 3,
        compiler_params=PARAMS,
        name="window",
    )(log_k, sto, rec)
    e, sto_w, rec_w, even_y, odd_y = pl.pallas_call(
        functools.partial(pack_y, plan),
        out_shape=[window] * 3 + [f32(rows_y, size_z)] * 2,
        in_specs=[vmem()] * 4,
        out_specs=[vmem()] * 5,
        input_output_aliases={1: 0, 2: 1, 3: 2},
        compiler_params=PARAMS,
        name="pack_y",
    )(got_x, e, sto_w, rec_w)
    even, odd = side_partners(n_by, groups)
    got_even = lax.ppermute(even_y, ("test", "by"), even)
    got_odd = lax.ppermute(odd_y, ("test", "by"), odd)

    table, obs, clear, clear_more = pl.pallas_call(
        functools.partial(wells_kernel, tests, per_brick, bricks),
        out_shape=[i32(8, LANES), f32(8, LANES), f32(*tiles), f32(*tiles)],
        in_specs=[vmem()] * 8,
        out_specs=[vmem()] * 4,
        compiler_params=PARAMS,
        name="wells",
    )(owner, place, top, in_window, owned, facts, other_facts, even_y)

    joined = groups == 2
    copies = groups * bricks if joined else bricks
    e, delta, gamma, inverse, head, row, _, _ = pl.pallas_call(
        functools.partial(heads_kernel, plan, tests, per_brick),
        out_shape=[window] * 4 + [f32(*tiles), f32(copies, 2, LANES)] + [window] * 2,
        in_specs=[vmem()] * 7,
        out_specs=[vmem()] * 8,
        scratch_shapes=[pltpu.VMEM((wide_x, wide_y, size_z), jnp.float32)] + [pltpu.VMEM(tiles, jnp.float32)] * 2 + table_scratch,
        input_output_aliases={2: 0, 3: 6, 4: 7},
        compiler_params=PARAMS,
        name="heads",
    )(got_even, got_odd, e, sto_w, rec_w, table, obs)

    if joined:
        residuals = lax.all_to_all(row, ("test", "bx", "by"), 0, 0)
    else:
        residuals = lax.all_to_all(row + lax.ppermute(row, "test", pairs), ("bx", "by"), 0, 0)

    scale = -0.5 / (tests * groups)
    _, _, adjoint, send = pl.pallas_call(
        functools.partial(adjoint_kernel, tests, per_brick, n_wells, joined, scale),
        out_shape=[f32(*tiles)] * 3 + [f32(half_x, size_y, LANES)],
        in_specs=[vmem()] * 9,
        out_specs=[vmem()] * 4,
        scratch_shapes=[pltpu.VMEM((bricks, 8, LANES), jnp.float32), pltpu.VMEM(tiles, jnp.float32)] + table_scratch,
        input_output_aliases={2: 0, 3: 1},
        compiler_params=PARAMS,
        name="adjoint",
    )(residuals, table, clear, clear_more, e, delta, gamma, inverse, head)
    other = lax.ppermute(send, "test", pairs) if joined else send
    keep = pl.pallas_call(
        functools.partial(keep_kernel, scale),
        out_shape=f32(half_x, size_y, LANES),
        in_specs=[vmem()] * 3,
        out_specs=vmem(),
        compiler_params=PARAMS,
        name="keep",
    )(e, head, adjoint)
    if joined:
        return jnp.where(second == 0, jnp.concatenate([keep, other], axis=0), jnp.concatenate([other, keep], axis=0))
    low, high = jnp.where(second == 0, keep, send), jnp.where(second == 0, send, keep)
    half = jnp.concatenate([low, high], axis=2)
    none = jnp.zeros_like(half)
    whole = jnp.where(second == 0, jnp.concatenate([half, none], axis=0), jnp.concatenate([none, half], axis=0))
    return lax.psum_scatter(whole, "test", scatter_dimension=2, tiled=True)


def solution(mesh):
    placed = (
        P("bx", "by", None),
        P("bx", "by", None),
        P("bx", "by", None),
        P("test"),
        P("test"),
        P("test", None),
        P(),
        P(),
        P(),
    )
    return jax.shard_map(local, mesh=mesh, in_specs=placed, out_specs=P("bx", "by", "test"), check_vma=False)
```

```python
import functools

import jax
import jax.numpy as jnp
from jax import lax
from jax.experimental import pallas as pl
from jax.experimental.pallas import tpu as pltpu
from jax.sharding import PartitionSpec as P

SCREEN = 8
LANES = 128
DEEP = 4
EPSILON = 1e-06
WELL_CHUNK = 512
WELLS_AT_ONCE = 16
COLUMNS_AT_ONCE = 1


def list_length(per_brick):
    return -(-6 * per_brick // LANES) * LANES


def slab_plan(half_x):
    plan = []
    for field, reach in ((0, DEEP), (1, DEEP - 1), (2, DEEP - 1)):
        for x in range(half_x + 2 * DEEP):
            rows = reach - max(DEEP - x, x - (DEEP + half_x - 1), 0)
            if rows > 0:
                plan.append((field, x, rows))
    return plan


def pair_of(test, tests):
    return test ^ 1 if (test ^ 1) < tests else test


def side_partners(count, tests):
    even, odd = [], []
    for test in range(tests):
        for place in range(count):
            me = test * count + place
            other = pair_of(test, tests) * count + place
            up = place ^ 1
            even.append((me, test * count + up if up < count else other))
            down = ((place + 1) ^ 1) - 1
            odd.append((me, test * count + down if 0 <= down < count else other))
    return even, odd


def circle(count, tests):
    pairs = []
    for test in range(tests):
        for place in range(count):
            to = place + 1 if test % 2 == 0 else place - 1
            me = test * count + place
            pairs.append((me, test * count + to if 0 <= to < count else pair_of(test, tests) * count + place))
    return pairs


def second_half():
    return lax.axis_index("test") % 2 == 1


def edge_kernel(log_ref, sto_ref, rec_ref, slab_ref, sems):
    size_x = log_ref.shape[0]
    copies, place = [], 0
    for field, (ref, reach) in enumerate(((log_ref, DEEP), (sto_ref, DEEP - 1), (rec_ref, DEEP - 1))):
        first = jnp.where(second_half(), 0, size_x - reach)
        copies.append(pltpu.make_async_copy(ref.at[pl.ds(first, reach)], slab_ref.at[pl.ds(place, reach)], sems.at[field]))
        place += reach
    for copy in copies:
        copy.start()
    for copy in copies:
        copy.wait()


def load_kernel(observed, rate, pumped, *refs):
    sources, loaded, facts_ref, (rate_ref, pumped_ref, sems) = refs[:6], refs[7:13], refs[13], refs[14:]
    tests = observed.shape[0]
    moves = [(observed, facts_ref.at[pl.ds(0, tests)]), (rate, rate_ref), (pumped, pumped_ref)] + list(zip(sources, loaded))
    copies = [pltpu.make_async_copy(a, b, sems.at[i]) for i, (a, b) in enumerate(moves)]
    for copy in copies:
        copy.start()
    for copy in copies:
        copy.wait()
    facts_ref[tests : tests + 1, 0:tests] = rate_ref[...]
    facts_ref[tests + 1 : tests + 2, 0:tests] = pumped_ref[...].astype(jnp.float32)


def wells_kernel(tests, per_brick, bricks, owner_ref, place_ref, top_ref, window_ref, owned_ref, facts_ref, other_ref, _, table_ref, obs_ref, clear_ref, clear_more_ref):
    n_wells = owner_ref.shape[1]
    chunk = WELL_CHUNK if n_wells % WELL_CHUNK == 0 else n_wells
    listed = list_length(per_brick)
    before = lax.broadcasted_iota(jnp.int32, (chunk, chunk), 0) < lax.broadcasted_iota(jnp.int32, (chunk, chunk), 1)
    before = jnp.where(before, 1.0, 0.0).astype(jnp.bfloat16)
    brick_at = lax.broadcasted_iota(jnp.int32, (bricks, chunk), 0)
    list_at = lax.broadcasted_iota(jnp.int32, (listed, chunk), 0).astype(jnp.float32)
    own_at = (lax.broadcasted_iota(jnp.int32, (LANES, chunk), 0) % per_brick).astype(jnp.float32)
    lane_at = lax.broadcasted_iota(jnp.int32, (1, chunk), 1).astype(jnp.float32)
    first_row = lax.broadcasted_iota(jnp.int32, (16, chunk), 0) == 0
    swapped = second_half()
    mine, theirs = facts_ref[...], other_ref[...]
    facts = (jnp.where(swapped, theirs, mine), jnp.where(swapped, mine, theirs))
    total = jnp.zeros((bricks + 16, 1), jnp.float32)
    found = jnp.zeros((listed + LANES + 16, 32), jnp.float32)
    result = jnp.zeros((32, LANES), jnp.float32)
    for start in range(0, n_wells, chunk):
        part = slice(start, start + chunk)
        owner = owner_ref[:, part]
        near, own = window_ref[:, part], owned_ref[:, part]
        ones = jnp.where(brick_at == owner, 1.0, 0.0)
        counted = jnp.concatenate([ones, jnp.where(first_row, near, 0.0)], axis=0)
        prefix = jnp.dot(counted.astype(jnp.bfloat16), before, preferred_element_type=jnp.float32) + total
        total = total + jnp.sum(counted, axis=1, keepdims=True)
        rank = jnp.sum(ones * prefix[:bricks], axis=0, keepdims=True)
        in_list = jnp.where((list_at == prefix[bricks : bricks + 1]) & (near > 0.5), 1.0, 0.0)
        in_own = jnp.where((own_at == rank) & (own > 0.5), 1.0, 0.0)
        pumps = []
        for test in range(2 * tests):
            pumped = facts[test // tests][tests + 1 : tests + 2, test % tests : test % tests + 1]
            pumps.append(jnp.where(lane_at + float(start) == pumped, 1.0, 0.0))
        pumps.append(jnp.zeros((16 - 2 * tests, chunk), jnp.float32))
        chosen = jnp.concatenate([in_list, in_own] + pumps, axis=0).astype(jnp.bfloat16)
        rows = [number.astype(jnp.float32) for number in (place_ref[:, part], top_ref[:, part], owner)] + [rank, near]
        for test in range(2 * tests):
            value = facts[test // tests][test % tests : test % tests + 1, part]
            for _ in range(3):
                piece = value.astype(jnp.bfloat16).astype(jnp.float32)
                rows.append(piece)
                value = value - piece
        rows.append(jnp.zeros((32 - len(rows), chunk), jnp.float32))
        carried = jnp.concatenate(rows, axis=0).astype(jnp.bfloat16)
        over_wells = (((1,), (1,)), ((), ()))
        found = found + lax.dot_general(chosen, carried, over_wells, preferred_element_type=jnp.float32)
        result = result + lax.dot_general(carried, chosen[listed : listed + LANES], over_wells, preferred_element_type=jnp.float32)
    column = lax.broadcasted_iota(jnp.int32, found.shape, 1)
    low = jnp.where(column == 0, 1.0, jnp.where(column == 1, 256.0, 0.0))
    high = jnp.where(column == 2, 1.0, jnp.where(column == 3, 256.0, jnp.where(column == 4, 16384.0, 0.0)))
    low, high = (jnp.sum(found * weights, axis=1, keepdims=True).astype(jnp.int32) for weights in (low, high))
    table_ref[0 : listed + LANES + 16, :] = low + (high << 16)
    table_ref[listed + LANES + 16 :, :] = jnp.broadcast_to(total[bricks : bricks + 1], (8, 1)).astype(jnp.int32)
    lane = lax.broadcasted_iota(jnp.int32, (1, LANES), 1)
    for part in range(2):
        values = jnp.zeros((1, LANES), jnp.float32)
        for test in range(tests):
            first = 5 + 3 * (part * tests + test)
            pieces = [result[row : row + 1] for row in range(first, first + 3)]
            values = jnp.where(lane // per_brick == test, pieces[0] + (pieces[1] + pieces[2]), values)
        obs_ref[part : part + 1, :] = values
        obs_ref[3 + part : 4 + part, 0:tests] = facts[part][tests : tests + 1, 0:tests]
    obs_ref[2:3, :] = result[4:5]
    clear_ref[...] = jnp.zeros(clear_ref.shape, jnp.float32)
    clear_more_ref[...] = jnp.zeros(clear_ref.shape, jnp.float32)


def at_window_rows(value):
    return pltpu.roll(jnp.concatenate([value, value], axis=0), DEEP, 0)


def window_kernel(log_ref, sto_ref, rec_ref, e_ref, sto_w, rec_w):
    base = jnp.where(second_half(), 0, DEEP)
    for x in range(log_ref.shape[0]):
        e_ref[base + x] = at_window_rows(jnp.exp(0.5 * log_ref[x]))
        sto_w[base + x] = at_window_rows(sto_ref[x])
        rec_w[base + x] = at_window_rows(rec_ref[x])


def pack_y(plan, slab_ref, e_in, sto_in, rec_in, e_ref, sto_w, rec_w, even_ref, odd_ref):
    size_y = slab_ref.shape[1]
    swapped = second_half()
    bx = lax.axis_index("bx")
    absent = jnp.where(swapped, bx == lax.axis_size("bx") - 1, bx == 0)
    y_even = lax.axis_index("by") % 2 == 0
    wides = (e_ref, sto_w, rec_w)
    half_x = e_ref.shape[0] - 2 * DEEP
    place = 0
    for field, reach in enumerate((DEEP, DEEP - 1, DEEP - 1)):
        base = jnp.where(swapped, DEEP + half_x, DEEP - reach)
        for i in range(reach):
            value = slab_ref[place + i]
            value = jnp.exp(0.5 * value) if field == 0 else value
            wides[field][base + i] = at_window_rows(jnp.where(absent, (1.0, 1.0, 0.0)[field], value))
        place += reach
    place = 0
    for field, x, count in plan:
        wide = wides[field]
        up = wide[x, DEEP + size_y - count : DEEP + size_y, :]
        down = wide[x, DEEP : DEEP + count, :]
        at = pl.ds(place, count)
        even_ref[at, :] = jnp.where(y_even, up, down)
        odd_ref[at, :] = jnp.where(y_even, down, up)
        place += count


def field_rows(e_ref, sto_w, rec_w, delta_ref, gamma_ref, beta_ref):
    wide_x, wide_y, size_z = e_ref.shape
    half_x, size_y = wide_x - 2 * DEEP, wide_y - 2 * DEEP
    bx, by, swapped = lax.axis_index("bx"), lax.axis_index("by"), second_half()
    row_at = lax.broadcasted_iota(jnp.int32, (wide_y, size_z), 0)
    z_at = lax.broadcasted_iota(jnp.int32, (wide_y, size_z), 1)
    inside_y = ((row_at >= DEEP) | (by > 0)) & ((row_at < DEEP + size_y) | (by < lax.axis_size("by") - 1))
    for x in range(1, wide_x - 1):
        e = e_ref[x]
        total = e_ref[x - 1] + e_ref[x + 1]
        total = total + pltpu.roll(e, 1, 0) + pltpu.roll(e, wide_y - 1, 0)
        total = total + jnp.where(z_at == 0, 1.0, pltpu.roll(e, 1, 1))
        total = total + jnp.where(z_at == size_z - 1, 1.0, pltpu.roll(e, size_z - 1, 1))
        inside = inside_y
        if x < DEEP:
            inside = inside & (swapped | (bx > 0))
        if x >= DEEP + half_x:
            inside = inside & (jnp.logical_not(swapped) | (bx < lax.axis_size("bx") - 1))
        delta = jnp.where(inside, e / (sto_w[x] + e * total), 0.0)
        delta_ref[x] = delta
        gamma_ref[x] = delta * e
        beta_ref[x] = delta * rec_w[x]


def spread(ref, x, low, high):
    tiles = []
    for y in range(low, high):
        halves = [ref[x, pl.ds(y, 1), part * LANES : (part + 1) * LANES] for part in range(2)]
        tiles.append(jnp.stack([jnp.broadcast_to(half, (8, LANES)) for half in halves]))
    return jnp.stack(tiles)


def lanes():
    return lax.broadcasted_iota(jnp.int32, (8, LANES), 1)


def z_down(values, edge):
    turned = pltpu.roll(values, 1, 3)
    first = lanes() == 0
    return jnp.stack([jnp.where(first, edge, turned[:, 0]), jnp.where(first, turned[:, 0], turned[:, 1])], axis=1)


def z_up(values, edge):
    turned = pltpu.roll(values, LANES - 1, 3)
    last = lanes() == LANES - 1
    return jnp.stack([jnp.where(last, turned[:, 1], turned[:, 0]), jnp.where(last, edge, turned[:, 1])], axis=1)


def columns(ref, wide_y, x, low, high):
    return ref[x * wide_y + low : x * wide_y + high]


def sweep(source_ref, gamma_ref, from_ref, x, low, high):
    wide_y = gamma_ref.shape[1]
    centre = columns(from_ref, wide_y, x, low, high)
    total = columns(from_ref, wide_y, x - 1, low, high) + columns(from_ref, wide_y, x + 1, low, high)
    total = total + columns(from_ref, wide_y, x, low - 1, high - 1) + columns(from_ref, wide_y, x, low + 1, high + 1)
    total = total + z_down(centre, 0.0) + z_up(centre, 0.0)
    return columns(source_ref, wide_y, x, low, high) + spread(gamma_ref, x, low, high) * total


def reached(wide_x, wide_y, reach):
    cells = []
    for x in range(DEEP - reach, wide_x - DEEP + reach):
        left = reach - max(DEEP - x, x - (wide_x - DEEP - 1), 0)
        cells.append((x, DEEP - left, wide_y - DEEP + left))
    return cells


def grouped(cells):
    for x, first, end in cells:
        for low in range(first, end, COLUMNS_AT_ONCE):
            yield x, low, min(low + COLUMNS_AT_ONCE, end)


def solve(bet_ref, gamma_ref, inv_ref, one_ref, two_ref):
    wide_x, wide_y, _ = gamma_ref.shape
    for x, low, high in grouped(reached(wide_x, wide_y, DEEP - 2)):
        one_ref[x * wide_y + low : x * wide_y + high] = sweep(bet_ref, gamma_ref, bet_ref, x, low, high)
    for x, low, high in grouped(reached(wide_x, wide_y, DEEP - 3)):
        scaled = sweep(bet_ref, gamma_ref, one_ref, x, low, high)
        two_ref[x * wide_y + low : x * wide_y + high] = scaled * spread(inv_ref, x, low, high)


def z_of_tile():
    return jnp.stack([lanes(), lanes() + LANES])


def unpack(packed):
    return packed & 255, (packed >> 8) & 255


def heads_kernel(plan, tests, per_brick, even_ref, odd_ref, e_in, sto_in, rec_in, table_ref, obs_ref,
                 e_ref, delta_ref, gamma_ref, inv_ref, head_ref, row_ref, sto_w, rec_w, beta_ref, bet_ref, one_ref):
    wide_x, wide_y, _ = e_ref.shape
    by = lax.axis_index("by")
    y_even = by % 2 == 0
    no_low, no_high = by == 0, by == lax.axis_size("by") - 1
    place = 0
    for field, x, count in plan:
        wide = (e_ref, sto_w, rec_w)[field]
        fill = (1.0, 1.0, 0.0)[field]
        got_e, got_o = even_ref[pl.ds(place, count), :], odd_ref[pl.ds(place, count), :]
        low, high = jnp.where(y_even, got_o, got_e), jnp.where(y_even, got_e, got_o)
        wide[x, DEEP - count : DEEP, :] = jnp.where(no_low, fill, low)
        wide[x, wide_y - DEEP : wide_y - DEEP + count, :] = jnp.where(no_high, fill, high)
        place += count
    field_rows(e_ref, sto_w, rec_w, delta_ref, gamma_ref, beta_ref)
    for x in range(3, wide_x - 3):
        inv_ref[x] = 1.0 / e_ref[x]
    for x, low, high in reached(wide_x, wide_y, DEEP - 1):
        bet_ref[x * wide_y + low : x * wide_y + high] = spread(beta_ref, x, low, high)
    sub = lax.broadcasted_iota(jnp.int32, (8, LANES), 0)
    z_of = z_of_tile()
    listed = list_length(per_brick)
    pumped = []
    for test in range(2 * tests):
        packed = table_ref[listed + LANES + test, 0]
        place, top = unpack(packed)
        near = (packed >> 30) & 1 == 1
        rate = obs_ref[3 + test // tests : 4 + test // tests, test % tests : test % tests + 1]
        delta = delta_ref[place // wide_y, pl.ds(place % wide_y, 1), :]
        delta = jnp.stack([jnp.broadcast_to(delta[:, part * LANES : (part + 1) * LANES], (8, LANES)) for part in range(2)])
        hit = (z_of >= top) & (z_of < top + SCREEN) & (sub == test) & near
        pumped.append((place, jnp.where(hit, delta * rate, 0.0)))
    for place, taken in pumped:
        bet_ref[place] = bet_ref[place] - taken
    solve(bet_ref, gamma_ref, inv_ref, one_ref, head_ref)
    slot_of = lanes() - per_brick * (sub % tests)
    gathered = jnp.zeros((8, LANES), jnp.float32)
    for rank in range(per_brick):
        place, top = unpack(table_ref[listed + rank, 0])
        hit = (z_of >= top) & (z_of < top + SCREEN)
        values = jnp.where(hit, head_ref[place], 0.0)
        gathered = jnp.where(slot_of == rank, jnp.sum(values[0] + values[1], axis=1, keepdims=True), gathered)
    mine = obs_ref[2:3, :] > 0.5
    parts = []
    for part in range(2):
        total = jnp.sum(jnp.where(sub // tests == part, gathered, 0.0), axis=0, keepdims=True)
        parts.append(jnp.where(mine, total * (1.0 / SCREEN) - obs_ref[part : part + 1, :], 0.0))
    row_ref[...] = jnp.broadcast_to(jnp.concatenate(parts, axis=0)[None], row_ref.shape)


def adjoint_kernel(tests, per_brick, n_wells, joined, scale, resid_ref, table_ref, clear_ref, clear_more_ref, e_ref, delta_ref, gamma_ref, inv_ref, head_ref,
                   bet_ref, more_ref, adj_ref, send_ref, norm_ref, weight_ref, one_ref):
    wide_x, wide_y, _ = e_ref.shape
    bricks = n_wells // per_brick
    sub = lax.broadcasted_iota(jnp.int32, (8, LANES), 0)
    z_of = z_of_tile()
    resid = resid_ref[:bricks] + resid_ref[bricks:] if joined else resid_ref[...]
    for brick in range(bricks):
        weight_ref[brick] = jnp.where(sub < tests, resid[brick, 0:1], resid[brick, 1:2])
    listed = list_length(per_brick)
    pick = per_brick * (sub % tests)

    def some_wells(turn, carry):
        todo = []
        for step in range(WELLS_AT_ONCE):
            packed = table_ref[turn * WELLS_AT_ONCE + step, 0]
            column, top = unpack(packed)
            brick, rank = (packed >> 16) & 255, (packed >> 24) & 31
            value = jnp.take_along_axis(weight_ref[brick], pick + rank, axis=1, mode="promise_in_bounds")
            todo.append((column, jnp.where((z_of >= top) & (z_of < top + SCREEN), value[None], 0.0)))
        for step, (column, value) in enumerate(todo):
            into_ref = (bet_ref, more_ref)[step % 2]
            into_ref[column] = into_ref[column] + value
        return carry

    turns = (table_ref[listed + LANES + 16, 0] + WELLS_AT_ONCE - 1) // WELLS_AT_ONCE
    lax.fori_loop(0, turns, some_wells, 0)
    for x, low, high in reached(wide_x, wide_y, DEEP - 1):
        row = pl.ds(x * wide_y + low, high - low)
        bet_ref[row] = (bet_ref[row] + more_ref[row]) * spread(delta_ref, x, low, high)
    solve(bet_ref, gamma_ref, inv_ref, one_ref, adj_ref)
    squares = jnp.sum(resid * resid, axis=0)
    squares = jnp.where(sub < tests, squares[0:1], squares[1:2])
    misfit = jnp.sum(jnp.where(lanes() // per_brick == sub % tests, squares, 0.0), axis=1, keepdims=True) / n_wells + EPSILON
    norm_ref[...] = jnp.broadcast_to(scale / misfit, (8, LANES))
    gradient_half(jnp.where(second_half(), 0, 1), norm_ref, e_ref, head_ref, adj_ref, send_ref)


def keep_kernel(norm_ref, e_ref, head_ref, adj_ref, keep_ref):
    gradient_half(jnp.where(second_half(), 1, 0), norm_ref, e_ref, head_ref, adj_ref, keep_ref)


def gradient_half(part, norm_ref, e_ref, head_ref, adj_ref, out_ref):
    wide_x, wide_y, _ = e_ref.shape
    low, high = DEEP, wide_y - DEEP
    is_first = part == 0
    at_first, at_last = lanes() == 0, lanes() == LANES - 1

    def spread_part(x, first, last):
        rows = [e_ref[x, pl.ds(y, 1), pl.ds(pl.multiple_of(part * LANES, LANES), LANES)] for y in range(first, last)]
        return jnp.stack([jnp.broadcast_to(row, (8, LANES)) for row in rows])

    def tiles(ref, x, first, last, which):
        return ref[x * wide_y + first : x * wide_y + last, which]

    def crossing(values, others, edge, turn, end):
        turned, other = pltpu.roll(values, turn, 2), pltpu.roll(others, turn, 2)
        return jnp.where(end, jnp.where(is_first == (turn != 1), other, edge), turned)

    before = None
    for x in range(DEEP - 1, wide_x - DEEP):
        e, head, adjoint = spread_part(x, low, high), tiles(head_ref, x, low, high, part), tiles(adj_ref, x, low, high, part)
        gap = (head - tiles(head_ref, x + 1, low, high, part)) * (adjoint - tiles(adj_ref, x + 1, low, high, part))
        after = e * spread_part(x + 1, low, high) * gap
        if x >= DEEP:
            total = before + after
            e_y = spread_part(x, low - 1, high + 1)
            head_y, adjoint_y = tiles(head_ref, x, low - 1, high + 1, part), tiles(adj_ref, x, low - 1, high + 1, part)
            sides = e_y[:-1] * e_y[1:] * (head_y[:-1] - head_y[1:]) * (adjoint_y[:-1] - adjoint_y[1:])
            total = total + sides[:-1] + sides[1:]
            halves = [ref[x, low:high, other * LANES : (other + 1) * LANES] for ref in (e_ref,) for other in range(2)]
            e_other = jnp.stack([jnp.broadcast_to(jnp.where(is_first, halves[1], halves[0])[y : y + 1], (8, LANES)) for y in range(high - low)])
            head_other, adjoint_other = tiles(head_ref, x, low, high, 1 - part), tiles(adj_ref, x, low, high, 1 - part)
            for turn, end in ((LANES - 1, at_last), (1, at_first)):
                e_near = crossing(e, e_other, 1.0, turn, end)
                head_near, adjoint_near = crossing(head, head_other, 0.0, turn, end), crossing(adjoint, adjoint_other, 0.0, turn, end)
                total = total + e * e_near * (head - head_near) * (adjoint - adjoint_near)
            total = jnp.sum(total * norm_ref[...], axis=1, keepdims=True)
            for y in range(high - low):
                out_ref[x - DEEP, pl.ds(y, 1), :] = total[y]
        before = after


def vmem():
    return pl.BlockSpec(memory_space=pltpu.VMEM)


def smem():
    return pl.BlockSpec(memory_space=pltpu.SMEM)


def f32(*shape):
    return jax.ShapeDtypeStruct(shape, jnp.float32)


def i32(*shape):
    return jax.ShapeDtypeStruct(shape, jnp.int32)


PARAMS = pltpu.CompilerParams(vmem_limit_bytes=24 * 1024 * 1024)


def local(log_conductivity, storage, recharge, pump_rate, pump_well, observed, owner, screen_column, screen_top):
    size_x, size_y, size_z = log_conductivity.shape
    half_x = size_x // 2
    tests = pump_rate.shape[0]
    n_wells = owner.shape[0]
    groups, n_bx, n_by = lax.axis_size("test"), lax.axis_size("bx"), lax.axis_size("by")
    bricks = n_bx * n_by
    per_brick = n_wells // bricks
    plan = slab_plan(half_x)
    rows_x = 3 * DEEP - 2
    rows_y = sum(count for _, _, count in plan)
    wide_x, wide_y = half_x + 2 * DEEP, size_y + 2 * DEEP
    tiles = (wide_x * wide_y, 2, 8, LANES)

    def in_hbm(*arrays):
        return [pltpu.with_memory_space_constraint(a, pltpu.HBM) for a in arrays]

    hbm = pl.BlockSpec(memory_space=pltpu.HBM)
    slab = pl.pallas_call(
        edge_kernel,
        out_shape=f32(rows_x, size_y, size_z),
        in_specs=[hbm] * 3,
        out_specs=vmem(),
        scratch_shapes=[pltpu.SemaphoreType.DMA((3,))],
        compiler_params=PARAMS,
        name="edge",
    )(*in_hbm(log_conductivity, storage, recharge))
    got_x = lax.ppermute(slab, ("test", "bx"), circle(n_bx, groups))

    inputs = (
        observed,
        pump_rate.reshape(1, tests),
        pump_well.reshape(1, tests),
        owner.reshape(1, n_wells),
        screen_column.reshape(1, n_wells),
        screen_top.reshape(1, n_wells),
        log_conductivity,
        storage,
        recharge,
    )
    owner, column, top, log_k, sto, rec, facts = pl.pallas_call(
        load_kernel,
        out_shape=[jax.ShapeDtypeStruct(a.shape, a.dtype) for a in inputs[3:]] + [f32(8, n_wells)],
        in_specs=[hbm] * len(inputs) + [vmem()],
        out_specs=[vmem()] * (len(inputs) - 2),
        scratch_shapes=[pltpu.VMEM((1, tests), jnp.float32), pltpu.VMEM((1, tests), jnp.int32), pltpu.SemaphoreType.DMA((len(inputs),))],
        compiler_params=PARAMS,
        name="load",
    )(*in_hbm(*inputs), slab)
    pairs = [(test, pair_of(test, groups)) for test in range(groups)]
    other_facts = lax.ppermute(facts, "test", pairs)

    bx, by, second = lax.axis_index("bx"), lax.axis_index("by"), lax.axis_index("test") % 2
    well_x = (owner // n_by - bx) * size_x + column // size_y + DEEP - second * half_x
    well_y = (owner % n_by - by) * size_y + column % size_y + DEEP
    out_x = jnp.maximum(jnp.maximum(DEEP - well_x, well_x - (DEEP + half_x - 1)), 0)
    out_y = jnp.maximum(jnp.maximum(DEEP - well_y, well_y - (DEEP + size_y - 1)), 0)
    in_window = (out_x + out_y < DEEP).astype(jnp.float32)
    owned = (out_x + out_y == 0).astype(jnp.float32)
    place = jnp.where(in_window > 0.5, well_x * wide_y + well_y, 0)
    window = f32(wide_x, wide_y, size_z)
    e, sto_w, rec_w = pl.pallas_call(
        window_kernel,
        out_shape=[window] * 3,
        in_specs=[vmem()] * 3,
        out_specs=[vmem()] * 3,
        compiler_params=PARAMS,
        name="window",
    )(log_k, sto, rec)
    e, sto_w, rec_w, even_y, odd_y = pl.pallas_call(
        functools.partial(pack_y, plan),
        out_shape=[window] * 3 + [f32(rows_y, size_z)] * 2,
        in_specs=[vmem()] * 4,
        out_specs=[vmem()] * 5,
        input_output_aliases={1: 0, 2: 1, 3: 2},
        compiler_params=PARAMS,
        name="pack_y",
    )(got_x, e, sto_w, rec_w)
    even, odd = side_partners(n_by, groups)
    got_even = lax.ppermute(even_y, ("test", "by"), even)
    got_odd = lax.ppermute(odd_y, ("test", "by"), odd)

    table, obs, clear, clear_more = pl.pallas_call(
        functools.partial(wells_kernel, tests, per_brick, bricks),
        out_shape=[i32(list_length(per_brick) + LANES + 24, 1), f32(8, LANES), f32(*tiles), f32(*tiles)],
        in_specs=[vmem()] * 8,
        out_specs=[vmem()] * 4,
        compiler_params=PARAMS,
        name="wells",
    )(owner, place, top, in_window, owned, facts, other_facts, even_y)

    joined = groups == 2
    copies = groups * bricks if joined else bricks
    e, delta, gamma, inverse, head, row, _, _ = pl.pallas_call(
        functools.partial(heads_kernel, plan, tests, per_brick),
        out_shape=[window] * 4 + [f32(*tiles), f32(copies, 2, LANES)] + [window] * 2,
        in_specs=[vmem()] * 7,
        out_specs=[vmem()] * 8,
        scratch_shapes=[pltpu.VMEM((wide_x, wide_y, size_z), jnp.float32)] + [pltpu.VMEM(tiles, jnp.float32)] * 2,
        input_output_aliases={2: 0, 3: 6, 4: 7},
        compiler_params=PARAMS,
        name="heads",
    )(got_even, got_odd, e, sto_w, rec_w, table, obs)

    if joined:
        residuals = lax.all_to_all(row, ("test", "bx", "by"), 0, 0)
    else:
        residuals = lax.all_to_all(row + lax.ppermute(row, "test", pairs), ("bx", "by"), 0, 0)

    scale = -0.5 / (tests * groups)
    _, _, adjoint, send, norm = pl.pallas_call(
        functools.partial(adjoint_kernel, tests, per_brick, n_wells, joined, scale),
        out_shape=[f32(*tiles)] * 3 + [f32(half_x, size_y, LANES), f32(8, LANES)],
        in_specs=[vmem()] * 9,
        out_specs=[vmem()] * 5,
        scratch_shapes=[pltpu.VMEM((bricks, 8, LANES), jnp.float32), pltpu.VMEM(tiles, jnp.float32)],
        input_output_aliases={2: 0, 3: 1},
        compiler_params=PARAMS,
        name="adjoint",
    )(residuals, table, clear, clear_more, e, delta, gamma, inverse, head)
    other = lax.ppermute(send, "test", pairs) if joined else send
    keep = pl.pallas_call(
        keep_kernel,
        out_shape=f32(half_x, size_y, LANES),
        in_specs=[vmem()] * 4,
        out_specs=vmem(),
        compiler_params=PARAMS,
        name="keep",
    )(norm, e, head, adjoint)
    if joined:
        return jnp.where(second == 0, jnp.concatenate([keep, other], axis=0), jnp.concatenate([other, keep], axis=0))
    low, high = jnp.where(second == 0, keep, send), jnp.where(second == 0, send, keep)
    half = jnp.concatenate([low, high], axis=2)
    none = jnp.zeros_like(half)
    whole = jnp.where(second == 0, jnp.concatenate([half, none], axis=0), jnp.concatenate([none, half], axis=0))
    return lax.psum_scatter(whole, "test", scatter_dimension=2, tiled=True)


def solution(mesh):
    placed = (
        P("bx", "by", None),
        P("bx", "by", None),
        P("bx", "by", None),
        P("test"),
        P("test"),
        P("test", None),
        P(),
        P(),
        P(),
    )
    return jax.shard_map(local, mesh=mesh, in_specs=placed, out_specs=P("bx", "by", "test"), check_vma=False)
```

```python
import functools

import jax
import jax.numpy as jnp
from jax import lax
from jax.experimental import pallas as pl
from jax.experimental.pallas import tpu as pltpu
from jax.sharding import PartitionSpec as P

SCREEN = 8
LANES = 128
DEEP = 4
EPSILON = 1e-06
WELL_CHUNK = 512
WELLS_AT_ONCE = 16
COLUMNS_AT_ONCE = 1


def list_length(per_brick):
    return -(-6 * per_brick // LANES) * LANES


def slab_plan(half_x):
    plan = []
    for field, reach in ((0, DEEP), (1, DEEP - 1), (2, DEEP - 1)):
        for x in range(half_x + 2 * DEEP):
            rows = reach - max(DEEP - x, x - (DEEP + half_x - 1), 0)
            if rows > 0:
                plan.append((field, x, rows))
    return plan


def pair_of(test, tests):
    return test ^ 1 if (test ^ 1) < tests else test


def side_partners(count, tests):
    even, odd = [], []
    for test in range(tests):
        for place in range(count):
            me = test * count + place
            other = pair_of(test, tests) * count + place
            up = place ^ 1
            even.append((me, test * count + up if up < count else other))
            down = ((place + 1) ^ 1) - 1
            odd.append((me, test * count + down if 0 <= down < count else other))
    return even, odd


def circle(count, tests):
    pairs = []
    for test in range(tests):
        for place in range(count):
            to = place + 1 if test % 2 == 0 else place - 1
            me = test * count + place
            pairs.append((me, test * count + to if 0 <= to < count else pair_of(test, tests) * count + place))
    return pairs


def second_half():
    return lax.axis_index("test") % 2 == 1


def edge_kernel(log_ref, sto_ref, rec_ref, slab_ref, sems):
    size_x = log_ref.shape[0]
    copies, place = [], 0
    for field, (ref, reach) in enumerate(((log_ref, DEEP), (sto_ref, DEEP - 1), (rec_ref, DEEP - 1))):
        first = jnp.where(second_half(), 0, size_x - reach)
        copies.append(pltpu.make_async_copy(ref.at[pl.ds(first, reach)], slab_ref.at[pl.ds(place, reach)], sems.at[field]))
        place += reach
    for copy in copies:
        copy.start()
    for copy in copies:
        copy.wait()


def load_kernel(observed, rate, pumped, *refs):
    sources, loaded, facts_ref, (rate_ref, pumped_ref, sems) = refs[:6], refs[7:13], refs[13], refs[14:]
    tests = observed.shape[0]
    moves = [(observed, facts_ref.at[pl.ds(0, tests)]), (rate, rate_ref), (pumped, pumped_ref)] + list(zip(sources, loaded))
    copies = [pltpu.make_async_copy(a, b, sems.at[i]) for i, (a, b) in enumerate(moves)]
    for copy in copies:
        copy.start()
    for copy in copies:
        copy.wait()
    facts_ref[tests : tests + 1, 0:tests] = rate_ref[...]
    facts_ref[tests + 1 : tests + 2, 0:tests] = pumped_ref[...].astype(jnp.float32)


def wells_kernel(tests, per_brick, bricks, owner_ref, place_ref, top_ref, window_ref, owned_ref, facts_ref, other_ref, _, table_ref, obs_ref, clear_ref, clear_more_ref):
    n_wells = owner_ref.shape[1]
    chunk = WELL_CHUNK if n_wells % WELL_CHUNK == 0 else n_wells
    listed = list_length(per_brick)
    before = lax.broadcasted_iota(jnp.int32, (chunk, chunk), 0) < lax.broadcasted_iota(jnp.int32, (chunk, chunk), 1)
    before = jnp.where(before, 1.0, 0.0).astype(jnp.bfloat16)
    brick_at = lax.broadcasted_iota(jnp.int32, (bricks, chunk), 0)
    list_at = lax.broadcasted_iota(jnp.int32, (listed, chunk), 0).astype(jnp.float32)
    own_at = (lax.broadcasted_iota(jnp.int32, (LANES, chunk), 0) % per_brick).astype(jnp.float32)
    lane_at = lax.broadcasted_iota(jnp.int32, (1, chunk), 1).astype(jnp.float32)
    first_row = lax.broadcasted_iota(jnp.int32, (16, chunk), 0) == 0
    swapped = second_half()
    mine, theirs = facts_ref[...], other_ref[...]
    facts = (jnp.where(swapped, theirs, mine), jnp.where(swapped, mine, theirs))
    total = jnp.zeros((bricks + 16, 1), jnp.float32)
    found = jnp.zeros((listed + LANES + 16, 32), jnp.float32)
    result = jnp.zeros((32, LANES), jnp.float32)
    for start in range(0, n_wells, chunk):
        part = slice(start, start + chunk)
        owner = owner_ref[:, part]
        near, own = window_ref[:, part], owned_ref[:, part]
        ones = jnp.where(brick_at == owner, 1.0, 0.0)
        counted = jnp.concatenate([ones, jnp.where(first_row, near, 0.0)], axis=0)
        prefix = jnp.dot(counted.astype(jnp.bfloat16), before, preferred_element_type=jnp.float32) + total
        total = total + jnp.sum(counted, axis=1, keepdims=True)
        rank = jnp.sum(ones * prefix[:bricks], axis=0, keepdims=True)
        in_list = jnp.where((list_at == prefix[bricks : bricks + 1]) & (near > 0.5), 1.0, 0.0)
        in_own = jnp.where((own_at == rank) & (own > 0.5), 1.0, 0.0)
        pumps = []
        for test in range(2 * tests):
            pumped = facts[test // tests][tests + 1 : tests + 2, test % tests : test % tests + 1]
            pumps.append(jnp.where(lane_at + float(start) == pumped, 1.0, 0.0))
        pumps.append(jnp.zeros((16 - 2 * tests, chunk), jnp.float32))
        chosen = jnp.concatenate([in_list, in_own] + pumps, axis=0).astype(jnp.bfloat16)
        rows = [number.astype(jnp.float32) for number in (place_ref[:, part], top_ref[:, part], owner)] + [rank, near]
        for test in range(2 * tests):
            value = facts[test // tests][test % tests : test % tests + 1, part]
            for _ in range(3):
                piece = value.astype(jnp.bfloat16).astype(jnp.float32)
                rows.append(piece)
                value = value - piece
        rows.append(jnp.zeros((32 - len(rows), chunk), jnp.float32))
        carried = jnp.concatenate(rows, axis=0).astype(jnp.bfloat16)
        over_wells = (((1,), (1,)), ((), ()))
        found = found + lax.dot_general(chosen, carried, over_wells, preferred_element_type=jnp.float32)
        result = result + lax.dot_general(carried, chosen[listed : listed + LANES], over_wells, preferred_element_type=jnp.float32)
    column = lax.broadcasted_iota(jnp.int32, found.shape, 1)
    low = jnp.where(column == 0, 1.0, jnp.where(column == 1, 256.0, 0.0))
    high = jnp.where(column == 2, 1.0, jnp.where(column == 3, 256.0, jnp.where(column == 4, 16384.0, 0.0)))
    low, high = (jnp.sum(found * weights, axis=1, keepdims=True).astype(jnp.int32) for weights in (low, high))
    table_ref[0 : listed + LANES + 16, :] = low + (high << 16)
    table_ref[listed + LANES + 16 :, :] = jnp.broadcast_to(total[bricks : bricks + 1], (8, 1)).astype(jnp.int32)
    lane = lax.broadcasted_iota(jnp.int32, (1, LANES), 1)
    for part in range(2):
        values = jnp.zeros((1, LANES), jnp.float32)
        for test in range(tests):
            first = 5 + 3 * (part * tests + test)
            pieces = [result[row : row + 1] for row in range(first, first + 3)]
            values = jnp.where(lane // per_brick == test, pieces[0] + (pieces[1] + pieces[2]), values)
        obs_ref[part : part + 1, :] = values
        obs_ref[3 + part : 4 + part, 0:tests] = facts[part][tests : tests + 1, 0:tests]
    obs_ref[2:3, :] = result[4:5]
    clear_ref[...] = jnp.zeros(clear_ref.shape, jnp.float32)
    clear_more_ref[...] = jnp.zeros(clear_ref.shape, jnp.float32)


def at_window_rows(value):
    return pltpu.roll(jnp.concatenate([value, value], axis=0), DEEP, 0)


def window_kernel(log_ref, sto_ref, rec_ref, e_ref, sto_w, rec_w, up_ref):
    base = jnp.where(second_half(), 0, DEEP)
    for x in range(log_ref.shape[0]):
        e = jnp.exp(0.5 * log_ref[x])
        e_ref[base + x] = at_window_rows(e)
        last = lax.broadcasted_iota(jnp.int32, e.shape, 1) == e.shape[1] - 1
        up_ref[base + x] = at_window_rows(e * jnp.where(last, 1.0, pltpu.roll(e, e.shape[1] - 1, 1)))
        sto_w[base + x] = at_window_rows(sto_ref[x])
        rec_w[base + x] = at_window_rows(rec_ref[x])


def pack_y(plan, slab_ref, e_in, sto_in, rec_in, e_ref, sto_w, rec_w, even_ref, odd_ref):
    size_y = slab_ref.shape[1]
    swapped = second_half()
    bx = lax.axis_index("bx")
    absent = jnp.where(swapped, bx == lax.axis_size("bx") - 1, bx == 0)
    y_even = lax.axis_index("by") % 2 == 0
    wides = (e_ref, sto_w, rec_w)
    half_x = e_ref.shape[0] - 2 * DEEP
    place = 0
    for field, reach in enumerate((DEEP, DEEP - 1, DEEP - 1)):
        base = jnp.where(swapped, DEEP + half_x, DEEP - reach)
        for i in range(reach):
            value = slab_ref[place + i]
            value = jnp.exp(0.5 * value) if field == 0 else value
            wides[field][base + i] = at_window_rows(jnp.where(absent, (1.0, 1.0, 0.0)[field], value))
        place += reach
    place = 0
    for field, x, count in plan:
        wide = wides[field]
        up = wide[x, DEEP + size_y - count : DEEP + size_y, :]
        down = wide[x, DEEP : DEEP + count, :]
        at = pl.ds(place, count)
        even_ref[at, :] = jnp.where(y_even, up, down)
        odd_ref[at, :] = jnp.where(y_even, down, up)
        place += count


def field_rows(e_ref, sto_w, rec_w, delta_ref, gamma_ref, beta_ref):
    wide_x, wide_y, size_z = e_ref.shape
    half_x, size_y = wide_x - 2 * DEEP, wide_y - 2 * DEEP
    bx, by, swapped = lax.axis_index("bx"), lax.axis_index("by"), second_half()
    row_at = lax.broadcasted_iota(jnp.int32, (wide_y, size_z), 0)
    z_at = lax.broadcasted_iota(jnp.int32, (wide_y, size_z), 1)
    inside_y = ((row_at >= DEEP) | (by > 0)) & ((row_at < DEEP + size_y) | (by < lax.axis_size("by") - 1))
    for x in range(1, wide_x - 1):
        e = e_ref[x]
        total = e_ref[x - 1] + e_ref[x + 1]
        total = total + pltpu.roll(e, 1, 0) + pltpu.roll(e, wide_y - 1, 0)
        total = total + jnp.where(z_at == 0, 1.0, pltpu.roll(e, 1, 1))
        total = total + jnp.where(z_at == size_z - 1, 1.0, pltpu.roll(e, size_z - 1, 1))
        inside = inside_y
        if x < DEEP:
            inside = inside & (swapped | (bx > 0))
        if x >= DEEP + half_x:
            inside = inside & (jnp.logical_not(swapped) | (bx < lax.axis_size("bx") - 1))
        delta = jnp.where(inside, e / (sto_w[x] + e * total), 0.0)
        delta_ref[x] = delta
        gamma_ref[x] = delta * e
        beta_ref[x] = delta * rec_w[x]


def spread(ref, x, low, high):
    tiles = []
    for y in range(low, high):
        halves = [ref[x, pl.ds(y, 1), part * LANES : (part + 1) * LANES] for part in range(2)]
        tiles.append(jnp.stack([jnp.broadcast_to(half, (8, LANES)) for half in halves]))
    return jnp.stack(tiles)


def lanes():
    return lax.broadcasted_iota(jnp.int32, (8, LANES), 1)


def z_down(values, edge):
    turned = pltpu.roll(values, 1, 3)
    first = lanes() == 0
    return jnp.stack([jnp.where(first, edge, turned[:, 0]), jnp.where(first, turned[:, 0], turned[:, 1])], axis=1)


def z_up(values, edge):
    turned = pltpu.roll(values, LANES - 1, 3)
    last = lanes() == LANES - 1
    return jnp.stack([jnp.where(last, turned[:, 1], turned[:, 0]), jnp.where(last, edge, turned[:, 1])], axis=1)


def columns(ref, wide_y, x, low, high):
    return ref[x * wide_y + low : x * wide_y + high]


def sweep(source_ref, gamma_ref, from_ref, x, low, high):
    wide_y = gamma_ref.shape[1]
    centre = columns(from_ref, wide_y, x, low, high)
    total = columns(from_ref, wide_y, x - 1, low, high) + columns(from_ref, wide_y, x + 1, low, high)
    total = total + columns(from_ref, wide_y, x, low - 1, high - 1) + columns(from_ref, wide_y, x, low + 1, high + 1)
    total = total + z_down(centre, 0.0) + z_up(centre, 0.0)
    return columns(source_ref, wide_y, x, low, high) + spread(gamma_ref, x, low, high) * total


def reached(wide_x, wide_y, reach):
    cells = []
    for x in range(DEEP - reach, wide_x - DEEP + reach):
        left = reach - max(DEEP - x, x - (wide_x - DEEP - 1), 0)
        cells.append((x, DEEP - left, wide_y - DEEP + left))
    return cells


def grouped(cells):
    for x, first, end in cells:
        for low in range(first, end, COLUMNS_AT_ONCE):
            yield x, low, min(low + COLUMNS_AT_ONCE, end)


def solve(bet_ref, gamma_ref, inv_ref, one_ref, two_ref):
    wide_x, wide_y, _ = gamma_ref.shape
    for x, low, high in grouped(reached(wide_x, wide_y, DEEP - 2)):
        one_ref[x * wide_y + low : x * wide_y + high] = sweep(bet_ref, gamma_ref, bet_ref, x, low, high)
    for x, low, high in grouped(reached(wide_x, wide_y, DEEP - 3)):
        scaled = sweep(bet_ref, gamma_ref, one_ref, x, low, high)
        two_ref[x * wide_y + low : x * wide_y + high] = scaled * spread(inv_ref, x, low, high)


def z_of_tile():
    return jnp.stack([lanes(), lanes() + LANES])


def unpack(packed):
    return packed & 255, (packed >> 8) & 255


def heads_kernel(plan, tests, per_brick, even_ref, odd_ref, e_in, sto_in, rec_in, table_ref, obs_ref,
                 e_ref, delta_ref, gamma_ref, inv_ref, head_ref, row_ref, sto_w, rec_w, beta_ref, bet_ref, one_ref):
    wide_x, wide_y, _ = e_ref.shape
    by = lax.axis_index("by")
    y_even = by % 2 == 0
    no_low, no_high = by == 0, by == lax.axis_size("by") - 1
    place = 0
    for field, x, count in plan:
        wide = (e_ref, sto_w, rec_w)[field]
        fill = (1.0, 1.0, 0.0)[field]
        got_e, got_o = even_ref[pl.ds(place, count), :], odd_ref[pl.ds(place, count), :]
        low, high = jnp.where(y_even, got_o, got_e), jnp.where(y_even, got_e, got_o)
        wide[x, DEEP - count : DEEP, :] = jnp.where(no_low, fill, low)
        wide[x, wide_y - DEEP : wide_y - DEEP + count, :] = jnp.where(no_high, fill, high)
        place += count
    field_rows(e_ref, sto_w, rec_w, delta_ref, gamma_ref, beta_ref)
    for x in range(3, wide_x - 3):
        inv_ref[x] = 1.0 / e_ref[x]
    for x, low, high in reached(wide_x, wide_y, DEEP - 1):
        bet_ref[x * wide_y + low : x * wide_y + high] = spread(beta_ref, x, low, high)
    sub = lax.broadcasted_iota(jnp.int32, (8, LANES), 0)
    z_of = z_of_tile()
    listed = list_length(per_brick)
    pumped = []
    for test in range(2 * tests):
        packed = table_ref[listed + LANES + test, 0]
        place, top = unpack(packed)
        near = (packed >> 30) & 1 == 1
        rate = obs_ref[3 + test // tests : 4 + test // tests, test % tests : test % tests + 1]
        delta = delta_ref[place // wide_y, pl.ds(place % wide_y, 1), :]
        delta = jnp.stack([jnp.broadcast_to(delta[:, part * LANES : (part + 1) * LANES], (8, LANES)) for part in range(2)])
        hit = (z_of >= top) & (z_of < top + SCREEN) & (sub == test) & near
        pumped.append((place, jnp.where(hit, delta * rate, 0.0)))
    for place, taken in pumped:
        bet_ref[place] = bet_ref[place] - taken
    solve(bet_ref, gamma_ref, inv_ref, one_ref, head_ref)
    slot_of = lanes() - per_brick * (sub % tests)
    gathered = jnp.zeros((8, LANES), jnp.float32)
    for rank in range(per_brick):
        place, top = unpack(table_ref[listed + rank, 0])
        hit = (z_of >= top) & (z_of < top + SCREEN)
        values = jnp.where(hit, head_ref[place], 0.0)
        gathered = jnp.where(slot_of == rank, jnp.sum(values[0] + values[1], axis=1, keepdims=True), gathered)
    mine = obs_ref[2:3, :] > 0.5
    parts = []
    for part in range(2):
        total = jnp.sum(jnp.where(sub // tests == part, gathered, 0.0), axis=0, keepdims=True)
        parts.append(jnp.where(mine, total * (1.0 / SCREEN) - obs_ref[part : part + 1, :], 0.0))
    row_ref[...] = jnp.broadcast_to(jnp.concatenate(parts, axis=0)[None], row_ref.shape)


def adjoint_kernel(tests, per_brick, n_wells, joined, scale, resid_ref, table_ref, clear_ref, clear_more_ref, e_ref, delta_ref, gamma_ref, inv_ref,
                   bet_ref, more_ref, adj_ref, norm_ref, weight_ref, one_ref):
    wide_x, wide_y, _ = e_ref.shape
    bricks = n_wells // per_brick
    sub = lax.broadcasted_iota(jnp.int32, (8, LANES), 0)
    z_of = z_of_tile()
    resid = resid_ref[:bricks] + resid_ref[bricks:] if joined else resid_ref[...]
    for brick in range(bricks):
        weight_ref[brick] = jnp.where(sub < tests, resid[brick, 0:1], resid[brick, 1:2])
    listed = list_length(per_brick)
    pick = per_brick * (sub % tests)

    def some_wells(turn, carry):
        todo = []
        for step in range(WELLS_AT_ONCE):
            packed = table_ref[turn * WELLS_AT_ONCE + step, 0]
            column, top = unpack(packed)
            brick, rank = (packed >> 16) & 255, (packed >> 24) & 31
            value = jnp.take_along_axis(weight_ref[brick], pick + rank, axis=1, mode="promise_in_bounds")
            todo.append((column, jnp.where((z_of >= top) & (z_of < top + SCREEN), value[None], 0.0)))
        for step, (column, value) in enumerate(todo):
            into_ref = (bet_ref, more_ref)[step % 2]
            into_ref[column] = into_ref[column] + value
        return carry

    turns = (table_ref[listed + LANES + 16, 0] + WELLS_AT_ONCE - 1) // WELLS_AT_ONCE
    lax.fori_loop(0, turns, some_wells, 0)
    for x, low, high in reached(wide_x, wide_y, DEEP - 1):
        row = pl.ds(x * wide_y + low, high - low)
        bet_ref[row] = (bet_ref[row] + more_ref[row]) * spread(delta_ref, x, low, high)
    solve(bet_ref, gamma_ref, inv_ref, one_ref, adj_ref)
    squares = jnp.sum(resid * resid, axis=0)
    squares = jnp.where(sub < tests, squares[0:1], squares[1:2])
    misfit = jnp.sum(jnp.where(lanes() // per_brick == sub % tests, squares, 0.0), axis=1, keepdims=True) / n_wells + EPSILON
    norm_ref[...] = jnp.broadcast_to(scale / misfit, (8, LANES))


def gradient_kernel(kept, norm_ref, e_ref, up_ref, head_ref, adj_ref, out_ref):
    wide_x, wide_y, _ = e_ref.shape
    low, high = DEEP, wide_y - DEEP
    part = jnp.where(second_half(), 1, 0) if kept else jnp.where(second_half(), 0, 1)
    is_first = part == 0
    at_first, at_last = lanes() == 0, lanes() == LANES - 1

    def spread_part(ref, x, first, last, which):
        rows = [ref[x, pl.ds(y, 1), pl.ds(pl.multiple_of(which * LANES, LANES), LANES)] for y in range(first, last)]
        return jnp.stack([jnp.broadcast_to(row, (8, LANES)) for row in rows])

    def tiles(ref, x, first, last, which):
        return ref[x * wide_y + first : x * wide_y + last, which]

    def next_cell(values, others):
        return pltpu.roll(jnp.where(at_first & is_first, others, values), LANES - 1, 2)

    before = None
    for x in range(DEEP - 1, wide_x - DEEP):
        e, head, adjoint = spread_part(e_ref, x, low, high, part), tiles(head_ref, x, low, high, part), tiles(adj_ref, x, low, high, part)
        gap = (head - tiles(head_ref, x + 1, low, high, part)) * (adjoint - tiles(adj_ref, x + 1, low, high, part))
        after = e * spread_part(e_ref, x + 1, low, high, part) * gap
        if x >= DEEP:
            total = before + after
            e_y = spread_part(e_ref, x, low - 1, high + 1, part)
            head_y, adjoint_y = tiles(head_ref, x, low - 1, high + 1, part), tiles(adj_ref, x, low - 1, high + 1, part)
            sides = e_y[:-1] * e_y[1:] * (head_y[:-1] - head_y[1:]) * (adjoint_y[:-1] - adjoint_y[1:])
            total = total + sides[:-1] + sides[1:]
            head_other, adjoint_other = tiles(head_ref, x, low, high, 1 - part), tiles(adj_ref, x, low, high, 1 - part)
            head_next, adjoint_next = next_cell(head, head_other), next_cell(adjoint, adjoint_other)
            at_top = at_last & jnp.logical_not(is_first)
            gap = (head - jnp.where(at_top, 0.0, head_next)) * (adjoint - jnp.where(at_top, 0.0, adjoint_next))
            upper = spread_part(up_ref, x, low, high, part) * gap
            middle = spread_part(up_ref, x, low, high, 1 - part) * (head_other - head_next) * (adjoint_other - adjoint_next)
            lower = pltpu.roll(jnp.where(at_top, middle, upper), 1, 2)
            total = total + upper + jnp.where(at_first & is_first, e * head * adjoint, lower)
            total = jnp.sum(total * norm_ref[...], axis=1, keepdims=True)
            for y in range(high - low):
                out_ref[x - DEEP, pl.ds(y, 1), :] = total[y]
        before = after


def join_kernel(keep_ref, other_ref, out_ref):
    half_x = keep_ref.shape[0]
    mine = jnp.where(second_half(), half_x, 0)
    out_ref[pl.ds(mine, half_x)] = keep_ref[...]
    out_ref[pl.ds(half_x - mine, half_x)] = other_ref[...]


def vmem():
    return pl.BlockSpec(memory_space=pltpu.VMEM)


def smem():
    return pl.BlockSpec(memory_space=pltpu.SMEM)


def f32(*shape):
    return jax.ShapeDtypeStruct(shape, jnp.float32)


def i32(*shape):
    return jax.ShapeDtypeStruct(shape, jnp.int32)


PARAMS = pltpu.CompilerParams(vmem_limit_bytes=24 * 1024 * 1024)


def local(log_conductivity, storage, recharge, pump_rate, pump_well, observed, owner, screen_column, screen_top):
    size_x, size_y, size_z = log_conductivity.shape
    half_x = size_x // 2
    tests = pump_rate.shape[0]
    n_wells = owner.shape[0]
    groups, n_bx, n_by = lax.axis_size("test"), lax.axis_size("bx"), lax.axis_size("by")
    bricks = n_bx * n_by
    per_brick = n_wells // bricks
    plan = slab_plan(half_x)
    rows_x = 3 * DEEP - 2
    rows_y = sum(count for _, _, count in plan)
    wide_x, wide_y = half_x + 2 * DEEP, size_y + 2 * DEEP
    tiles = (wide_x * wide_y, 2, 8, LANES)

    def in_hbm(*arrays):
        return [pltpu.with_memory_space_constraint(a, pltpu.HBM) for a in arrays]

    hbm = pl.BlockSpec(memory_space=pltpu.HBM)
    slab = pl.pallas_call(
        edge_kernel,
        out_shape=f32(rows_x, size_y, size_z),
        in_specs=[hbm] * 3,
        out_specs=vmem(),
        scratch_shapes=[pltpu.SemaphoreType.DMA((3,))],
        compiler_params=PARAMS,
        name="edge",
    )(*in_hbm(log_conductivity, storage, recharge))
    got_x = lax.ppermute(slab, ("test", "bx"), circle(n_bx, groups))

    inputs = (
        observed,
        pump_rate.reshape(1, tests),
        pump_well.reshape(1, tests),
        owner.reshape(1, n_wells),
        screen_column.reshape(1, n_wells),
        screen_top.reshape(1, n_wells),
        log_conductivity,
        storage,
        recharge,
    )
    owner, column, top, log_k, sto, rec, facts = pl.pallas_call(
        load_kernel,
        out_shape=[jax.ShapeDtypeStruct(a.shape, a.dtype) for a in inputs[3:]] + [f32(8, n_wells)],
        in_specs=[hbm] * len(inputs) + [vmem()],
        out_specs=[vmem()] * (len(inputs) - 2),
        scratch_shapes=[pltpu.VMEM((1, tests), jnp.float32), pltpu.VMEM((1, tests), jnp.int32), pltpu.SemaphoreType.DMA((len(inputs),))],
        compiler_params=PARAMS,
        name="load",
    )(*in_hbm(*inputs), slab)
    pairs = [(test, pair_of(test, groups)) for test in range(groups)]
    other_facts = lax.ppermute(facts, "test", pairs)

    bx, by, second = lax.axis_index("bx"), lax.axis_index("by"), lax.axis_index("test") % 2
    well_x = (owner // n_by - bx) * size_x + column // size_y + DEEP - second * half_x
    well_y = (owner % n_by - by) * size_y + column % size_y + DEEP
    out_x = jnp.maximum(jnp.maximum(DEEP - well_x, well_x - (DEEP + half_x - 1)), 0)
    out_y = jnp.maximum(jnp.maximum(DEEP - well_y, well_y - (DEEP + size_y - 1)), 0)
    in_window = (out_x + out_y < DEEP).astype(jnp.float32)
    owned = (out_x + out_y == 0).astype(jnp.float32)
    place = jnp.where(in_window > 0.5, well_x * wide_y + well_y, 0)
    window = f32(wide_x, wide_y, size_z)
    e, sto_w, rec_w, up = pl.pallas_call(
        window_kernel,
        out_shape=[window] * 4,
        in_specs=[vmem()] * 3,
        out_specs=[vmem()] * 4,
        compiler_params=PARAMS,
        name="window",
    )(log_k, sto, rec)
    e, sto_w, rec_w, even_y, odd_y = pl.pallas_call(
        functools.partial(pack_y, plan),
        out_shape=[window] * 3 + [f32(rows_y, size_z)] * 2,
        in_specs=[vmem()] * 4,
        out_specs=[vmem()] * 5,
        input_output_aliases={1: 0, 2: 1, 3: 2},
        compiler_params=PARAMS,
        name="pack_y",
    )(got_x, e, sto_w, rec_w)
    even, odd = side_partners(n_by, groups)
    got_even = lax.ppermute(even_y, ("test", "by"), even)
    got_odd = lax.ppermute(odd_y, ("test", "by"), odd)

    table, obs, clear, clear_more = pl.pallas_call(
        functools.partial(wells_kernel, tests, per_brick, bricks),
        out_shape=[i32(list_length(per_brick) + LANES + 24, 1), f32(8, LANES), f32(*tiles), f32(*tiles)],
        in_specs=[vmem()] * 8,
        out_specs=[vmem()] * 4,
        compiler_params=PARAMS,
        name="wells",
    )(owner, place, top, in_window, owned, facts, other_facts, even_y)

    joined = groups == 2
    copies = groups * bricks if joined else bricks
    e, delta, gamma, inverse, head, row, _, _ = pl.pallas_call(
        functools.partial(heads_kernel, plan, tests, per_brick),
        out_shape=[window] * 4 + [f32(*tiles), f32(copies, 2, LANES)] + [window] * 2,
        in_specs=[vmem()] * 7,
        out_specs=[vmem()] * 8,
        scratch_shapes=[pltpu.VMEM((wide_x, wide_y, size_z), jnp.float32)] + [pltpu.VMEM(tiles, jnp.float32)] * 2,
        input_output_aliases={2: 0, 3: 6, 4: 7},
        compiler_params=PARAMS,
        name="heads",
    )(got_even, got_odd, e, sto_w, rec_w, table, obs)

    if joined:
        residuals = lax.all_to_all(row, ("test", "bx", "by"), 0, 0)
    else:
        residuals = lax.all_to_all(row + lax.ppermute(row, "test", pairs), ("bx", "by"), 0, 0)

    scale = -0.5 / (tests * groups)
    _, _, adjoint, norm = pl.pallas_call(
        functools.partial(adjoint_kernel, tests, per_brick, n_wells, joined, scale),
        out_shape=[f32(*tiles)] * 3 + [f32(8, LANES)],
        in_specs=[vmem()] * 8,
        out_specs=[vmem()] * 4,
        scratch_shapes=[pltpu.VMEM((bricks, 8, LANES), jnp.float32), pltpu.VMEM(tiles, jnp.float32)],
        input_output_aliases={2: 0, 3: 1},
        compiler_params=PARAMS,
        name="adjoint",
    )(residuals, table, clear, clear_more, e, delta, gamma, inverse)

    def gradient_of(kept):
        return pl.pallas_call(
            functools.partial(gradient_kernel, kept),
            out_shape=f32(half_x, size_y, LANES),
            in_specs=[vmem()] * 5,
            out_specs=vmem(),
            compiler_params=PARAMS,
            name="keep" if kept else "send",
        )(norm, e, up, head, adjoint)

    send = gradient_of(False)
    other = lax.ppermute(send, "test", pairs) if joined else send
    keep = gradient_of(True)
    if joined:
        return pl.pallas_call(
            join_kernel,
            out_shape=f32(size_x, size_y, LANES),
            in_specs=[vmem()] * 2,
            out_specs=vmem(),
            compiler_params=PARAMS,
            name="join",
        )(pltpu.with_memory_space_constraint(keep, pltpu.VMEM), pltpu.with_memory_space_constraint(other, pltpu.VMEM))
    low, high = jnp.where(second == 0, keep, send), jnp.where(second == 0, send, keep)
    half = jnp.concatenate([low, high], axis=2)
    none = jnp.zeros_like(half)
    whole = jnp.where(second == 0, jnp.concatenate([half, none], axis=0), jnp.concatenate([none, half], axis=0))
    return lax.psum_scatter(whole, "test", scatter_dimension=2, tiled=True)


def solution(mesh):
    placed = (
        P("bx", "by", None),
        P("bx", "by", None),
        P("bx", "by", None),
        P("test"),
        P("test"),
        P("test", None),
        P(),
        P(),
        P(),
    )
    return jax.shard_map(local, mesh=mesh, in_specs=placed, out_specs=P("bx", "by", "test"), check_vma=False)
```

```python
import functools

import jax
import jax.numpy as jnp
from jax import lax
from jax.experimental import pallas as pl
from jax.experimental.pallas import tpu as pltpu
from jax.sharding import PartitionSpec as P

SCREEN = 8
LANES = 128
DEEP = 4
EPSILON = 1e-06
WELL_CHUNK = 512
WELLS_AT_ONCE = 32
COLUMNS_AT_ONCE = 1


def list_length(per_brick):
    return -(-6 * per_brick // LANES) * LANES


def slab_plan(half_x):
    plan = []
    for field, reach in ((0, DEEP), (1, DEEP - 1), (2, DEEP - 1)):
        for x in range(half_x + 2 * DEEP):
            rows = reach - max(DEEP - x, x - (DEEP + half_x - 1), 0)
            if rows > 0:
                plan.append((field, x, rows))
    return plan


def pair_of(test, tests):
    return test ^ 1 if (test ^ 1) < tests else test


def side_partners(count, tests):
    even, odd = [], []
    for test in range(tests):
        for place in range(count):
            me = test * count + place
            other = pair_of(test, tests) * count + place
            up = place ^ 1
            even.append((me, test * count + up if up < count else other))
            down = ((place + 1) ^ 1) - 1
            odd.append((me, test * count + down if 0 <= down < count else other))
    return even, odd


def circle(count, tests):
    pairs = []
    for test in range(tests):
        for place in range(count):
            to = place + 1 if test % 2 == 0 else place - 1
            me = test * count + place
            pairs.append((me, test * count + to if 0 <= to < count else pair_of(test, tests) * count + place))
    return pairs


def second_half():
    return lax.axis_index("test") % 2 == 1


def edge_kernel(log_ref, sto_ref, rec_ref, slab_ref, sems):
    size_x = log_ref.shape[0]
    copies, place = [], 0
    for field, (ref, reach) in enumerate(((log_ref, DEEP), (sto_ref, DEEP - 1), (rec_ref, DEEP - 1))):
        first = jnp.where(second_half(), 0, size_x - reach)
        copies.append(pltpu.make_async_copy(ref.at[pl.ds(first, reach)], slab_ref.at[pl.ds(place, reach)], sems.at[field]))
        place += reach
    for copy in copies:
        copy.start()
    for copy in copies:
        copy.wait()


def load_kernel(observed, rate, pumped, *refs):
    sources, loaded, facts_ref, (rate_ref, pumped_ref, sems) = refs[:6], refs[7:13], refs[13], refs[14:]
    tests = observed.shape[0]
    moves = [(observed, facts_ref.at[pl.ds(0, tests)]), (rate, rate_ref), (pumped, pumped_ref)] + list(zip(sources, loaded))
    copies = [pltpu.make_async_copy(a, b, sems.at[i]) for i, (a, b) in enumerate(moves)]
    for copy in copies:
        copy.start()
    for copy in copies:
        copy.wait()
    facts_ref[tests : tests + 1, 0:tests] = rate_ref[...]
    facts_ref[tests + 1 : tests + 2, 0:tests] = pumped_ref[...].astype(jnp.float32)


def wells_kernel(tests, per_brick, bricks, owner_ref, place_ref, top_ref, window_ref, owned_ref, facts_ref, other_ref, _, table_ref, obs_ref, clear_ref, clear_more_ref):
    n_wells = owner_ref.shape[1]
    chunk = WELL_CHUNK if n_wells % WELL_CHUNK == 0 else n_wells
    listed = list_length(per_brick)
    before = lax.broadcasted_iota(jnp.int32, (chunk, chunk), 0) < lax.broadcasted_iota(jnp.int32, (chunk, chunk), 1)
    before = jnp.where(before, 1.0, 0.0).astype(jnp.bfloat16)
    brick_at = lax.broadcasted_iota(jnp.int32, (bricks, chunk), 0)
    list_at = lax.broadcasted_iota(jnp.int32, (listed, chunk), 0).astype(jnp.float32)
    own_at = (lax.broadcasted_iota(jnp.int32, (LANES, chunk), 0) % per_brick).astype(jnp.float32)
    lane_at = lax.broadcasted_iota(jnp.int32, (1, chunk), 1).astype(jnp.float32)
    first_row = lax.broadcasted_iota(jnp.int32, (16, chunk), 0) == 0
    swapped = second_half()
    mine, theirs = facts_ref[...], other_ref[...]
    facts = (jnp.where(swapped, theirs, mine), jnp.where(swapped, mine, theirs))
    total = jnp.zeros((bricks + 16, 1), jnp.float32)
    found = jnp.zeros((listed + LANES + 16, 32), jnp.float32)
    result = jnp.zeros((32, LANES), jnp.float32)
    for start in range(0, n_wells, chunk):
        part = slice(start, start + chunk)
        owner = owner_ref[:, part]
        near, own = window_ref[:, part], owned_ref[:, part]
        ones = jnp.where(brick_at == owner, 1.0, 0.0)
        counted = jnp.concatenate([ones, jnp.where(first_row, near, 0.0)], axis=0)
        prefix = jnp.dot(counted.astype(jnp.bfloat16), before, preferred_element_type=jnp.float32) + total
        total = total + jnp.sum(counted, axis=1, keepdims=True)
        rank = jnp.sum(ones * prefix[:bricks], axis=0, keepdims=True)
        in_list = jnp.where((list_at == prefix[bricks : bricks + 1]) & (near > 0.5), 1.0, 0.0)
        in_own = jnp.where((own_at == rank) & (own > 0.5), 1.0, 0.0)
        pumps = []
        for test in range(2 * tests):
            pumped = facts[test // tests][tests + 1 : tests + 2, test % tests : test % tests + 1]
            pumps.append(jnp.where(lane_at + float(start) == pumped, 1.0, 0.0))
        pumps.append(jnp.zeros((16 - 2 * tests, chunk), jnp.float32))
        chosen = jnp.concatenate([in_list, in_own] + pumps, axis=0).astype(jnp.bfloat16)
        rows = [number.astype(jnp.float32) for number in (place_ref[:, part], top_ref[:, part], owner)] + [rank, near]
        for test in range(2 * tests):
            value = facts[test // tests][test % tests : test % tests + 1, part]
            for _ in range(3):
                piece = value.astype(jnp.bfloat16).astype(jnp.float32)
                rows.append(piece)
                value = value - piece
        rows.append(jnp.zeros((32 - len(rows), chunk), jnp.float32))
        carried = jnp.concatenate(rows, axis=0).astype(jnp.bfloat16)
        over_wells = (((1,), (1,)), ((), ()))
        found = found + lax.dot_general(chosen, carried, over_wells, preferred_element_type=jnp.float32)
        result = result + lax.dot_general(carried, chosen[listed : listed + LANES], over_wells, preferred_element_type=jnp.float32)
    column = lax.broadcasted_iota(jnp.int32, found.shape, 1)
    low = jnp.where(column == 0, 1.0, jnp.where(column == 1, 256.0, 0.0))
    high = jnp.where(column == 2, 1.0, jnp.where(column == 3, 256.0, jnp.where(column == 4, 16384.0, 0.0)))
    low, high = (jnp.sum(found * weights, axis=1, keepdims=True).astype(jnp.int32) for weights in (low, high))
    table_ref[0 : listed + LANES + 16, :] = low + (high << 16)
    table_ref[listed + LANES + 16 :, :] = jnp.broadcast_to(total[bricks : bricks + 1], (8, 1)).astype(jnp.int32)
    lane = lax.broadcasted_iota(jnp.int32, (1, LANES), 1)
    for part in range(2):
        values = jnp.zeros((1, LANES), jnp.float32)
        for test in range(tests):
            first = 5 + 3 * (part * tests + test)
            pieces = [result[row : row + 1] for row in range(first, first + 3)]
            values = jnp.where(lane // per_brick == test, pieces[0] + (pieces[1] + pieces[2]), values)
        obs_ref[part : part + 1, :] = values
        obs_ref[3 + part : 4 + part, 0:tests] = facts[part][tests : tests + 1, 0:tests]
    obs_ref[2:3, :] = result[4:5]
    clear_ref[...] = jnp.zeros(clear_ref.shape, jnp.float32)
    clear_more_ref[...] = jnp.zeros(clear_ref.shape, jnp.float32)


def at_window_rows(value):
    return pltpu.roll(jnp.concatenate([value, value], axis=0), DEEP, 0)


def window_kernel(log_ref, sto_ref, rec_ref, e_ref, sto_w, rec_w, up_ref):
    base = jnp.where(second_half(), 0, DEEP)
    for x in range(log_ref.shape[0]):
        e = jnp.exp(0.5 * log_ref[x])
        e_ref[base + x] = at_window_rows(e)
        last = lax.broadcasted_iota(jnp.int32, e.shape, 1) == e.shape[1] - 1
        up_ref[base + x] = at_window_rows(e * jnp.where(last, 1.0, pltpu.roll(e, e.shape[1] - 1, 1)))
        sto_w[base + x] = at_window_rows(sto_ref[x])
        rec_w[base + x] = at_window_rows(rec_ref[x])


def pack_y(plan, slab_ref, e_in, sto_in, rec_in, e_ref, sto_w, rec_w, even_ref, odd_ref):
    size_y = slab_ref.shape[1]
    swapped = second_half()
    bx = lax.axis_index("bx")
    absent = jnp.where(swapped, bx == lax.axis_size("bx") - 1, bx == 0)
    y_even = lax.axis_index("by") % 2 == 0
    wides = (e_ref, sto_w, rec_w)
    half_x = e_ref.shape[0] - 2 * DEEP
    place = 0
    for field, reach in enumerate((DEEP, DEEP - 1, DEEP - 1)):
        base = jnp.where(swapped, DEEP + half_x, DEEP - reach)
        for i in range(reach):
            value = slab_ref[place + i]
            value = jnp.exp(0.5 * value) if field == 0 else value
            wides[field][base + i] = at_window_rows(jnp.where(absent, (1.0, 1.0, 0.0)[field], value))
        place += reach
    place = 0
    for field, x, count in plan:
        wide = wides[field]
        up = wide[x, DEEP + size_y - count : DEEP + size_y, :]
        down = wide[x, DEEP : DEEP + count, :]
        at = pl.ds(place, count)
        even_ref[at, :] = jnp.where(y_even, up, down)
        odd_ref[at, :] = jnp.where(y_even, down, up)
        place += count


def field_rows(e_ref, sto_w, rec_w, delta_ref, gamma_ref, beta_ref):
    wide_x, wide_y, size_z = e_ref.shape
    half_x, size_y = wide_x - 2 * DEEP, wide_y - 2 * DEEP
    bx, by, swapped = lax.axis_index("bx"), lax.axis_index("by"), second_half()
    row_at = lax.broadcasted_iota(jnp.int32, (wide_y, size_z), 0)
    z_at = lax.broadcasted_iota(jnp.int32, (wide_y, size_z), 1)
    inside_y = ((row_at >= DEEP) | (by > 0)) & ((row_at < DEEP + size_y) | (by < lax.axis_size("by") - 1))
    for x in range(1, wide_x - 1):
        e = e_ref[x]
        total = e_ref[x - 1] + e_ref[x + 1]
        total = total + pltpu.roll(e, 1, 0) + pltpu.roll(e, wide_y - 1, 0)
        total = total + jnp.where(z_at == 0, 1.0, pltpu.roll(e, 1, 1))
        total = total + jnp.where(z_at == size_z - 1, 1.0, pltpu.roll(e, size_z - 1, 1))
        inside = inside_y
        if x < DEEP:
            inside = inside & (swapped | (bx > 0))
        if x >= DEEP + half_x:
            inside = inside & (jnp.logical_not(swapped) | (bx < lax.axis_size("bx") - 1))
        delta = jnp.where(inside, e / (sto_w[x] + e * total), 0.0)
        delta_ref[x] = delta
        gamma_ref[x] = delta * e
        beta_ref[x] = delta * rec_w[x]


def spread(ref, x, low, high):
    tiles = []
    for y in range(low, high):
        halves = [ref[x, pl.ds(y, 1), part * LANES : (part + 1) * LANES] for part in range(2)]
        tiles.append(jnp.stack([jnp.broadcast_to(half, (8, LANES)) for half in halves]))
    return jnp.stack(tiles)


def lanes():
    return lax.broadcasted_iota(jnp.int32, (8, LANES), 1)


def z_down(values, edge):
    turned = pltpu.roll(values, 1, 3)
    first = lanes() == 0
    return jnp.stack([jnp.where(first, edge, turned[:, 0]), jnp.where(first, turned[:, 0], turned[:, 1])], axis=1)


def z_up(values, edge):
    turned = pltpu.roll(values, LANES - 1, 3)
    last = lanes() == LANES - 1
    return jnp.stack([jnp.where(last, turned[:, 1], turned[:, 0]), jnp.where(last, edge, turned[:, 1])], axis=1)


def columns(ref, wide_y, x, low, high):
    return ref[x * wide_y + low : x * wide_y + high]


def sweep(source_ref, gamma_ref, from_ref, x, low, high):
    wide_y = gamma_ref.shape[1]
    centre = columns(from_ref, wide_y, x, low, high)
    total = columns(from_ref, wide_y, x - 1, low, high) + columns(from_ref, wide_y, x + 1, low, high)
    total = total + columns(from_ref, wide_y, x, low - 1, high - 1) + columns(from_ref, wide_y, x, low + 1, high + 1)
    total = total + z_down(centre, 0.0) + z_up(centre, 0.0)
    return columns(source_ref, wide_y, x, low, high) + spread(gamma_ref, x, low, high) * total


def reached(wide_x, wide_y, reach):
    cells = []
    for x in range(DEEP - reach, wide_x - DEEP + reach):
        left = reach - max(DEEP - x, x - (wide_x - DEEP - 1), 0)
        cells.append((x, DEEP - left, wide_y - DEEP + left))
    return cells


def grouped(cells):
    for x, first, end in cells:
        for low in range(first, end, COLUMNS_AT_ONCE):
            yield x, low, min(low + COLUMNS_AT_ONCE, end)


def solve(bet_ref, gamma_ref, inv_ref, one_ref, two_ref):
    wide_x, wide_y, _ = gamma_ref.shape
    for x, low, high in grouped(reached(wide_x, wide_y, DEEP - 2)):
        one_ref[x * wide_y + low : x * wide_y + high] = sweep(bet_ref, gamma_ref, bet_ref, x, low, high)
    for x, low, high in grouped(reached(wide_x, wide_y, DEEP - 3)):
        scaled = sweep(bet_ref, gamma_ref, one_ref, x, low, high)
        two_ref[x * wide_y + low : x * wide_y + high] = scaled * spread(inv_ref, x, low, high)


def z_of_tile():
    return jnp.stack([lanes(), lanes() + LANES])


def unpack(packed):
    return packed & 255, (packed >> 8) & 255


def heads_kernel(plan, tests, per_brick, even_ref, odd_ref, e_in, sto_in, rec_in, table_ref, obs_ref,
                 e_ref, delta_ref, gamma_ref, inv_ref, head_ref, row_ref, sto_w, rec_w, beta_ref, bet_ref, one_ref):
    wide_x, wide_y, _ = e_ref.shape
    by = lax.axis_index("by")
    y_even = by % 2 == 0
    no_low, no_high = by == 0, by == lax.axis_size("by") - 1
    place = 0
    for field, x, count in plan:
        wide = (e_ref, sto_w, rec_w)[field]
        fill = (1.0, 1.0, 0.0)[field]
        got_e, got_o = even_ref[pl.ds(place, count), :], odd_ref[pl.ds(place, count), :]
        low, high = jnp.where(y_even, got_o, got_e), jnp.where(y_even, got_e, got_o)
        wide[x, DEEP - count : DEEP, :] = jnp.where(no_low, fill, low)
        wide[x, wide_y - DEEP : wide_y - DEEP + count, :] = jnp.where(no_high, fill, high)
        place += count
    field_rows(e_ref, sto_w, rec_w, delta_ref, gamma_ref, beta_ref)
    for x in range(3, wide_x - 3):
        inv_ref[x] = 1.0 / e_ref[x]
    for x, low, high in reached(wide_x, wide_y, DEEP - 1):
        bet_ref[x * wide_y + low : x * wide_y + high] = spread(beta_ref, x, low, high)
    sub = lax.broadcasted_iota(jnp.int32, (8, LANES), 0)
    z_of = z_of_tile()
    listed = list_length(per_brick)
    pumped = []
    for test in range(2 * tests):
        packed = table_ref[listed + LANES + test, 0]
        place, top = unpack(packed)
        near = (packed >> 30) & 1 == 1
        rate = obs_ref[3 + test // tests : 4 + test // tests, test % tests : test % tests + 1]
        delta = delta_ref[place // wide_y, pl.ds(place % wide_y, 1), :]
        delta = jnp.stack([jnp.broadcast_to(delta[:, part * LANES : (part + 1) * LANES], (8, LANES)) for part in range(2)])
        hit = (z_of >= top) & (z_of < top + SCREEN) & (sub == test) & near
        pumped.append((place, jnp.where(hit, delta * rate, 0.0)))
    for place, taken in pumped:
        bet_ref[place] = bet_ref[place] - taken
    solve(bet_ref, gamma_ref, inv_ref, one_ref, head_ref)
    slot_of = lanes() - per_brick * (sub % tests)
    gathered = jnp.zeros((8, LANES), jnp.float32)
    for rank in range(per_brick):
        place, top = unpack(table_ref[listed + rank, 0])
        hit = (z_of >= top) & (z_of < top + SCREEN)
        values = jnp.where(hit, head_ref[place], 0.0)
        gathered = jnp.where(slot_of == rank, jnp.sum(values[0] + values[1], axis=1, keepdims=True), gathered)
    mine = obs_ref[2:3, :] > 0.5
    parts = []
    for part in range(2):
        total = jnp.sum(jnp.where(sub // tests == part, gathered, 0.0), axis=0, keepdims=True)
        parts.append(jnp.where(mine, total * (1.0 / SCREEN) - obs_ref[part : part + 1, :], 0.0))
    row_ref[...] = jnp.broadcast_to(jnp.concatenate(parts, axis=0)[None], row_ref.shape)


def adjoint_kernel(tests, per_brick, n_wells, joined, scale, resid_ref, table_ref, clear_ref, clear_more_ref, e_ref, delta_ref, gamma_ref, inv_ref,
                   bet_ref, more_ref, adj_ref, norm_ref, weight_ref, one_ref):
    wide_x, wide_y, _ = e_ref.shape
    bricks = n_wells // per_brick
    sub = lax.broadcasted_iota(jnp.int32, (8, LANES), 0)
    z_of = z_of_tile()
    resid = resid_ref[:bricks] + resid_ref[bricks:] if joined else resid_ref[...]
    for brick in range(bricks):
        weight_ref[brick] = jnp.where(sub < tests, resid[brick, 0:1], resid[brick, 1:2])
    listed = list_length(per_brick)
    pick = per_brick * (sub % tests)

    def some_wells(turn, carry):
        todo = []
        for step in range(WELLS_AT_ONCE):
            packed = table_ref[turn * WELLS_AT_ONCE + step, 0]
            column, top = unpack(packed)
            brick, rank = (packed >> 16) & 255, (packed >> 24) & 31
            value = jnp.take_along_axis(weight_ref[brick], pick + rank, axis=1, mode="promise_in_bounds")
            todo.append((column, jnp.where((z_of >= top) & (z_of < top + SCREEN), value[None], 0.0)))
        for step, (column, value) in enumerate(todo):
            into_ref = (bet_ref, more_ref)[step % 2]
            into_ref[column] = into_ref[column] + value
        return carry

    turns = (table_ref[listed + LANES + 16, 0] + WELLS_AT_ONCE - 1) // WELLS_AT_ONCE
    lax.fori_loop(0, turns, some_wells, 0)
    for x, low, high in reached(wide_x, wide_y, DEEP - 1):
        row = pl.ds(x * wide_y + low, high - low)
        bet_ref[row] = (bet_ref[row] + more_ref[row]) * spread(delta_ref, x, low, high)
    solve(bet_ref, gamma_ref, inv_ref, one_ref, adj_ref)
    squares = jnp.sum(resid * resid, axis=0)
    squares = jnp.where(sub < tests, squares[0:1], squares[1:2])
    misfit = jnp.sum(jnp.where(lanes() // per_brick == sub % tests, squares, 0.0), axis=1, keepdims=True) / n_wells + EPSILON
    norm_ref[...] = jnp.broadcast_to(scale / misfit, (8, LANES))


def gradient_kernel(kept, norm_ref, e_ref, up_ref, head_ref, adj_ref, out_ref):
    wide_x, wide_y, _ = e_ref.shape
    low, high = DEEP, wide_y - DEEP
    part = jnp.where(second_half(), 1, 0) if kept else jnp.where(second_half(), 0, 1)
    is_first = part == 0
    at_first, at_last = lanes() == 0, lanes() == LANES - 1

    def spread_part(ref, x, first, last, which):
        rows = [ref[x, pl.ds(y, 1), pl.ds(pl.multiple_of(which * LANES, LANES), LANES)] for y in range(first, last)]
        return jnp.stack([jnp.broadcast_to(row, (8, LANES)) for row in rows])

    def tiles(ref, x, first, last, which):
        return ref[x * wide_y + first : x * wide_y + last, which]

    def next_cell(values, others):
        return pltpu.roll(jnp.where(at_first & is_first, others, values), LANES - 1, 2)

    before = None
    for x in range(DEEP - 1, wide_x - DEEP):
        e, head, adjoint = spread_part(e_ref, x, low, high, part), tiles(head_ref, x, low, high, part), tiles(adj_ref, x, low, high, part)
        gap = (head - tiles(head_ref, x + 1, low, high, part)) * (adjoint - tiles(adj_ref, x + 1, low, high, part))
        after = e * spread_part(e_ref, x + 1, low, high, part) * gap
        if x >= DEEP:
            total = before + after
            e_y = spread_part(e_ref, x, low - 1, high + 1, part)
            head_y, adjoint_y = tiles(head_ref, x, low - 1, high + 1, part), tiles(adj_ref, x, low - 1, high + 1, part)
            sides = e_y[:-1] * e_y[1:] * (head_y[:-1] - head_y[1:]) * (adjoint_y[:-1] - adjoint_y[1:])
            total = total + sides[:-1] + sides[1:]
            head_other, adjoint_other = tiles(head_ref, x, low, high, 1 - part), tiles(adj_ref, x, low, high, 1 - part)
            head_next, adjoint_next = next_cell(head, head_other), next_cell(adjoint, adjoint_other)
            at_top = at_last & jnp.logical_not(is_first)
            gap = (head - jnp.where(at_top, 0.0, head_next)) * (adjoint - jnp.where(at_top, 0.0, adjoint_next))
            upper = spread_part(up_ref, x, low, high, part) * gap
            middle = spread_part(up_ref, x, low, high, 1 - part) * (head_other - head_next) * (adjoint_other - adjoint_next)
            lower = pltpu.roll(jnp.where(at_top, middle, upper), 1, 2)
            total = total + upper + jnp.where(at_first & is_first, e * head * adjoint, lower)
            total = jnp.sum(total * norm_ref[...], axis=1, keepdims=True)
            for y in range(high - low):
                out_ref[x - DEEP, pl.ds(y, 1), :] = total[y]
        before = after


def join_kernel(keep_ref, other_ref, out_ref):
    half_x = keep_ref.shape[0]
    mine = jnp.where(second_half(), half_x, 0)
    out_ref[pl.ds(mine, half_x)] = keep_ref[...]
    out_ref[pl.ds(half_x - mine, half_x)] = other_ref[...]


def vmem():
    return pl.BlockSpec(memory_space=pltpu.VMEM)


def smem():
    return pl.BlockSpec(memory_space=pltpu.SMEM)


def f32(*shape):
    return jax.ShapeDtypeStruct(shape, jnp.float32)


def i32(*shape):
    return jax.ShapeDtypeStruct(shape, jnp.int32)


PARAMS = pltpu.CompilerParams(vmem_limit_bytes=24 * 1024 * 1024)


def local(log_conductivity, storage, recharge, pump_rate, pump_well, observed, owner, screen_column, screen_top):
    size_x, size_y, size_z = log_conductivity.shape
    half_x = size_x // 2
    tests = pump_rate.shape[0]
    n_wells = owner.shape[0]
    groups, n_bx, n_by = lax.axis_size("test"), lax.axis_size("bx"), lax.axis_size("by")
    bricks = n_bx * n_by
    per_brick = n_wells // bricks
    plan = slab_plan(half_x)
    rows_x = 3 * DEEP - 2
    rows_y = sum(count for _, _, count in plan)
    wide_x, wide_y = half_x + 2 * DEEP, size_y + 2 * DEEP
    tiles = (wide_x * wide_y, 2, 8, LANES)

    def in_hbm(*arrays):
        return [pltpu.with_memory_space_constraint(a, pltpu.HBM) for a in arrays]

    hbm = pl.BlockSpec(memory_space=pltpu.HBM)
    slab = pl.pallas_call(
        edge_kernel,
        out_shape=f32(rows_x, size_y, size_z),
        in_specs=[hbm] * 3,
        out_specs=vmem(),
        scratch_shapes=[pltpu.SemaphoreType.DMA((3,))],
        compiler_params=PARAMS,
        name="edge",
    )(*in_hbm(log_conductivity, storage, recharge))
    got_x = lax.ppermute(slab, ("test", "bx"), circle(n_bx, groups))

    inputs = (
        observed,
        pump_rate.reshape(1, tests),
        pump_well.reshape(1, tests),
        owner.reshape(1, n_wells),
        screen_column.reshape(1, n_wells),
        screen_top.reshape(1, n_wells),
        log_conductivity,
        storage,
        recharge,
    )
    owner, column, top, log_k, sto, rec, facts = pl.pallas_call(
        load_kernel,
        out_shape=[jax.ShapeDtypeStruct(a.shape, a.dtype) for a in inputs[3:]] + [f32(8, n_wells)],
        in_specs=[hbm] * len(inputs) + [vmem()],
        out_specs=[vmem()] * (len(inputs) - 2),
        scratch_shapes=[pltpu.VMEM((1, tests), jnp.float32), pltpu.VMEM((1, tests), jnp.int32), pltpu.SemaphoreType.DMA((len(inputs),))],
        compiler_params=PARAMS,
        name="load",
    )(*in_hbm(*inputs), slab)
    pairs = [(test, pair_of(test, groups)) for test in range(groups)]
    other_facts = lax.ppermute(facts, "test", pairs)

    bx, by, second = lax.axis_index("bx"), lax.axis_index("by"), lax.axis_index("test") % 2
    well_x = (owner // n_by - bx) * size_x + column // size_y + DEEP - second * half_x
    well_y = (owner % n_by - by) * size_y + column % size_y + DEEP
    out_x = jnp.maximum(jnp.maximum(DEEP - well_x, well_x - (DEEP + half_x - 1)), 0)
    out_y = jnp.maximum(jnp.maximum(DEEP - well_y, well_y - (DEEP + size_y - 1)), 0)
    in_window = (out_x + out_y < DEEP).astype(jnp.float32)
    owned = (out_x + out_y == 0).astype(jnp.float32)
    place = jnp.where(in_window > 0.5, well_x * wide_y + well_y, 0)
    window = f32(wide_x, wide_y, size_z)
    e, sto_w, rec_w, up = pl.pallas_call(
        window_kernel,
        out_shape=[window] * 4,
        in_specs=[vmem()] * 3,
        out_specs=[vmem()] * 4,
        compiler_params=PARAMS,
        name="window",
    )(log_k, sto, rec)
    e, sto_w, rec_w, even_y, odd_y = pl.pallas_call(
        functools.partial(pack_y, plan),
        out_shape=[window] * 3 + [f32(rows_y, size_z)] * 2,
        in_specs=[vmem()] * 4,
        out_specs=[vmem()] * 5,
        input_output_aliases={1: 0, 2: 1, 3: 2},
        compiler_params=PARAMS,
        name="pack_y",
    )(got_x, e, sto_w, rec_w)
    even, odd = side_partners(n_by, groups)
    got_even = lax.ppermute(even_y, ("test", "by"), even)
    got_odd = lax.ppermute(odd_y, ("test", "by"), odd)

    table, obs, clear, clear_more = pl.pallas_call(
        functools.partial(wells_kernel, tests, per_brick, bricks),
        out_shape=[i32(list_length(per_brick) + LANES + 24, 1), f32(8, LANES), f32(*tiles), f32(*tiles)],
        in_specs=[vmem()] * 8,
        out_specs=[vmem()] * 4,
        compiler_params=PARAMS,
        name="wells",
    )(owner, place, top, in_window, owned, facts, other_facts, even_y)

    joined = groups == 2
    copies = groups * bricks if joined else bricks
    e, delta, gamma, inverse, head, row, _, _ = pl.pallas_call(
        functools.partial(heads_kernel, plan, tests, per_brick),
        out_shape=[window] * 4 + [f32(*tiles), f32(copies, 2, LANES)] + [window] * 2,
        in_specs=[vmem()] * 7,
        out_specs=[vmem()] * 8,
        scratch_shapes=[pltpu.VMEM((wide_x, wide_y, size_z), jnp.float32)] + [pltpu.VMEM(tiles, jnp.float32)] * 2,
        input_output_aliases={2: 0, 3: 6, 4: 7},
        compiler_params=PARAMS,
        name="heads",
    )(got_even, got_odd, e, sto_w, rec_w, table, obs)

    if joined:
        residuals = lax.all_to_all(row, ("test", "bx", "by"), 0, 0)
    else:
        residuals = lax.all_to_all(row + lax.ppermute(row, "test", pairs), ("bx", "by"), 0, 0)

    scale = -0.5 / (tests * groups)
    _, _, adjoint, norm = pl.pallas_call(
        functools.partial(adjoint_kernel, tests, per_brick, n_wells, joined, scale),
        out_shape=[f32(*tiles)] * 3 + [f32(8, LANES)],
        in_specs=[vmem()] * 8,
        out_specs=[vmem()] * 4,
        scratch_shapes=[pltpu.VMEM((bricks, 8, LANES), jnp.float32), pltpu.VMEM(tiles, jnp.float32)],
        input_output_aliases={2: 0, 3: 1},
        compiler_params=PARAMS,
        name="adjoint",
    )(residuals, table, clear, clear_more, e, delta, gamma, inverse)

    def gradient_of(kept):
        return pl.pallas_call(
            functools.partial(gradient_kernel, kept),
            out_shape=f32(half_x, size_y, LANES),
            in_specs=[vmem()] * 5,
            out_specs=vmem(),
            compiler_params=PARAMS,
            name="keep" if kept else "send",
        )(norm, e, up, head, adjoint)

    send = gradient_of(False)
    other = lax.ppermute(send, "test", pairs) if joined else send
    keep = gradient_of(True)
    if joined:
        return pl.pallas_call(
            join_kernel,
            out_shape=f32(size_x, size_y, LANES),
            in_specs=[vmem()] * 2,
            out_specs=vmem(),
            compiler_params=PARAMS,
            name="join",
        )(pltpu.with_memory_space_constraint(keep, pltpu.VMEM), pltpu.with_memory_space_constraint(other, pltpu.VMEM))
    low, high = jnp.where(second == 0, keep, send), jnp.where(second == 0, send, keep)
    half = jnp.concatenate([low, high], axis=2)
    none = jnp.zeros_like(half)
    whole = jnp.where(second == 0, jnp.concatenate([half, none], axis=0), jnp.concatenate([none, half], axis=0))
    return lax.psum_scatter(whole, "test", scatter_dimension=2, tiled=True)


def solution(mesh):
    placed = (
        P("bx", "by", None),
        P("bx", "by", None),
        P("bx", "by", None),
        P("test"),
        P("test"),
        P("test", None),
        P(),
        P(),
        P(),
    )
    return jax.shard_map(local, mesh=mesh, in_specs=placed, out_specs=P("bx", "by", "test"), check_vma=False)
```

```python
import functools

import jax
import jax.numpy as jnp
from jax import lax
from jax.experimental import pallas as pl
from jax.experimental.pallas import tpu as pltpu
from jax.sharding import PartitionSpec as P

SCREEN = 8
LANES = 128
DEEP = 4
EPSILON = 1e-06
WELL_CHUNK = 512
WELLS_AT_ONCE = 32
COLUMNS_AT_ONCE = 1


def list_length(per_brick):
    return -(-6 * per_brick // LANES) * LANES


def slab_plan(half_x):
    plan = []
    for field, reach in ((0, DEEP), (1, DEEP - 1), (2, DEEP - 1)):
        for x in range(half_x + 2 * DEEP):
            rows = reach - max(DEEP - x, x - (DEEP + half_x - 1), 0)
            if rows > 0:
                plan.append((field, x, rows))
    return plan


def pair_of(test, tests):
    return test ^ 1 if (test ^ 1) < tests else test


def side_partners(count, tests):
    even, odd = [], []
    for test in range(tests):
        for place in range(count):
            me = test * count + place
            other = pair_of(test, tests) * count + place
            up = place ^ 1
            even.append((me, test * count + up if up < count else other))
            down = ((place + 1) ^ 1) - 1
            odd.append((me, test * count + down if 0 <= down < count else other))
    return even, odd


def circle(count, tests):
    pairs = []
    for test in range(tests):
        for place in range(count):
            to = place + 1 if test % 2 == 0 else place - 1
            me = test * count + place
            pairs.append((me, test * count + to if 0 <= to < count else pair_of(test, tests) * count + place))
    return pairs


def second_half():
    return lax.axis_index("test") % 2 == 1


def edge_kernel(log_ref, sto_ref, rec_ref, slab_ref, sems):
    size_x = log_ref.shape[0]
    copies, place = [], 0
    for field, (ref, reach) in enumerate(((log_ref, DEEP), (sto_ref, DEEP - 1), (rec_ref, DEEP - 1))):
        first = jnp.where(second_half(), 0, size_x - reach)
        copies.append(pltpu.make_async_copy(ref.at[pl.ds(first, reach)], slab_ref.at[pl.ds(place, reach)], sems.at[field]))
        place += reach
    for copy in copies:
        copy.start()
    for copy in copies:
        copy.wait()


def load_kernel(observed, rate, pumped, *refs):
    sources, loaded, facts_ref, (rate_ref, pumped_ref, sems) = refs[:6], refs[7:13], refs[13], refs[14:]
    tests = observed.shape[0]
    moves = [(observed, facts_ref.at[pl.ds(0, tests)]), (rate, rate_ref), (pumped, pumped_ref)] + list(zip(sources, loaded))
    copies = [pltpu.make_async_copy(a, b, sems.at[i]) for i, (a, b) in enumerate(moves)]
    for copy in copies:
        copy.start()
    for copy in copies:
        copy.wait()
    facts_ref[tests : tests + 1, 0:tests] = rate_ref[...]
    facts_ref[tests + 1 : tests + 2, 0:tests] = pumped_ref[...].astype(jnp.float32)


def wells_kernel(tests, per_brick, bricks, owner_ref, place_ref, top_ref, window_ref, owned_ref, facts_ref, other_ref, _, table_ref, obs_ref, clear_ref, clear_more_ref):
    n_wells = owner_ref.shape[1]
    chunk = WELL_CHUNK if n_wells % WELL_CHUNK == 0 else n_wells
    listed = list_length(per_brick)
    before = lax.broadcasted_iota(jnp.int32, (chunk, chunk), 0) < lax.broadcasted_iota(jnp.int32, (chunk, chunk), 1)
    before = jnp.where(before, 1.0, 0.0).astype(jnp.bfloat16)
    brick_at = lax.broadcasted_iota(jnp.int32, (bricks, chunk), 0)
    list_at = lax.broadcasted_iota(jnp.int32, (listed, chunk), 0).astype(jnp.float32)
    own_at = (lax.broadcasted_iota(jnp.int32, (LANES, chunk), 0) % per_brick).astype(jnp.float32)
    lane_at = lax.broadcasted_iota(jnp.int32, (1, chunk), 1).astype(jnp.float32)
    first_row = lax.broadcasted_iota(jnp.int32, (16, chunk), 0) == 0
    swapped = second_half()
    mine, theirs = facts_ref[...], other_ref[...]
    facts = (jnp.where(swapped, theirs, mine), jnp.where(swapped, mine, theirs))
    total = jnp.zeros((bricks + 16, 1), jnp.float32)
    found = jnp.zeros((listed + LANES + 16, 32), jnp.float32)
    result = jnp.zeros((32, LANES), jnp.float32)
    for start in range(0, n_wells, chunk):
        part = slice(start, start + chunk)
        owner = owner_ref[:, part]
        near, own = window_ref[:, part], owned_ref[:, part]
        ones = jnp.where(brick_at == owner, 1.0, 0.0)
        counted = jnp.concatenate([ones, jnp.where(first_row, near, 0.0)], axis=0)
        prefix = jnp.dot(counted.astype(jnp.bfloat16), before, preferred_element_type=jnp.float32) + total
        total = total + jnp.sum(counted, axis=1, keepdims=True)
        rank = jnp.sum(ones * prefix[:bricks], axis=0, keepdims=True)
        in_list = jnp.where((list_at == prefix[bricks : bricks + 1]) & (near > 0.5), 1.0, 0.0)
        in_own = jnp.where((own_at == rank) & (own > 0.5), 1.0, 0.0)
        pumps = []
        for test in range(2 * tests):
            pumped = facts[test // tests][tests + 1 : tests + 2, test % tests : test % tests + 1]
            pumps.append(jnp.where(lane_at + float(start) == pumped, 1.0, 0.0))
        pumps.append(jnp.zeros((16 - 2 * tests, chunk), jnp.float32))
        chosen = jnp.concatenate([in_list, in_own] + pumps, axis=0).astype(jnp.bfloat16)
        rows = [number.astype(jnp.float32) for number in (place_ref[:, part], top_ref[:, part], owner)] + [rank, near]
        for test in range(2 * tests):
            value = facts[test // tests][test % tests : test % tests + 1, part]
            for _ in range(3):
                piece = value.astype(jnp.bfloat16).astype(jnp.float32)
                rows.append(piece)
                value = value - piece
        rows.append(jnp.zeros((32 - len(rows), chunk), jnp.float32))
        carried = jnp.concatenate(rows, axis=0).astype(jnp.bfloat16)
        over_wells = (((1,), (1,)), ((), ()))
        found = found + lax.dot_general(chosen, carried, over_wells, preferred_element_type=jnp.float32)
        result = result + lax.dot_general(carried, chosen[listed : listed + LANES], over_wells, preferred_element_type=jnp.float32)
    column = lax.broadcasted_iota(jnp.int32, found.shape, 1)
    low = jnp.where(column == 0, 1.0, jnp.where(column == 1, 256.0, 0.0))
    high = jnp.where(column == 2, 1.0, jnp.where(column == 3, 256.0, jnp.where(column == 4, 16384.0, 0.0)))
    low, high = (jnp.sum(found * weights, axis=1, keepdims=True).astype(jnp.int32) for weights in (low, high))
    table_ref[0 : listed + LANES + 16, :] = low + (high << 16)
    table_ref[listed + LANES + 16 :, :] = jnp.broadcast_to(total[bricks : bricks + 1], (8, 1)).astype(jnp.int32)
    lane = lax.broadcasted_iota(jnp.int32, (1, LANES), 1)
    for part in range(2):
        values = jnp.zeros((1, LANES), jnp.float32)
        for test in range(tests):
            first = 5 + 3 * (part * tests + test)
            pieces = [result[row : row + 1] for row in range(first, first + 3)]
            values = jnp.where(lane // per_brick == test, pieces[0] + (pieces[1] + pieces[2]), values)
        obs_ref[part : part + 1, :] = values
        obs_ref[3 + part : 4 + part, 0:tests] = facts[part][tests : tests + 1, 0:tests]
    obs_ref[2:3, :] = result[4:5]
    clear_ref[...] = jnp.zeros(clear_ref.shape, jnp.float32)
    clear_more_ref[...] = jnp.zeros(clear_ref.shape, jnp.float32)


def at_window_rows(value):
    return pltpu.roll(jnp.concatenate([value, value], axis=0), DEEP, 0)


def window_kernel(log_ref, sto_ref, rec_ref, e_ref, sto_w, rec_w, up_ref):
    base = jnp.where(second_half(), 0, DEEP)
    for x in range(log_ref.shape[0]):
        e = jnp.exp(0.5 * log_ref[x])
        e_ref[base + x] = at_window_rows(e)
        last = lax.broadcasted_iota(jnp.int32, e.shape, 1) == e.shape[1] - 1
        up_ref[base + x] = at_window_rows(e * jnp.where(last, 1.0, pltpu.roll(e, e.shape[1] - 1, 1)))
        sto_w[base + x] = at_window_rows(sto_ref[x])
        rec_w[base + x] = at_window_rows(rec_ref[x])


def pack_y(plan, slab_ref, e_in, sto_in, rec_in, e_ref, sto_w, rec_w, even_ref, odd_ref):
    size_y = slab_ref.shape[1]
    swapped = second_half()
    bx = lax.axis_index("bx")
    absent = jnp.where(swapped, bx == lax.axis_size("bx") - 1, bx == 0)
    y_even = lax.axis_index("by") % 2 == 0
    wides = (e_ref, sto_w, rec_w)
    half_x = e_ref.shape[0] - 2 * DEEP
    place = 0
    for field, reach in enumerate((DEEP, DEEP - 1, DEEP - 1)):
        base = jnp.where(swapped, DEEP + half_x, DEEP - reach)
        for i in range(reach):
            value = slab_ref[place + i]
            value = jnp.exp(0.5 * value) if field == 0 else value
            wides[field][base + i] = at_window_rows(jnp.where(absent, (1.0, 1.0, 0.0)[field], value))
        place += reach
    place = 0
    for field, x, count in plan:
        wide = wides[field]
        up = wide[x, DEEP + size_y - count : DEEP + size_y, :]
        down = wide[x, DEEP : DEEP + count, :]
        at = pl.ds(place, count)
        even_ref[at, :] = jnp.where(y_even, up, down)
        odd_ref[at, :] = jnp.where(y_even, down, up)
        place += count


def field_rows(e_ref, sto_w, rec_w, delta_ref, gamma_ref, beta_ref):
    wide_x, wide_y, size_z = e_ref.shape
    half_x, size_y = wide_x - 2 * DEEP, wide_y - 2 * DEEP
    bx, by, swapped = lax.axis_index("bx"), lax.axis_index("by"), second_half()
    row_at = lax.broadcasted_iota(jnp.int32, (wide_y, size_z), 0)
    z_at = lax.broadcasted_iota(jnp.int32, (wide_y, size_z), 1)
    inside_y = ((row_at >= DEEP) | (by > 0)) & ((row_at < DEEP + size_y) | (by < lax.axis_size("by") - 1))
    for x in range(1, wide_x - 1):
        e = e_ref[x]
        total = e_ref[x - 1] + e_ref[x + 1]
        total = total + pltpu.roll(e, 1, 0) + pltpu.roll(e, wide_y - 1, 0)
        total = total + jnp.where(z_at == 0, 1.0, pltpu.roll(e, 1, 1))
        total = total + jnp.where(z_at == size_z - 1, 1.0, pltpu.roll(e, size_z - 1, 1))
        inside = inside_y
        if x < DEEP:
            inside = inside & (swapped | (bx > 0))
        if x >= DEEP + half_x:
            inside = inside & (jnp.logical_not(swapped) | (bx < lax.axis_size("bx") - 1))
        delta = jnp.where(inside, e / (sto_w[x] + e * total), 0.0)
        delta_ref[x] = delta
        gamma_ref[x] = delta * e
        beta_ref[x] = delta * rec_w[x]


def spread(ref, x, low, high):
    tiles = []
    for y in range(low, high):
        halves = [ref[x, pl.ds(y, 1), part * LANES : (part + 1) * LANES] for part in range(2)]
        tiles.append(jnp.stack([jnp.broadcast_to(half, (8, LANES)) for half in halves]))
    return jnp.stack(tiles)


def lanes():
    return lax.broadcasted_iota(jnp.int32, (8, LANES), 1)


def z_down(values, edge):
    turned = pltpu.roll(values, 1, 3)
    first = lanes() == 0
    return jnp.stack([jnp.where(first, edge, turned[:, 0]), jnp.where(first, turned[:, 0], turned[:, 1])], axis=1)


def z_up(values, edge):
    turned = pltpu.roll(values, LANES - 1, 3)
    last = lanes() == LANES - 1
    return jnp.stack([jnp.where(last, turned[:, 1], turned[:, 0]), jnp.where(last, edge, turned[:, 1])], axis=1)


def columns(ref, wide_y, x, low, high):
    return ref[x * wide_y + low : x * wide_y + high]


def sweep(source_ref, gamma_ref, from_ref, x, low, high):
    wide_y = gamma_ref.shape[1]
    centre = columns(from_ref, wide_y, x, low, high)
    total = columns(from_ref, wide_y, x - 1, low, high) + columns(from_ref, wide_y, x + 1, low, high)
    total = total + columns(from_ref, wide_y, x, low - 1, high - 1) + columns(from_ref, wide_y, x, low + 1, high + 1)
    total = total + z_down(centre, 0.0) + z_up(centre, 0.0)
    return columns(source_ref, wide_y, x, low, high) + spread(gamma_ref, x, low, high) * total


def reached(wide_x, wide_y, reach):
    cells = []
    for x in range(DEEP - reach, wide_x - DEEP + reach):
        left = reach - max(DEEP - x, x - (wide_x - DEEP - 1), 0)
        cells.append((x, DEEP - left, wide_y - DEEP + left))
    return cells


def without(cells, wide_y, margin):
    for x, low, high in cells:
        yield x, low, margin
        yield x, wide_y - margin, high


def grouped(cells):
    for x, first, end in cells:
        for low in range(first, end, COLUMNS_AT_ONCE):
            yield x, low, min(low + COLUMNS_AT_ONCE, end)


def solve(bet_ref, gamma_ref, inv_ref, one_ref, two_ref):
    wide_x, wide_y, _ = gamma_ref.shape
    for x, low, high in grouped(reached(wide_x, wide_y, DEEP - 2)):
        one_ref[x * wide_y + low : x * wide_y + high] = sweep(bet_ref, gamma_ref, bet_ref, x, low, high)
    for x, low, high in grouped(reached(wide_x, wide_y, DEEP - 3)):
        scaled = sweep(bet_ref, gamma_ref, one_ref, x, low, high)
        two_ref[x * wide_y + low : x * wide_y + high] = scaled * spread(inv_ref, x, low, high)


def z_of_tile():
    return jnp.stack([lanes(), lanes() + LANES])


def unpack(packed):
    return packed & 255, (packed >> 8) & 255


def pump(tests, per_brick, inner, wide_y, table_ref, obs_ref, delta_ref, bet_ref):
    sub = lax.broadcasted_iota(jnp.int32, (8, LANES), 0)
    z_of = z_of_tile()
    listed = list_length(per_brick)
    pumped = []
    for test in range(2 * tests):
        packed = table_ref[listed + LANES + test, 0]
        place, top = unpack(packed)
        y = place % wide_y
        is_inner = (y >= DEEP + 1) & (y < wide_y - DEEP - 1)
        near = ((packed >> 30) & 1 == 1) & (is_inner if inner else jnp.logical_not(is_inner))
        rate = obs_ref[3 + test // tests : 4 + test // tests, test % tests : test % tests + 1]
        delta = delta_ref[place // wide_y, pl.ds(y, 1), :]
        delta = jnp.stack([jnp.broadcast_to(delta[:, part * LANES : (part + 1) * LANES], (8, LANES)) for part in range(2)])
        hit = (z_of >= top) & (z_of < top + SCREEN) & (sub == test) & near
        pumped.append((place, jnp.where(hit, delta * rate, 0.0)))
    for place, taken in pumped:
        bet_ref[place] = bet_ref[place] - taken


def inner_kernel(tests, per_brick, e_ref, sto_w, rec_w, table_ref, obs_ref,
                 bet_ref, one_ref, head_ref, delta_ref, gamma_ref, beta_ref, inv_ref):
    wide_x, wide_y, _ = e_ref.shape
    field_rows(e_ref, sto_w, rec_w, delta_ref, gamma_ref, beta_ref)
    for x in range(3, wide_x - 3):
        inv_ref[x] = 1.0 / e_ref[x]
    for x in range(1, wide_x - 1):
        bet_ref[x * wide_y + DEEP + 1 : (x + 1) * wide_y - DEEP - 1] = spread(beta_ref, x, DEEP + 1, wide_y - DEEP - 1)
    pump(tests, per_brick, True, wide_y, table_ref, obs_ref, delta_ref, bet_ref)
    for x in range(2, wide_x - 2):
        low, high = DEEP + 2, wide_y - DEEP - 2
        one_ref[x * wide_y + low : x * wide_y + high] = sweep(bet_ref, gamma_ref, bet_ref, x, low, high)
    for x in range(3, wide_x - 3):
        low, high = DEEP + 3, wide_y - DEEP - 3
        scaled = sweep(bet_ref, gamma_ref, one_ref, x, low, high)
        head_ref[x * wide_y + low : x * wide_y + high] = scaled * spread(inv_ref, x, low, high)


def heads_kernel(plan, tests, per_brick, even_ref, odd_ref, e_in, sto_in, rec_in, table_ref, obs_ref, bet_in, one_in, head_in,
                 e_ref, delta_ref, gamma_ref, inv_ref, head_ref, row_ref, sto_w, rec_w, bet_ref, one_ref, beta_ref):
    wide_x, wide_y, _ = e_ref.shape
    by = lax.axis_index("by")
    y_even = by % 2 == 0
    no_low, no_high = by == 0, by == lax.axis_size("by") - 1
    place = 0
    for field, x, count in plan:
        wide = (e_ref, sto_w, rec_w)[field]
        fill = (1.0, 1.0, 0.0)[field]
        got_e, got_o = even_ref[pl.ds(place, count), :], odd_ref[pl.ds(place, count), :]
        low, high = jnp.where(y_even, got_o, got_e), jnp.where(y_even, got_e, got_o)
        wide[x, DEEP - count : DEEP, :] = jnp.where(no_low, fill, low)
        wide[x, wide_y - DEEP : wide_y - DEEP + count, :] = jnp.where(no_high, fill, high)
        place += count
    field_rows(e_ref, sto_w, rec_w, delta_ref, gamma_ref, beta_ref)
    for x in range(3, wide_x - 3):
        inv_ref[x] = 1.0 / e_ref[x]
    for x, low, high in without(reached(wide_x, wide_y, DEEP - 1), wide_y, DEEP + 1):
        bet_ref[x * wide_y + low : x * wide_y + high] = spread(beta_ref, x, low, high)
    sub = lax.broadcasted_iota(jnp.int32, (8, LANES), 0)
    z_of = z_of_tile()
    listed = list_length(per_brick)
    pump(tests, per_brick, False, wide_y, table_ref, obs_ref, delta_ref, bet_ref)
    for x, low, high in without(reached(wide_x, wide_y, DEEP - 2), wide_y, DEEP + 2):
        one_ref[x * wide_y + low : x * wide_y + high] = sweep(bet_ref, gamma_ref, bet_ref, x, low, high)
    for x, low, high in without(reached(wide_x, wide_y, DEEP - 3), wide_y, DEEP + 3):
        scaled = sweep(bet_ref, gamma_ref, one_ref, x, low, high)
        head_ref[x * wide_y + low : x * wide_y + high] = scaled * spread(inv_ref, x, low, high)
    slot_of = lanes() - per_brick * (sub % tests)
    gathered = jnp.zeros((8, LANES), jnp.float32)
    for rank in range(per_brick):
        place, top = unpack(table_ref[listed + rank, 0])
        hit = (z_of >= top) & (z_of < top + SCREEN)
        values = jnp.where(hit, head_ref[place], 0.0)
        gathered = jnp.where(slot_of == rank, jnp.sum(values[0] + values[1], axis=1, keepdims=True), gathered)
    mine = obs_ref[2:3, :] > 0.5
    parts = []
    for part in range(2):
        total = jnp.sum(jnp.where(sub // tests == part, gathered, 0.0), axis=0, keepdims=True)
        parts.append(jnp.where(mine, total * (1.0 / SCREEN) - obs_ref[part : part + 1, :], 0.0))
    row_ref[...] = jnp.broadcast_to(jnp.concatenate(parts, axis=0)[None], row_ref.shape)


def adjoint_kernel(tests, per_brick, n_wells, joined, scale, resid_ref, table_ref, clear_ref, clear_more_ref, e_ref, delta_ref, gamma_ref, inv_ref,
                   bet_ref, more_ref, adj_ref, norm_ref, weight_ref, one_ref):
    wide_x, wide_y, _ = e_ref.shape
    bricks = n_wells // per_brick
    sub = lax.broadcasted_iota(jnp.int32, (8, LANES), 0)
    z_of = z_of_tile()
    resid = resid_ref[:bricks] + resid_ref[bricks:] if joined else resid_ref[...]
    for brick in range(bricks):
        weight_ref[brick] = jnp.where(sub < tests, resid[brick, 0:1], resid[brick, 1:2])
    listed = list_length(per_brick)
    pick = per_brick * (sub % tests)

    def some_wells(turn, carry):
        todo = []
        for step in range(WELLS_AT_ONCE):
            packed = table_ref[turn * WELLS_AT_ONCE + step, 0]
            column, top = unpack(packed)
            brick, rank = (packed >> 16) & 255, (packed >> 24) & 31
            value = jnp.take_along_axis(weight_ref[brick], pick + rank, axis=1, mode="promise_in_bounds")
            todo.append((column, jnp.where((z_of >= top) & (z_of < top + SCREEN), value[None], 0.0)))
        for step, (column, value) in enumerate(todo):
            into_ref = (bet_ref, more_ref)[step % 2]
            into_ref[column] = into_ref[column] + value
        return carry

    turns = (table_ref[listed + LANES + 16, 0] + WELLS_AT_ONCE - 1) // WELLS_AT_ONCE
    lax.fori_loop(0, turns, some_wells, 0)
    for x, low, high in reached(wide_x, wide_y, DEEP - 1):
        row = pl.ds(x * wide_y + low, high - low)
        bet_ref[row] = (bet_ref[row] + more_ref[row]) * spread(delta_ref, x, low, high)
    solve(bet_ref, gamma_ref, inv_ref, one_ref, adj_ref)
    squares = jnp.sum(resid * resid, axis=0)
    squares = jnp.where(sub < tests, squares[0:1], squares[1:2])
    misfit = jnp.sum(jnp.where(lanes() // per_brick == sub % tests, squares, 0.0), axis=1, keepdims=True) / n_wells + EPSILON
    norm_ref[...] = jnp.broadcast_to(scale / misfit, (8, LANES))


def gradient_kernel(kept, norm_ref, e_ref, up_ref, head_ref, adj_ref, out_ref):
    wide_x, wide_y, _ = e_ref.shape
    low, high = DEEP, wide_y - DEEP
    part = jnp.where(second_half(), 1, 0) if kept else jnp.where(second_half(), 0, 1)
    is_first = part == 0
    at_first, at_last = lanes() == 0, lanes() == LANES - 1

    def spread_part(ref, x, first, last, which):
        rows = [ref[x, pl.ds(y, 1), pl.ds(pl.multiple_of(which * LANES, LANES), LANES)] for y in range(first, last)]
        return jnp.stack([jnp.broadcast_to(row, (8, LANES)) for row in rows])

    def tiles(ref, x, first, last, which):
        return ref[x * wide_y + first : x * wide_y + last, which]

    def next_cell(values, others):
        return pltpu.roll(jnp.where(at_first & is_first, others, values), LANES - 1, 2)

    before = None
    for x in range(DEEP - 1, wide_x - DEEP):
        e, head, adjoint = spread_part(e_ref, x, low, high, part), tiles(head_ref, x, low, high, part), tiles(adj_ref, x, low, high, part)
        gap = (head - tiles(head_ref, x + 1, low, high, part)) * (adjoint - tiles(adj_ref, x + 1, low, high, part))
        after = e * spread_part(e_ref, x + 1, low, high, part) * gap
        if x >= DEEP:
            total = before + after
            e_y = spread_part(e_ref, x, low - 1, high + 1, part)
            head_y, adjoint_y = tiles(head_ref, x, low - 1, high + 1, part), tiles(adj_ref, x, low - 1, high + 1, part)
            sides = e_y[:-1] * e_y[1:] * (head_y[:-1] - head_y[1:]) * (adjoint_y[:-1] - adjoint_y[1:])
            total = total + sides[:-1] + sides[1:]
            head_other, adjoint_other = tiles(head_ref, x, low, high, 1 - part), tiles(adj_ref, x, low, high, 1 - part)
            head_next, adjoint_next = next_cell(head, head_other), next_cell(adjoint, adjoint_other)
            at_top = at_last & jnp.logical_not(is_first)
            gap = (head - jnp.where(at_top, 0.0, head_next)) * (adjoint - jnp.where(at_top, 0.0, adjoint_next))
            upper = spread_part(up_ref, x, low, high, part) * gap
            middle = spread_part(up_ref, x, low, high, 1 - part) * (head_other - head_next) * (adjoint_other - adjoint_next)
            lower = pltpu.roll(jnp.where(at_top, middle, upper), 1, 2)
            total = total + upper + jnp.where(at_first & is_first, e * head * adjoint, lower)
            total = jnp.sum(total * norm_ref[...], axis=1, keepdims=True)
            for y in range(high - low):
                out_ref[x - DEEP, pl.ds(y, 1), :] = total[y]
        before = after


def join_kernel(keep_ref, other_ref, out_ref):
    half_x = keep_ref.shape[0]
    mine = jnp.where(second_half(), half_x, 0)
    out_ref[pl.ds(mine, half_x)] = keep_ref[...]
    out_ref[pl.ds(half_x - mine, half_x)] = other_ref[...]


def vmem():
    return pl.BlockSpec(memory_space=pltpu.VMEM)


def smem():
    return pl.BlockSpec(memory_space=pltpu.SMEM)


def f32(*shape):
    return jax.ShapeDtypeStruct(shape, jnp.float32)


def i32(*shape):
    return jax.ShapeDtypeStruct(shape, jnp.int32)


PARAMS = pltpu.CompilerParams(vmem_limit_bytes=24 * 1024 * 1024)


def local(log_conductivity, storage, recharge, pump_rate, pump_well, observed, owner, screen_column, screen_top):
    size_x, size_y, size_z = log_conductivity.shape
    half_x = size_x // 2
    tests = pump_rate.shape[0]
    n_wells = owner.shape[0]
    groups, n_bx, n_by = lax.axis_size("test"), lax.axis_size("bx"), lax.axis_size("by")
    bricks = n_bx * n_by
    per_brick = n_wells // bricks
    plan = slab_plan(half_x)
    rows_x = 3 * DEEP - 2
    rows_y = sum(count for _, _, count in plan)
    wide_x, wide_y = half_x + 2 * DEEP, size_y + 2 * DEEP
    tiles = (wide_x * wide_y, 2, 8, LANES)

    def in_hbm(*arrays):
        return [pltpu.with_memory_space_constraint(a, pltpu.HBM) for a in arrays]

    hbm = pl.BlockSpec(memory_space=pltpu.HBM)
    slab = pl.pallas_call(
        edge_kernel,
        out_shape=f32(rows_x, size_y, size_z),
        in_specs=[hbm] * 3,
        out_specs=vmem(),
        scratch_shapes=[pltpu.SemaphoreType.DMA((3,))],
        compiler_params=PARAMS,
        name="edge",
    )(*in_hbm(log_conductivity, storage, recharge))
    got_x = lax.ppermute(slab, ("test", "bx"), circle(n_bx, groups))

    inputs = (
        observed,
        pump_rate.reshape(1, tests),
        pump_well.reshape(1, tests),
        owner.reshape(1, n_wells),
        screen_column.reshape(1, n_wells),
        screen_top.reshape(1, n_wells),
        log_conductivity,
        storage,
        recharge,
    )
    owner, column, top, log_k, sto, rec, facts = pl.pallas_call(
        load_kernel,
        out_shape=[jax.ShapeDtypeStruct(a.shape, a.dtype) for a in inputs[3:]] + [f32(8, n_wells)],
        in_specs=[hbm] * len(inputs) + [vmem()],
        out_specs=[vmem()] * (len(inputs) - 2),
        scratch_shapes=[pltpu.VMEM((1, tests), jnp.float32), pltpu.VMEM((1, tests), jnp.int32), pltpu.SemaphoreType.DMA((len(inputs),))],
        compiler_params=PARAMS,
        name="load",
    )(*in_hbm(*inputs), slab)
    pairs = [(test, pair_of(test, groups)) for test in range(groups)]
    other_facts = lax.ppermute(facts, "test", pairs)

    bx, by, second = lax.axis_index("bx"), lax.axis_index("by"), lax.axis_index("test") % 2
    well_x = (owner // n_by - bx) * size_x + column // size_y + DEEP - second * half_x
    well_y = (owner % n_by - by) * size_y + column % size_y + DEEP
    out_x = jnp.maximum(jnp.maximum(DEEP - well_x, well_x - (DEEP + half_x - 1)), 0)
    out_y = jnp.maximum(jnp.maximum(DEEP - well_y, well_y - (DEEP + size_y - 1)), 0)
    in_window = (out_x + out_y < DEEP).astype(jnp.float32)
    owned = (out_x + out_y == 0).astype(jnp.float32)
    place = jnp.where(in_window > 0.5, well_x * wide_y + well_y, 0)
    window = f32(wide_x, wide_y, size_z)
    e, sto_w, rec_w, up = pl.pallas_call(
        window_kernel,
        out_shape=[window] * 4,
        in_specs=[vmem()] * 3,
        out_specs=[vmem()] * 4,
        compiler_params=PARAMS,
        name="window",
    )(log_k, sto, rec)
    e, sto_w, rec_w, even_y, odd_y = pl.pallas_call(
        functools.partial(pack_y, plan),
        out_shape=[window] * 3 + [f32(rows_y, size_z)] * 2,
        in_specs=[vmem()] * 4,
        out_specs=[vmem()] * 5,
        input_output_aliases={1: 0, 2: 1, 3: 2},
        compiler_params=PARAMS,
        name="pack_y",
    )(got_x, e, sto_w, rec_w)
    even, odd = side_partners(n_by, groups)
    got_even = lax.ppermute(even_y, ("test", "by"), even)
    got_odd = lax.ppermute(odd_y, ("test", "by"), odd)

    table, obs, clear, clear_more = pl.pallas_call(
        functools.partial(wells_kernel, tests, per_brick, bricks),
        out_shape=[i32(list_length(per_brick) + LANES + 24, 1), f32(8, LANES), f32(*tiles), f32(*tiles)],
        in_specs=[vmem()] * 8,
        out_specs=[vmem()] * 4,
        compiler_params=PARAMS,
        name="wells",
    )(owner, place, top, in_window, owned, facts, other_facts, even_y)

    joined = groups == 2
    copies = groups * bricks if joined else bricks
    inner = pl.pallas_call(
        functools.partial(inner_kernel, tests, per_brick),
        out_shape=[f32(*tiles)] * 3,
        in_specs=[vmem()] * 5,
        out_specs=[vmem()] * 3,
        scratch_shapes=[pltpu.VMEM((wide_x, wide_y, size_z), jnp.float32)] * 4,
        compiler_params=PARAMS,
        name="inner",
    )(e, sto_w, rec_w, table, obs)
    e, delta, gamma, inverse, head, row = pl.pallas_call(
        functools.partial(heads_kernel, plan, tests, per_brick),
        out_shape=[window] * 4 + [f32(*tiles), f32(copies, 2, LANES)] + [window] * 2 + [f32(*tiles)] * 2,
        in_specs=[vmem()] * 10,
        out_specs=[vmem()] * 10,
        scratch_shapes=[pltpu.VMEM((wide_x, wide_y, size_z), jnp.float32)],
        input_output_aliases={2: 0, 3: 6, 4: 7, 7: 8, 8: 9, 9: 4},
        compiler_params=PARAMS,
        name="heads",
    )(got_even, got_odd, e, sto_w, rec_w, table, obs, *inner)[:6]

    if joined:
        residuals = lax.all_to_all(row, ("test", "bx", "by"), 0, 0)
    else:
        residuals = lax.all_to_all(row + lax.ppermute(row, "test", pairs), ("bx", "by"), 0, 0)

    scale = -0.5 / (tests * groups)
    _, _, adjoint, norm = pl.pallas_call(
        functools.partial(adjoint_kernel, tests, per_brick, n_wells, joined, scale),
        out_shape=[f32(*tiles)] * 3 + [f32(8, LANES)],
        in_specs=[vmem()] * 8,
        out_specs=[vmem()] * 4,
        scratch_shapes=[pltpu.VMEM((bricks, 8, LANES), jnp.float32), pltpu.VMEM(tiles, jnp.float32)],
        input_output_aliases={2: 0, 3: 1},
        compiler_params=PARAMS,
        name="adjoint",
    )(residuals, table, clear, clear_more, e, delta, gamma, inverse)

    def gradient_of(kept):
        return pl.pallas_call(
            functools.partial(gradient_kernel, kept),
            out_shape=f32(half_x, size_y, LANES),
            in_specs=[vmem()] * 5,
            out_specs=vmem(),
            compiler_params=PARAMS,
            name="keep" if kept else "send",
        )(norm, e, up, head, adjoint)

    send = gradient_of(False)
    other = lax.ppermute(send, "test", pairs) if joined else send
    keep = gradient_of(True)
    if joined:
        return pl.pallas_call(
            join_kernel,
            out_shape=f32(size_x, size_y, LANES),
            in_specs=[vmem()] * 2,
            out_specs=vmem(),
            compiler_params=PARAMS,
            name="join",
        )(pltpu.with_memory_space_constraint(keep, pltpu.VMEM), pltpu.with_memory_space_constraint(other, pltpu.VMEM))
    low, high = jnp.where(second == 0, keep, send), jnp.where(second == 0, send, keep)
    half = jnp.concatenate([low, high], axis=2)
    none = jnp.zeros_like(half)
    whole = jnp.where(second == 0, jnp.concatenate([half, none], axis=0), jnp.concatenate([none, half], axis=0))
    return lax.psum_scatter(whole, "test", scatter_dimension=2, tiled=True)


def solution(mesh):
    placed = (
        P("bx", "by", None),
        P("bx", "by", None),
        P("bx", "by", None),
        P("test"),
        P("test"),
        P("test", None),
        P(),
        P(),
        P(),
    )
    return jax.shard_map(local, mesh=mesh, in_specs=placed, out_specs=P("bx", "by", "test"), check_vma=False)
```

```python
import functools

import jax
import jax.numpy as jnp
from jax import lax
from jax.experimental import pallas as pl
from jax.experimental.pallas import tpu as pltpu
from jax.sharding import PartitionSpec as P

SCREEN = 8
LANES = 128
DEEP = 4
EPSILON = 1e-06
WELL_CHUNK = 512
WELLS_AT_ONCE = 32
COLUMNS_AT_ONCE = 1


def list_length(per_brick):
    return -(-6 * per_brick // LANES) * LANES


def slab_plan(half_x):
    plan = []
    for field, reach in ((0, DEEP), (1, DEEP - 1), (2, DEEP - 1)):
        for x in range(half_x + 2 * DEEP):
            rows = reach - max(DEEP - x, x - (DEEP + half_x - 1), 0)
            if rows > 0:
                plan.append((field, x, rows))
    return plan


def pair_of(test, tests):
    return test ^ 1 if (test ^ 1) < tests else test


def side_partners(count, tests):
    even, odd = [], []
    for test in range(tests):
        for place in range(count):
            me = test * count + place
            other = pair_of(test, tests) * count + place
            up = place ^ 1
            even.append((me, test * count + up if up < count else other))
            down = ((place + 1) ^ 1) - 1
            odd.append((me, test * count + down if 0 <= down < count else other))
    return even, odd


def circle(count, tests):
    pairs = []
    for test in range(tests):
        for place in range(count):
            to = place + 1 if test % 2 == 0 else place - 1
            me = test * count + place
            pairs.append((me, test * count + to if 0 <= to < count else pair_of(test, tests) * count + place))
    return pairs


def second_half():
    return lax.axis_index("test") % 2 == 1


def edge_kernel(log_ref, sto_ref, rec_ref, slab_ref, sems):
    size_x = log_ref.shape[0]
    copies, place = [], 0
    for field, (ref, reach) in enumerate(((log_ref, DEEP), (sto_ref, DEEP - 1), (rec_ref, DEEP - 1))):
        first = jnp.where(second_half(), 0, size_x - reach)
        copies.append(pltpu.make_async_copy(ref.at[pl.ds(first, reach)], slab_ref.at[pl.ds(place, reach)], sems.at[field]))
        place += reach
    for copy in copies:
        copy.start()
    for copy in copies:
        copy.wait()


def load_kernel(observed, rate, pumped, *refs):
    sources, loaded, facts_ref, (rate_ref, pumped_ref, sems) = refs[:6], refs[7:13], refs[13], refs[14:]
    tests = observed.shape[0]
    moves = [(observed, facts_ref.at[pl.ds(0, tests)]), (rate, rate_ref), (pumped, pumped_ref)] + list(zip(sources, loaded))
    copies = [pltpu.make_async_copy(a, b, sems.at[i]) for i, (a, b) in enumerate(moves)]
    for copy in copies:
        copy.start()
    for copy in copies:
        copy.wait()
    facts_ref[tests : tests + 1, 0:tests] = rate_ref[...]
    facts_ref[tests + 1 : tests + 2, 0:tests] = pumped_ref[...].astype(jnp.float32)


def wells_kernel(tests, per_brick, bricks, owner_ref, place_ref, top_ref, window_ref, owned_ref, facts_ref, other_ref, _, table_ref, obs_ref, clear_ref, clear_more_ref):
    n_wells = owner_ref.shape[1]
    chunk = WELL_CHUNK if n_wells % WELL_CHUNK == 0 else n_wells
    listed = list_length(per_brick)
    before = lax.broadcasted_iota(jnp.int32, (chunk, chunk), 0) < lax.broadcasted_iota(jnp.int32, (chunk, chunk), 1)
    before = jnp.where(before, 1.0, 0.0).astype(jnp.bfloat16)
    brick_at = lax.broadcasted_iota(jnp.int32, (bricks, chunk), 0)
    list_at = lax.broadcasted_iota(jnp.int32, (listed, chunk), 0).astype(jnp.float32)
    own_at = (lax.broadcasted_iota(jnp.int32, (LANES, chunk), 0) % per_brick).astype(jnp.float32)
    lane_at = lax.broadcasted_iota(jnp.int32, (1, chunk), 1).astype(jnp.float32)
    first_row = lax.broadcasted_iota(jnp.int32, (16, chunk), 0) == 0
    swapped = second_half()
    mine, theirs = facts_ref[...], other_ref[...]
    facts = (jnp.where(swapped, theirs, mine), jnp.where(swapped, mine, theirs))
    total = jnp.zeros((bricks + 16, 1), jnp.float32)
    found = jnp.zeros((listed + LANES + 16, 32), jnp.float32)
    result = jnp.zeros((32, LANES), jnp.float32)
    for start in range(0, n_wells, chunk):
        part = slice(start, start + chunk)
        owner = owner_ref[:, part]
        near, own = window_ref[:, part], owned_ref[:, part]
        ones = jnp.where(brick_at == owner, 1.0, 0.0)
        counted = jnp.concatenate([ones, jnp.where(first_row, near, 0.0)], axis=0)
        prefix = jnp.dot(counted.astype(jnp.bfloat16), before, preferred_element_type=jnp.float32) + total
        total = total + jnp.sum(counted, axis=1, keepdims=True)
        rank = jnp.sum(ones * prefix[:bricks], axis=0, keepdims=True)
        in_list = jnp.where((list_at == prefix[bricks : bricks + 1]) & (near > 0.5), 1.0, 0.0)
        in_own = jnp.where((own_at == rank) & (own > 0.5), 1.0, 0.0)
        pumps = []
        for test in range(2 * tests):
            pumped = facts[test // tests][tests + 1 : tests + 2, test % tests : test % tests + 1]
            pumps.append(jnp.where(lane_at + float(start) == pumped, 1.0, 0.0))
        pumps.append(jnp.zeros((16 - 2 * tests, chunk), jnp.float32))
        chosen = jnp.concatenate([in_list, in_own] + pumps, axis=0).astype(jnp.bfloat16)
        rows = [number.astype(jnp.float32) for number in (place_ref[:, part], top_ref[:, part], owner)] + [rank, near]
        for test in range(2 * tests):
            value = facts[test // tests][test % tests : test % tests + 1, part]
            for _ in range(3):
                piece = value.astype(jnp.bfloat16).astype(jnp.float32)
                rows.append(piece)
                value = value - piece
        rows.append(jnp.zeros((32 - len(rows), chunk), jnp.float32))
        carried = jnp.concatenate(rows, axis=0).astype(jnp.bfloat16)
        over_wells = (((1,), (1,)), ((), ()))
        found = found + lax.dot_general(chosen, carried, over_wells, preferred_element_type=jnp.float32)
        result = result + lax.dot_general(carried, chosen[listed : listed + LANES], over_wells, preferred_element_type=jnp.float32)
    column = lax.broadcasted_iota(jnp.int32, found.shape, 1)
    low = jnp.where(column == 0, 1.0, jnp.where(column == 1, 256.0, 0.0))
    high = jnp.where(column == 2, 1.0, jnp.where(column == 3, 256.0, jnp.where(column == 4, 16384.0, 0.0)))
    low, high = (jnp.sum(found * weights, axis=1, keepdims=True).astype(jnp.int32) for weights in (low, high))
    table_ref[0 : listed + LANES + 16, :] = low + (high << 16)
    table_ref[listed + LANES + 16 :, :] = jnp.broadcast_to(total[bricks : bricks + 1], (8, 1)).astype(jnp.int32)
    lane = lax.broadcasted_iota(jnp.int32, (1, LANES), 1)
    for part in range(2):
        values = jnp.zeros((1, LANES), jnp.float32)
        for test in range(tests):
            first = 5 + 3 * (part * tests + test)
            pieces = [result[row : row + 1] for row in range(first, first + 3)]
            values = jnp.where(lane // per_brick == test, pieces[0] + (pieces[1] + pieces[2]), values)
        obs_ref[part : part + 1, :] = values
        obs_ref[3 + part : 4 + part, 0:tests] = facts[part][tests : tests + 1, 0:tests]
    obs_ref[2:3, :] = result[4:5]
    clear_ref[...] = jnp.zeros(clear_ref.shape, jnp.float32)
    clear_more_ref[...] = jnp.zeros(clear_ref.shape, jnp.float32)


def at_window_rows(value):
    return pltpu.roll(jnp.concatenate([value, value], axis=0), DEEP, 0)


def window_kernel(log_ref, sto_ref, rec_ref, e_ref, sto_w, rec_w, up_ref):
    base = jnp.where(second_half(), 0, DEEP)
    for x in range(log_ref.shape[0]):
        e = jnp.exp(0.5 * log_ref[x])
        e_ref[base + x] = at_window_rows(e)
        last = lax.broadcasted_iota(jnp.int32, e.shape, 1) == e.shape[1] - 1
        up_ref[base + x] = at_window_rows(e * jnp.where(last, 1.0, pltpu.roll(e, e.shape[1] - 1, 1)))
        sto_w[base + x] = at_window_rows(sto_ref[x])
        rec_w[base + x] = at_window_rows(rec_ref[x])


def pack_y(plan, slab_ref, e_in, sto_in, rec_in, e_ref, sto_w, rec_w, even_ref, odd_ref):
    size_y = slab_ref.shape[1]
    swapped = second_half()
    bx = lax.axis_index("bx")
    absent = jnp.where(swapped, bx == lax.axis_size("bx") - 1, bx == 0)
    y_even = lax.axis_index("by") % 2 == 0
    wides = (e_ref, sto_w, rec_w)
    half_x = e_ref.shape[0] - 2 * DEEP
    place = 0
    for field, reach in enumerate((DEEP, DEEP - 1, DEEP - 1)):
        base = jnp.where(swapped, DEEP + half_x, DEEP - reach)
        for i in range(reach):
            value = slab_ref[place + i]
            value = jnp.exp(0.5 * value) if field == 0 else value
            wides[field][base + i] = at_window_rows(jnp.where(absent, (1.0, 1.0, 0.0)[field], value))
        place += reach
    place = 0
    for field, x, count in plan:
        wide = wides[field]
        up = wide[x, DEEP + size_y - count : DEEP + size_y, :]
        down = wide[x, DEEP : DEEP + count, :]
        at = pl.ds(place, count)
        even_ref[at, :] = jnp.where(y_even, up, down)
        odd_ref[at, :] = jnp.where(y_even, down, up)
        place += count


def field_rows(e_ref, sto_w, rec_w, delta_ref, gamma_ref, beta_ref):
    wide_x, wide_y, size_z = e_ref.shape
    half_x, size_y = wide_x - 2 * DEEP, wide_y - 2 * DEEP
    bx, by, swapped = lax.axis_index("bx"), lax.axis_index("by"), second_half()
    row_at = lax.broadcasted_iota(jnp.int32, (wide_y, size_z), 0)
    z_at = lax.broadcasted_iota(jnp.int32, (wide_y, size_z), 1)
    inside_y = ((row_at >= DEEP) | (by > 0)) & ((row_at < DEEP + size_y) | (by < lax.axis_size("by") - 1))
    for x in range(1, wide_x - 1):
        e = e_ref[x]
        total = e_ref[x - 1] + e_ref[x + 1]
        total = total + pltpu.roll(e, 1, 0) + pltpu.roll(e, wide_y - 1, 0)
        total = total + jnp.where(z_at == 0, 1.0, pltpu.roll(e, 1, 1))
        total = total + jnp.where(z_at == size_z - 1, 1.0, pltpu.roll(e, size_z - 1, 1))
        inside = inside_y
        if x < DEEP:
            inside = inside & (swapped | (bx > 0))
        if x >= DEEP + half_x:
            inside = inside & (jnp.logical_not(swapped) | (bx < lax.axis_size("bx") - 1))
        delta = jnp.where(inside, e / (sto_w[x] + e * total), 0.0)
        delta_ref[x] = delta
        gamma_ref[x] = delta * e
        beta_ref[x] = delta * rec_w[x]


def spread(ref, x, low, high):
    tiles = []
    for y in range(low, high):
        halves = [ref[x, pl.ds(y, 1), part * LANES : (part + 1) * LANES] for part in range(2)]
        tiles.append(jnp.stack([jnp.broadcast_to(half, (8, LANES)) for half in halves]))
    return jnp.stack(tiles)


def lanes():
    return lax.broadcasted_iota(jnp.int32, (8, LANES), 1)


def z_down(values, edge):
    turned = pltpu.roll(values, 1, 3)
    first = lanes() == 0
    return jnp.stack([jnp.where(first, edge, turned[:, 0]), jnp.where(first, turned[:, 0], turned[:, 1])], axis=1)


def z_up(values, edge):
    turned = pltpu.roll(values, LANES - 1, 3)
    last = lanes() == LANES - 1
    return jnp.stack([jnp.where(last, turned[:, 1], turned[:, 0]), jnp.where(last, edge, turned[:, 1])], axis=1)


def columns(ref, wide_y, x, low, high):
    return ref[x * wide_y + low : x * wide_y + high]


def sweep(source_ref, gamma_ref, from_ref, x, low, high):
    wide_y = gamma_ref.shape[1]
    centre = columns(from_ref, wide_y, x, low, high)
    total = columns(from_ref, wide_y, x - 1, low, high) + columns(from_ref, wide_y, x + 1, low, high)
    total = total + columns(from_ref, wide_y, x, low - 1, high - 1) + columns(from_ref, wide_y, x, low + 1, high + 1)
    total = total + z_down(centre, 0.0) + z_up(centre, 0.0)
    return columns(source_ref, wide_y, x, low, high) + spread(gamma_ref, x, low, high) * total


def reached(wide_x, wide_y, reach):
    cells = []
    for x in range(DEEP - reach, wide_x - DEEP + reach):
        left = reach - max(DEEP - x, x - (wide_x - DEEP - 1), 0)
        cells.append((x, DEEP - left, wide_y - DEEP + left))
    return cells


def without(cells, wide_y, margin):
    for x, low, high in cells:
        yield x, low, margin
        yield x, wide_y - margin, high


def grouped(cells):
    for x, first, end in cells:
        for low in range(first, end, COLUMNS_AT_ONCE):
            yield x, low, min(low + COLUMNS_AT_ONCE, end)


def solve(bet_ref, gamma_ref, inv_ref, one_ref, two_ref):
    wide_x, wide_y, _ = gamma_ref.shape
    for x, low, high in grouped(reached(wide_x, wide_y, DEEP - 2)):
        one_ref[x * wide_y + low : x * wide_y + high] = sweep(bet_ref, gamma_ref, bet_ref, x, low, high)
    for x, low, high in grouped(reached(wide_x, wide_y, DEEP - 3)):
        scaled = sweep(bet_ref, gamma_ref, one_ref, x, low, high)
        two_ref[x * wide_y + low : x * wide_y + high] = scaled * spread(inv_ref, x, low, high)


def z_of_tile():
    return jnp.stack([lanes(), lanes() + LANES])


def unpack(packed):
    return packed & 255, (packed >> 8) & 255


def pump(tests, per_brick, inner, wide_y, table_ref, obs_ref, delta_ref, bet_ref):
    sub = lax.broadcasted_iota(jnp.int32, (8, LANES), 0)
    z_of = z_of_tile()
    listed = list_length(per_brick)
    pumped = []
    for test in range(2 * tests):
        packed = table_ref[listed + LANES + test, 0]
        place, top = unpack(packed)
        y = place % wide_y
        is_inner = (y >= DEEP + 1) & (y < wide_y - DEEP - 1)
        near = ((packed >> 30) & 1 == 1) & (is_inner if inner else jnp.logical_not(is_inner))
        rate = obs_ref[3 + test // tests : 4 + test // tests, test % tests : test % tests + 1]
        delta = delta_ref[place // wide_y, pl.ds(y, 1), :]
        delta = jnp.stack([jnp.broadcast_to(delta[:, part * LANES : (part + 1) * LANES], (8, LANES)) for part in range(2)])
        hit = (z_of >= top) & (z_of < top + SCREEN) & (sub == test) & near
        pumped.append((place, jnp.where(hit, delta * rate, 0.0)))
    for place, taken in pumped:
        bet_ref[place] = bet_ref[place] - taken


def inner_kernel(tests, per_brick, e_ref, sto_w, rec_w, table_ref, obs_ref,
                 bet_ref, one_ref, head_ref, delta_ref, gamma_ref, beta_ref, inv_ref):
    wide_x, wide_y, _ = e_ref.shape
    field_rows(e_ref, sto_w, rec_w, delta_ref, gamma_ref, beta_ref)
    for x in range(3, wide_x - 3):
        inv_ref[x] = 1.0 / e_ref[x]
    for x in range(1, wide_x - 1):
        bet_ref[x * wide_y + DEEP + 1 : (x + 1) * wide_y - DEEP - 1] = spread(beta_ref, x, DEEP + 1, wide_y - DEEP - 1)
    pump(tests, per_brick, True, wide_y, table_ref, obs_ref, delta_ref, bet_ref)
    for x in range(2, wide_x - 2):
        low, high = DEEP + 2, wide_y - DEEP - 2
        one_ref[x * wide_y + low : x * wide_y + high] = sweep(bet_ref, gamma_ref, bet_ref, x, low, high)
    for x in range(3, wide_x - 3):
        low, high = DEEP + 3, wide_y - DEEP - 3
        scaled = sweep(bet_ref, gamma_ref, one_ref, x, low, high)
        head_ref[x * wide_y + low : x * wide_y + high] = scaled * spread(inv_ref, x, low, high)


def heads_kernel(plan, tests, per_brick, even_ref, odd_ref, e_in, sto_in, rec_in, table_ref, obs_ref, bet_in, one_in, head_in,
                 e_ref, delta_ref, gamma_ref, inv_ref, head_ref, row_ref, sto_w, rec_w, bet_ref, one_ref, beta_ref):
    wide_x, wide_y, _ = e_ref.shape
    by = lax.axis_index("by")
    y_even = by % 2 == 0
    no_low, no_high = by == 0, by == lax.axis_size("by") - 1
    place = 0
    for field, x, count in plan:
        wide = (e_ref, sto_w, rec_w)[field]
        fill = (1.0, 1.0, 0.0)[field]
        got_e, got_o = even_ref[pl.ds(place, count), :], odd_ref[pl.ds(place, count), :]
        low, high = jnp.where(y_even, got_o, got_e), jnp.where(y_even, got_e, got_o)
        wide[x, DEEP - count : DEEP, :] = jnp.where(no_low, fill, low)
        wide[x, wide_y - DEEP : wide_y - DEEP + count, :] = jnp.where(no_high, fill, high)
        place += count
    field_rows(e_ref, sto_w, rec_w, delta_ref, gamma_ref, beta_ref)
    for x in range(3, wide_x - 3):
        inv_ref[x] = 1.0 / e_ref[x]
    for x, low, high in without(reached(wide_x, wide_y, DEEP - 1), wide_y, DEEP + 1):
        bet_ref[x * wide_y + low : x * wide_y + high] = spread(beta_ref, x, low, high)
    sub = lax.broadcasted_iota(jnp.int32, (8, LANES), 0)
    z_of = z_of_tile()
    listed = list_length(per_brick)
    pump(tests, per_brick, False, wide_y, table_ref, obs_ref, delta_ref, bet_ref)
    for x, low, high in without(reached(wide_x, wide_y, DEEP - 2), wide_y, DEEP + 2):
        one_ref[x * wide_y + low : x * wide_y + high] = sweep(bet_ref, gamma_ref, bet_ref, x, low, high)
    for x, low, high in without(reached(wide_x, wide_y, DEEP - 3), wide_y, DEEP + 3):
        scaled = sweep(bet_ref, gamma_ref, one_ref, x, low, high)
        head_ref[x * wide_y + low : x * wide_y + high] = scaled * spread(inv_ref, x, low, high)
    slot_of = lanes() - per_brick * (sub % tests)
    gathered = jnp.zeros((8, LANES), jnp.float32)
    for rank in range(per_brick):
        place, top = unpack(table_ref[listed + rank, 0])
        hit = (z_of >= top) & (z_of < top + SCREEN)
        values = jnp.where(hit, head_ref[place], 0.0)
        gathered = jnp.where(slot_of == rank, jnp.sum(values[0] + values[1], axis=1, keepdims=True), gathered)
    mine = obs_ref[2:3, :] > 0.5
    parts = []
    for part in range(2):
        total = jnp.sum(jnp.where(sub // tests == part, gathered, 0.0), axis=0, keepdims=True)
        parts.append(jnp.where(mine, total * (1.0 / SCREEN) - obs_ref[part : part + 1, :], 0.0))
    row_ref[...] = jnp.broadcast_to(jnp.concatenate(parts, axis=1)[None], row_ref.shape)


def adjoint_kernel(tests, per_brick, n_wells, joined, scale, resid_ref, table_ref, clear_ref, clear_more_ref, e_ref, delta_ref, gamma_ref, inv_ref,
                   bet_ref, more_ref, adj_ref, norm_ref, weight_ref, one_ref):
    wide_x, wide_y, _ = e_ref.shape
    bricks = n_wells // per_brick
    sub = lax.broadcasted_iota(jnp.int32, (8, LANES), 0)
    z_of = z_of_tile()
    resid = resid_ref[:bricks] + resid_ref[bricks:] if joined else resid_ref[...]
    for brick in range(bricks):
        weight_ref[brick] = jnp.where(sub < tests, resid[brick, :, :LANES], resid[brick, :, LANES:])
    listed = list_length(per_brick)
    pick = per_brick * (sub % tests)

    def some_wells(turn, carry):
        todo = []
        for step in range(WELLS_AT_ONCE):
            packed = table_ref[turn * WELLS_AT_ONCE + step, 0]
            column, top = unpack(packed)
            brick, rank = (packed >> 16) & 255, (packed >> 24) & 31
            value = jnp.take_along_axis(weight_ref[brick], pick + rank, axis=1, mode="promise_in_bounds")
            todo.append((column, jnp.where((z_of >= top) & (z_of < top + SCREEN), value[None], 0.0)))
        for step, (column, value) in enumerate(todo):
            into_ref = (bet_ref, more_ref)[step % 2]
            into_ref[column] = into_ref[column] + value
        return carry

    turns = (table_ref[listed + LANES + 16, 0] + WELLS_AT_ONCE - 1) // WELLS_AT_ONCE
    lax.fori_loop(0, turns, some_wells, 0)
    for x, low, high in reached(wide_x, wide_y, DEEP - 1):
        row = pl.ds(x * wide_y + low, high - low)
        bet_ref[row] = (bet_ref[row] + more_ref[row]) * spread(delta_ref, x, low, high)
    solve(bet_ref, gamma_ref, inv_ref, one_ref, adj_ref)
    squares = jnp.sum(resid * resid, axis=0)
    squares = jnp.where(sub < tests, squares[:, :LANES], squares[:, LANES:])
    misfit = jnp.sum(jnp.where(lanes() // per_brick == sub % tests, squares, 0.0), axis=1, keepdims=True) / n_wells + EPSILON
    norm_ref[...] = jnp.broadcast_to(scale / misfit, (8, LANES))


def gradient_kernel(kept, norm_ref, e_ref, up_ref, head_ref, adj_ref, out_ref):
    wide_x, wide_y, _ = e_ref.shape
    low, high = DEEP, wide_y - DEEP
    part = jnp.where(second_half(), 1, 0) if kept else jnp.where(second_half(), 0, 1)
    is_first = part == 0
    at_first, at_last = lanes() == 0, lanes() == LANES - 1

    def spread_part(ref, x, first, last, which):
        rows = [ref[x, pl.ds(y, 1), pl.ds(pl.multiple_of(which * LANES, LANES), LANES)] for y in range(first, last)]
        return jnp.stack([jnp.broadcast_to(row, (8, LANES)) for row in rows])

    def tiles(ref, x, first, last, which):
        return ref[x * wide_y + first : x * wide_y + last, which]

    def next_cell(values, others):
        return pltpu.roll(jnp.where(at_first & is_first, others, values), LANES - 1, 2)

    before = None
    for x in range(DEEP - 1, wide_x - DEEP):
        e, head, adjoint = spread_part(e_ref, x, low, high, part), tiles(head_ref, x, low, high, part), tiles(adj_ref, x, low, high, part)
        gap = (head - tiles(head_ref, x + 1, low, high, part)) * (adjoint - tiles(adj_ref, x + 1, low, high, part))
        after = e * spread_part(e_ref, x + 1, low, high, part) * gap
        if x >= DEEP:
            total = before + after
            e_y = spread_part(e_ref, x, low - 1, high + 1, part)
            head_y, adjoint_y = tiles(head_ref, x, low - 1, high + 1, part), tiles(adj_ref, x, low - 1, high + 1, part)
            sides = e_y[:-1] * e_y[1:] * (head_y[:-1] - head_y[1:]) * (adjoint_y[:-1] - adjoint_y[1:])
            total = total + sides[:-1] + sides[1:]
            head_other, adjoint_other = tiles(head_ref, x, low, high, 1 - part), tiles(adj_ref, x, low, high, 1 - part)
            head_next, adjoint_next = next_cell(head, head_other), next_cell(adjoint, adjoint_other)
            at_top = at_last & jnp.logical_not(is_first)
            gap = (head - jnp.where(at_top, 0.0, head_next)) * (adjoint - jnp.where(at_top, 0.0, adjoint_next))
            upper = spread_part(up_ref, x, low, high, part) * gap
            middle = spread_part(up_ref, x, low, high, 1 - part) * (head_other - head_next) * (adjoint_other - adjoint_next)
            lower = pltpu.roll(jnp.where(at_top, middle, upper), 1, 2)
            total = total + upper + jnp.where(at_first & is_first, e * head * adjoint, lower)
            total = jnp.sum(total * norm_ref[...], axis=1, keepdims=True)
            for y in range(high - low):
                out_ref[x - DEEP, pl.ds(y, 1), :] = total[y]
        before = after


def join_kernel(keep_ref, other_ref, out_ref):
    half_x = keep_ref.shape[0]
    mine = jnp.where(second_half(), half_x, 0)
    out_ref[pl.ds(mine, half_x)] = keep_ref[...]
    out_ref[pl.ds(half_x - mine, half_x)] = other_ref[...]


def vmem():
    return pl.BlockSpec(memory_space=pltpu.VMEM)


def smem():
    return pl.BlockSpec(memory_space=pltpu.SMEM)


def f32(*shape):
    return jax.ShapeDtypeStruct(shape, jnp.float32)


def i32(*shape):
    return jax.ShapeDtypeStruct(shape, jnp.int32)


PARAMS = pltpu.CompilerParams(vmem_limit_bytes=24 * 1024 * 1024)


def local(log_conductivity, storage, recharge, pump_rate, pump_well, observed, owner, screen_column, screen_top):
    size_x, size_y, size_z = log_conductivity.shape
    half_x = size_x // 2
    tests = pump_rate.shape[0]
    n_wells = owner.shape[0]
    groups, n_bx, n_by = lax.axis_size("test"), lax.axis_size("bx"), lax.axis_size("by")
    bricks = n_bx * n_by
    per_brick = n_wells // bricks
    plan = slab_plan(half_x)
    rows_x = 3 * DEEP - 2
    rows_y = sum(count for _, _, count in plan)
    wide_x, wide_y = half_x + 2 * DEEP, size_y + 2 * DEEP
    tiles = (wide_x * wide_y, 2, 8, LANES)

    def in_hbm(*arrays):
        return [pltpu.with_memory_space_constraint(a, pltpu.HBM) for a in arrays]

    hbm = pl.BlockSpec(memory_space=pltpu.HBM)
    slab = pl.pallas_call(
        edge_kernel,
        out_shape=f32(rows_x, size_y, size_z),
        in_specs=[hbm] * 3,
        out_specs=vmem(),
        scratch_shapes=[pltpu.SemaphoreType.DMA((3,))],
        compiler_params=PARAMS,
        name="edge",
    )(*in_hbm(log_conductivity, storage, recharge))
    got_x = lax.ppermute(slab, ("test", "bx"), circle(n_bx, groups))

    inputs = (
        observed,
        pump_rate.reshape(1, tests),
        pump_well.reshape(1, tests),
        owner.reshape(1, n_wells),
        screen_column.reshape(1, n_wells),
        screen_top.reshape(1, n_wells),
        log_conductivity,
        storage,
        recharge,
    )
    owner, column, top, log_k, sto, rec, facts = pl.pallas_call(
        load_kernel,
        out_shape=[jax.ShapeDtypeStruct(a.shape, a.dtype) for a in inputs[3:]] + [f32(8, n_wells)],
        in_specs=[hbm] * len(inputs) + [vmem()],
        out_specs=[vmem()] * (len(inputs) - 2),
        scratch_shapes=[pltpu.VMEM((1, tests), jnp.float32), pltpu.VMEM((1, tests), jnp.int32), pltpu.SemaphoreType.DMA((len(inputs),))],
        compiler_params=PARAMS,
        name="load",
    )(*in_hbm(*inputs), slab)
    pairs = [(test, pair_of(test, groups)) for test in range(groups)]
    other_facts = lax.ppermute(facts, "test", pairs)

    bx, by, second = lax.axis_index("bx"), lax.axis_index("by"), lax.axis_index("test") % 2
    well_x = (owner // n_by - bx) * size_x + column // size_y + DEEP - second * half_x
    well_y = (owner % n_by - by) * size_y + column % size_y + DEEP
    out_x = jnp.maximum(jnp.maximum(DEEP - well_x, well_x - (DEEP + half_x - 1)), 0)
    out_y = jnp.maximum(jnp.maximum(DEEP - well_y, well_y - (DEEP + size_y - 1)), 0)
    in_window = (out_x + out_y < DEEP).astype(jnp.float32)
    owned = (out_x + out_y == 0).astype(jnp.float32)
    place = jnp.where(in_window > 0.5, well_x * wide_y + well_y, 0)
    window = f32(wide_x, wide_y, size_z)
    e, sto_w, rec_w, up = pl.pallas_call(
        window_kernel,
        out_shape=[window] * 4,
        in_specs=[vmem()] * 3,
        out_specs=[vmem()] * 4,
        compiler_params=PARAMS,
        name="window",
    )(log_k, sto, rec)
    e, sto_w, rec_w, even_y, odd_y = pl.pallas_call(
        functools.partial(pack_y, plan),
        out_shape=[window] * 3 + [f32(rows_y, size_z)] * 2,
        in_specs=[vmem()] * 4,
        out_specs=[vmem()] * 5,
        input_output_aliases={1: 0, 2: 1, 3: 2},
        compiler_params=PARAMS,
        name="pack_y",
    )(got_x, e, sto_w, rec_w)
    even, odd = side_partners(n_by, groups)
    got_even = lax.ppermute(even_y, ("test", "by"), even)
    got_odd = lax.ppermute(odd_y, ("test", "by"), odd)

    table, obs, clear, clear_more = pl.pallas_call(
        functools.partial(wells_kernel, tests, per_brick, bricks),
        out_shape=[i32(list_length(per_brick) + LANES + 24, 1), f32(8, LANES), f32(*tiles), f32(*tiles)],
        in_specs=[vmem()] * 8,
        out_specs=[vmem()] * 4,
        compiler_params=PARAMS,
        name="wells",
    )(owner, place, top, in_window, owned, facts, other_facts, even_y)

    joined = groups == 2
    copies = groups * bricks if joined else bricks
    inner = pl.pallas_call(
        functools.partial(inner_kernel, tests, per_brick),
        out_shape=[f32(*tiles)] * 3,
        in_specs=[vmem()] * 5,
        out_specs=[vmem()] * 3,
        scratch_shapes=[pltpu.VMEM((wide_x, wide_y, size_z), jnp.float32)] * 4,
        compiler_params=PARAMS,
        name="inner",
    )(e, sto_w, rec_w, table, obs)
    e, delta, gamma, inverse, head, row = pl.pallas_call(
        functools.partial(heads_kernel, plan, tests, per_brick),
        out_shape=[window] * 4 + [f32(*tiles), f32(copies, 1, 2 * LANES)] + [window] * 2 + [f32(*tiles)] * 2,
        in_specs=[vmem()] * 10,
        out_specs=[vmem()] * 10,
        scratch_shapes=[pltpu.VMEM((wide_x, wide_y, size_z), jnp.float32)],
        input_output_aliases={2: 0, 3: 6, 4: 7, 7: 8, 8: 9, 9: 4},
        compiler_params=PARAMS,
        name="heads",
    )(got_even, got_odd, e, sto_w, rec_w, table, obs, *inner)[:6]

    if joined:
        residuals = lax.all_to_all(row, ("test", "bx", "by"), 0, 0)
    else:
        residuals = lax.all_to_all(row + lax.ppermute(row, "test", pairs), ("bx", "by"), 0, 0)

    scale = -0.5 / (tests * groups)
    _, _, adjoint, norm = pl.pallas_call(
        functools.partial(adjoint_kernel, tests, per_brick, n_wells, joined, scale),
        out_shape=[f32(*tiles)] * 3 + [f32(8, LANES)],
        in_specs=[vmem()] * 8,
        out_specs=[vmem()] * 4,
        scratch_shapes=[pltpu.VMEM((bricks, 8, LANES), jnp.float32), pltpu.VMEM(tiles, jnp.float32)],
        input_output_aliases={2: 0, 3: 1},
        compiler_params=PARAMS,
        name="adjoint",
    )(residuals, table, clear, clear_more, e, delta, gamma, inverse)

    def gradient_of(kept):
        return pl.pallas_call(
            functools.partial(gradient_kernel, kept),
            out_shape=f32(half_x, size_y, LANES),
            in_specs=[vmem()] * 5,
            out_specs=vmem(),
            compiler_params=PARAMS,
            name="keep" if kept else "send",
        )(norm, e, up, head, adjoint)

    send = gradient_of(False)
    other = lax.ppermute(send, "test", pairs) if joined else send
    keep = gradient_of(True)
    if joined:
        return pl.pallas_call(
            join_kernel,
            out_shape=f32(size_x, size_y, LANES),
            in_specs=[vmem()] * 2,
            out_specs=vmem(),
            compiler_params=PARAMS,
            name="join",
        )(pltpu.with_memory_space_constraint(keep, pltpu.VMEM), pltpu.with_memory_space_constraint(other, pltpu.VMEM))
    low, high = jnp.where(second == 0, keep, send), jnp.where(second == 0, send, keep)
    half = jnp.concatenate([low, high], axis=2)
    none = jnp.zeros_like(half)
    whole = jnp.where(second == 0, jnp.concatenate([half, none], axis=0), jnp.concatenate([none, half], axis=0))
    return lax.psum_scatter(whole, "test", scatter_dimension=2, tiled=True)


def solution(mesh):
    placed = (
        P("bx", "by", None),
        P("bx", "by", None),
        P("bx", "by", None),
        P("test"),
        P("test"),
        P("test", None),
        P(),
        P(),
        P(),
    )
    return jax.shard_map(local, mesh=mesh, in_specs=placed, out_specs=P("bx", "by", "test"), check_vma=False)
```
